32 devices in a mesh: seq: 32 (over z, y, x, core), tp: 1.
Axes of the slice: x: 2, y: 2, z: 4, core: 2. Of those that a mesh axis runs over, the one named last changes fastest.
Arguments:
- queries: bfloat16 [4096, 4096], P('seq', 'tp'), may hold values from -6 to 6
- keys: bfloat16 [4096, 4096], P('seq', 'tp'), may hold values from -6 to 6
- values: bfloat16 [4096, 4096], P('seq', 'tp'), may hold values from -6 to 6
- w_out: bfloat16 [4096, 4096], P('seq', 'tp'), may hold values from -0.09375 to 0.09375
- taps: bfloat16 [4096, 128], P('tp'), may hold values from -0.6 to 0.6, as said below
- seg_ids: int32 [32], replicated, may hold values from 0 to 3, never falling along the last dimension, each value on 1 to 16 neighbouring positions
- cotangent: bfloat16 [4096, 4096], P('seq', 'tp'), may hold values from -6 to 6
Outputs:
- outputs: bfloat16 [4096, 4096], P('seq', 'tp')
- grad_queries: bfloat16 [4096, 4096], P('seq', 'tp')
- grad_keys: bfloat16 [4096, 4096], P('seq', 'tp')
- grad_values: bfloat16 [4096, 4096], P('seq', 'tp')
- taps_grad: float32 [4096, 128], P(('tp', 'seq'))
The draws below stay inside these ranges and needn't reach their ends.
Inputs may be any that keep to these rules, and one draw needn't show every extreme that they name: `seg_ids`: ids never fall along the pack, each segment covers 1 to 16 blocks. taps decay along the lag at a rate of each channel.
All inputs are finite; a program needn't handle non-finite values.
Results may differ from the reference program's by a relative error of at most 0.013.
Values may be sent and summed in bfloat16 or wider, within the bound.
No kernel may reach another device: no remote copies, remote signals or barrier semaphores. Data moves between devices by JAX's collectives and lax.ppermute only.
A program may use at most 128 MiB of HBM per device.

```python
import math
import jax
import jax.numpy as jnp
import numpy as np
from jax import lax

C = 4096
D = 4096
FILT = 128
TOKENS = 4096
BLOCKS = 32
SEGS = 4
SEG_MOST = 16


def draw_taps(key, part):
    rate_key, amp_key = jax.random.split(jax.random.fold_in(key, 11))
    rates = jnp.exp(jax.random.uniform(rate_key, (C, 1), jnp.float32, math.log(0.004), math.log(0.08)))
    lags = jnp.arange(FILT, dtype=jnp.float32)[None, :]
    amps = jnp.clip(jax.random.normal(amp_key, (C, FILT), jnp.float32), -4.0, 4.0)
    return (0.15 * amps * jnp.exp(-rates * lags)).astype(jnp.bfloat16)


def block_levels(own_key, shape, pieces, smallest, high):
    def one(dim, blocks):
        heights = jax.random.uniform(jax.random.fold_in(jax.random.fold_in(own_key, 6), dim), (blocks,), jnp.float32, smallest / len(pieces), high / len(pieces))
        return jnp.repeat(jnp.exp(heights), shape[dim] // blocks).reshape((-1,) + (1,) * (len(shape) - dim - 1))

    gain = one(*pieces[0])
    for cut in pieces[1:]:
        gain = gain * one(*cut)
    return gain


def length_profile(amount, total, most, skew):
    portions = [(1 << 20) // math.isqrt(standing ** skew) + 1 for standing in range(2, amount + 1)]
    surplus, counts = total - most - (amount - 1), [1] * (amount - 1)
    while surplus > 0:
        candidates = [i for i in range(amount - 1) if counts[i] < most]
        pool, left = sum([portions[i] for i in candidates]), surplus
        for i in candidates:
            more = min(most - counts[i], max(1, left * portions[i] // pool), surplus)
            counts[i] = counts[i] + more
            surplus = surplus - more
    return np.array([most] + counts)


def ragged_sizes(stream_key, count, total, bound, skew):
    if count == 2:
        one = jax.random.randint(stream_key, (), max(1, total - bound), min(bound, total - 1) + 1)
        return jnp.stack([one, total - one])
    sizes = jnp.asarray(length_profile(count, total, bound, skew), jnp.int32)
    pairs = (count - 1) // 2
    giver, receiver = sizes[1:1 + 2 * pairs:2], sizes[2:2 + 2 * pairs:2]
    margin = jnp.minimum(giver - 1, bound - receiver)
    passed = jax.random.randint(jax.random.fold_in(stream_key, 1), (pairs,), 0, 1 << 20) % (margin + 1)
    sizes = sizes.at[1:1 + 2 * pairs:2].set(giver - passed).at[2:2 + 2 * pairs:2].set(receiver + passed)
    return sizes[jax.random.permutation(jax.random.fold_in(stream_key, 2), count)]


def scatter_about(stream_key, extent, scale, limit, shards=(), kind=jnp.bfloat16):
    gain = block_levels(stream_key, extent, shards, -0.22, 0.18) if shards else 1.0
    drawn = jax.random.normal(stream_key, extent, jnp.float32) * scale * gain
    return jnp.minimum(jnp.maximum(drawn, -limit), limit).astype(kind)


def setup_inputs(seed: int = 0) -> dict:
    seeds = jax.random.split(jax.random.key(seed), 8)
    return {
        "queries": scatter_about(seeds[0], (TOKENS, C), 1.0, 6.0, ((0, 32),)),
        "keys": scatter_about(seeds[1], (TOKENS, C), 1.0, 6.0, ((0, 32),)),
        "values": scatter_about(seeds[2], (TOKENS, C), 1.0, 6.0, ((0, 32),)),
        "w_out": scatter_about(seeds[3], (C, D), C ** -0.5, 0.09375, ((0, 32),)),
        "taps": draw_taps(jax.random.fold_in(seeds[7], 71), 0),
        "seg_ids": jnp.searchsorted(jnp.cumsum(ragged_sizes(seeds[5], SEGS, BLOCKS, SEG_MOST, 0)), jnp.arange(BLOCKS), side="right").astype(jnp.int32),
        "cotangent": scatter_about(seeds[6], (TOKENS, D), 1.0, 6.0, ((0, 32),)),
    }


def lag_tables(length):
    rows = jnp.arange(length)[:, None]
    cols = jnp.arange(length)[None, :]
    lagged = (rows - cols).reshape(1, -1)
    shifts = jnp.arange(length)[:, None]
    inside = (lagged == shifts).astype(jnp.float32)
    across = (lagged + length == shifts).astype(jnp.float32)
    return inside, across


def dense_taps(taps_grp, table):
    count, length = taps_grp.shape
    dense = jnp.dot(taps_grp.astype(jnp.float32), table, precision=lax.Precision.HIGHEST)
    return dense.reshape(count, length, length)


def to_groups(blocks, group):
    count, length, chans = blocks.shape
    return blocks.reshape(count, length, chans // group, group).transpose(2, 0, 1, 3)


def from_groups(grouped):
    parts, count, length, group = grouped.shape
    return grouped.transpose(1, 2, 0, 3).reshape(count, length, parts * group)


def reference(queries, keys, values, w_out, taps, seg_ids, cotangent):
    tokens, chans = queries.shape
    length = taps.shape[1]
    count = tokens // length
    group = min(256, chans)
    inside, across = lag_tables(length)
    product = (keys.astype(jnp.float32) * values.astype(jnp.float32)).astype(jnp.bfloat16)
    linked = jnp.concatenate([jnp.zeros((1,), jnp.float32), (seg_ids[1:] == seg_ids[:-1]).astype(jnp.float32)])
    linked_next = jnp.concatenate([linked[1:], jnp.zeros((1,), jnp.float32)])
    blocks = product.reshape(count, length, chans)
    before = jnp.concatenate([jnp.zeros_like(blocks[:1]), blocks[:-1]], 0)
    taps_groups = taps.reshape(chans // group, group, length)

    def forward_group(items):
        taps_grp, current, prior = items
        near = dense_taps(taps_grp, inside)
        far = dense_taps(taps_grp, across)
        own = jnp.einsum("cij,bjc->bic", near, current.astype(jnp.float32), precision=lax.Precision.HIGHEST)
        back = jnp.einsum("cij,bjc->bic", far, prior.astype(jnp.float32), precision=lax.Precision.HIGHEST)
        return (own + linked[:, None, None] * back).astype(jnp.bfloat16)

    filtered_grp = lax.map(forward_group, (taps_groups, to_groups(blocks, group), to_groups(before, group)))
    filtered = from_groups(filtered_grp).reshape(tokens, chans)
    gated = (queries.astype(jnp.float32) * filtered.astype(jnp.float32)).astype(jnp.bfloat16)
    outputs = jnp.dot(gated, w_out, preferred_element_type=jnp.float32).astype(jnp.bfloat16)
    grad_gated = jnp.dot(cotangent, w_out.T, preferred_element_type=jnp.float32).astype(jnp.bfloat16)
    grad_filtered = (grad_gated.astype(jnp.float32) * queries.astype(jnp.float32)).astype(jnp.bfloat16)
    grad_queries = (grad_gated.astype(jnp.float32) * filtered.astype(jnp.float32)).astype(jnp.bfloat16)
    grads = grad_filtered.reshape(count, length, chans)
    after = jnp.concatenate([grads[1:], jnp.zeros_like(grads[:1])], 0)

    def backward_group(items):
        taps_grp, grad, later, current, prior = items
        near = dense_taps(taps_grp, inside)
        far = dense_taps(taps_grp, across)
        gradf = grad.astype(jnp.float32)
        own = jnp.einsum("cij,bic->bjc", near, gradf, precision=lax.Precision.HIGHEST)
        ahead = jnp.einsum("cij,bic->bjc", far, later.astype(jnp.float32), precision=lax.Precision.HIGHEST)
        back_grad = (own + linked_next[:, None, None] * ahead).astype(jnp.bfloat16)
        near_sum = jnp.einsum("bic,bjc->cij", gradf, current.astype(jnp.float32), precision=lax.Precision.HIGHEST)
        far_sum = jnp.einsum("bic,bjc->cij", gradf * linked[:, None, None], prior.astype(jnp.float32), precision=lax.Precision.HIGHEST)
        width = near_sum.shape[0]
        dims = (((1,), (1,)), ((), ()))
        taps_part = lax.dot_general(near_sum.reshape(width, -1), inside, dims, precision=lax.Precision.HIGHEST)
        taps_part = taps_part + lax.dot_general(far_sum.reshape(width, -1), across, dims, precision=lax.Precision.HIGHEST)
        return back_grad, taps_part

    back_grp, taps_grp_grad = lax.map(backward_group, (taps_groups, to_groups(grads, group), to_groups(after, group), to_groups(blocks, group), to_groups(before, group)))
    grad_product = from_groups(back_grp).reshape(tokens, chans).astype(jnp.float32)
    grad_keys = (grad_product * values.astype(jnp.float32)).astype(jnp.bfloat16)
    grad_values = (grad_product * keys.astype(jnp.float32)).astype(jnp.bfloat16)
    taps_grad = taps_grp_grad.reshape(chans, length)
    return (outputs, grad_queries, grad_keys, grad_values, taps_grad)
```

```python
import jax
import jax.numpy as jnp
import numpy as np
from jax import lax
from jax.sharding import PartitionSpec as P

F32 = jnp.float32
BF16 = jnp.bfloat16


def spectrum_table(length):
    angles = np.pi * (2 * np.arange(length)[:, None] + 1) * np.arange(-length, length)[None, :] / (2 * length)
    table = np.concatenate([np.cos(angles), -np.sin(angles)], 0).astype(np.float32)
    high = table.astype(BF16)
    low = (table - high.astype(np.float32)).astype(BF16)
    return table, high, low


def forward_dft(high, low, data, dims):
    first = lax.dot_general(high, data, (dims, ((), ())), preferred_element_type=F32)
    second = lax.dot_general(low, data, (dims, ((), ())), preferred_element_type=F32)
    return first + second


def times(a, b):
    half = a.shape[0] // 2
    ar, ai, br, bi = a[:half], a[half:], b[:half], b[half:]
    return jnp.concatenate([ar * br - ai * bi, ar * bi + ai * br], 0)


def times_conj(a, b):
    half = a.shape[0] // 2
    ar, ai, br, bi = a[:half], a[half:], b[:half], b[half:]
    return jnp.concatenate([ar * br + ai * bi, ai * br - ar * bi], 0)


def inverse_dft(table, spectrum, scale):
    done = lax.dot_general(
        table, spectrum, (((0,), (0,)), ((), ())), precision=lax.Precision.HIGH, preferred_element_type=F32
    )
    return done * scale


def mul(a, b):
    return (a.astype(F32) * b.astype(F32)).astype(BF16)


def scatter_sum(part, nseq, place):
    chans, lags = part.shape
    bits = nseq.bit_length() - 1
    if nseq != 1 << bits:
        return lax.psum_scatter(part, "seq", scatter_dimension=0, tiled=True)
    for step in range(bits):
        mine = (place >> step) & 1
        part = part.reshape(-1, 2, chans // nseq, lags)
        away = lax.dynamic_index_in_dim(part, 1 - mine, 1, False)
        kept = lax.dynamic_index_in_dim(part, mine, 1, False)
        part = kept + lax.ppermute(away, "seq", [(i, i ^ (1 << step)) for i in range(nseq)])
    return part.reshape(chans // nseq, lags)


def on_device(queries, keys, values, w_out, taps, seg_ids, cotangent):
    rows, chans = queries.shape
    length = taps.shape[1]
    assert rows == length
    nseq = lax.axis_size("seq")
    place = lax.axis_index("seq")
    table, high, low = spectrum_table(length)
    table_now, high_now, low_now = table[:, length:], high[:, length:], low[:, length:]
    scale = 1.0 / length
    weights = lax.all_gather(w_out, "seq", axis=0, tiled=True)
    later = [(i, i + 1) for i in range(nseq - 1)]
    earlier = [(i + 1, i) for i in range(nseq - 1)]
    own = lax.dynamic_index_in_dim(seg_ids, place, 0, False)
    prior = lax.dynamic_index_in_dim(seg_ids, jnp.maximum(place - 1, 0), 0, False)
    linked = (place > 0) & (own == prior)

    product = mul(keys, values)
    before = lax.ppermute(product, "seq", later)
    before = jnp.where(linked, before, jnp.zeros_like(before))
    data = forward_dft(high, low, jnp.concatenate([before, product], 0), ((1,), (0,)))
    filt = forward_dft(high_now, low_now, taps, ((1,), (1,)))
    filtered = inverse_dft(table_now, times(filt, data), scale).astype(BF16)
    gated = mul(queries, filtered)

    grad_gated = lax.dot_general(cotangent, weights, (((1,), (1,)), ((), ())), preferred_element_type=F32)
    grad_gated = lax.psum_scatter(grad_gated, "tp", scatter_dimension=1, tiled=True).astype(BF16)
    grad_queries = mul(grad_gated, filtered)
    grad_filtered = mul(grad_gated, queries)
    grads = forward_dft(high_now, low_now, grad_filtered, ((1,), (0,)))
    back = inverse_dft(table, times_conj(grads, filt), scale)
    across = jnp.where(linked, back[:length], 0.0).astype(BF16)
    ahead = lax.ppermute(across, "seq", earlier)
    taps_part = lax.dot_general(
        times_conj(grads, data), table_now, (((0,), (0,)), ((), ())),
        precision=lax.Precision.HIGH, preferred_element_type=F32,
    ) * scale
    taps_grad = scatter_sum(taps_part, nseq, place)
    outputs = jnp.dot(
        lax.all_gather(gated, "tp", axis=1, tiled=True), weights, preferred_element_type=F32
    ).astype(BF16)
    grad_product = (back[length:] + ahead.astype(F32)).astype(BF16)
    grad_keys = mul(grad_product, values)
    grad_values = mul(grad_product, keys)
    return (outputs, grad_queries, grad_keys, grad_values, taps_grad)


def solution(mesh):
    block = P("seq", "tp")
    return jax.shard_map(
        on_device,
        mesh=mesh,
        in_specs=(block, block, block, block, P("tp", None), P(), block),
        out_specs=(block, block, block, block, P(("tp", "seq"), None)),
        check_vma=False,
    )
```

```python
import functools

import jax
import jax.numpy as jnp
import numpy as np
from jax import lax
from jax.experimental import pallas as pl
from jax.experimental.pallas import tpu as pltpu
from jax.sharding import PartitionSpec as P

F32 = jnp.float32
BF16 = jnp.bfloat16


def spectrum_table(length):
    angles = np.pi * (2 * np.arange(length)[:, None] + 1) * np.arange(-length, length)[None, :] / (2 * length)
    table = np.concatenate([np.cos(angles), -np.sin(angles)], 0).astype(np.float32)
    high = table.astype(BF16)
    low = (table - high.astype(np.float32)).astype(BF16)
    return table, high, low


def forward_dft(high, low, data, dims):
    first = lax.dot_general(high, data, (dims, ((), ())), preferred_element_type=F32)
    second = lax.dot_general(low, data, (dims, ((), ())), preferred_element_type=F32)
    return first + second


def times(a, b):
    half = a.shape[0] // 2
    ar, ai, br, bi = a[:half], a[half:], b[:half], b[half:]
    return jnp.concatenate([ar * br - ai * bi, ar * bi + ai * br], 0)


def times_conj(a, b):
    half = a.shape[0] // 2
    ar, ai, br, bi = a[:half], a[half:], b[:half], b[half:]
    return jnp.concatenate([ar * br + ai * bi, ai * br - ar * bi], 0)


def inverse_dft(table, spectrum, scale):
    done = lax.dot_general(
        table, spectrum, (((0,), (0,)), ((), ())), precision=lax.Precision.HIGH, preferred_element_type=F32
    )
    return done * scale


def mul(a, b):
    return (a.astype(F32) * b.astype(F32)).astype(BF16)


def pick(data, width, side):
    blocks = [data[:, i : i + width] for i in range(0, data.shape[1], width)]
    return jnp.concatenate([jnp.where(side == 0, a, b) for a, b in zip(blocks[::2], blocks[1::2])], 1)


def scatter_sum(part, nseq, place, order):
    share = part.shape[1] // nseq
    bits = nseq.bit_length() - 1
    if nseq != 1 << bits:
        return lax.psum_scatter(part, "seq", scatter_dimension=1, tiled=True)
    left = list(range(bits))
    for step in [b for b in order if b < bits] + [b for b in range(bits) if b not in order]:
        width = share << sum(b < step for b in left)
        left.remove(step)
        mine = (place >> step) & 1
        away = pick(part, width, 1 - mine)
        if step:
            away = away.astype(BF16)
        away = lax.ppermute(away, "seq", [(i, i ^ (1 << step)) for i in range(nseq)])
        part = pick(part, width, mine) + away.astype(F32)
    return part


def links(seg_ids, place):
    own = lax.dynamic_index_in_dim(seg_ids, place, 0, False)
    prior = lax.dynamic_index_in_dim(seg_ids, jnp.maximum(place - 1, 0), 0, False)
    return (place > 0) & (own == prior)


def gathered_products(gated, cotangent, w_out):
    weights = lax.all_gather(w_out, "seq", axis=0, tiled=True)
    grad_gated = lax.dot_general(cotangent, weights, (((1,), (1,)), ((), ())), preferred_element_type=F32)
    grad_gated = lax.psum_scatter(grad_gated, "tp", scatter_dimension=1, tiled=True).astype(BF16)
    outputs = jnp.dot(
        lax.all_gather(gated, "tp", axis=1, tiled=True), weights, preferred_element_type=F32
    ).astype(BF16)
    return grad_gated, outputs


def ring_place(step, size):
    half = (size + 1) // 2
    return jnp.where(step < half, 2 * step, 2 * (size - 1 - step) + 1)


def ring_step(row, size):
    return jnp.where(row & 1 == 0, row >> 1, size - 1 - (row >> 1))


def assemble_kernel(count, where_ref, *refs):
    pieces, out_ref = refs[:-1], refs[-1]
    width = out_ref.shape[0]
    for i in range(count):
        for half in range(2):
            at = pl.ds(pl.multiple_of(where_ref[2 * i + half] * width, width), width)
            out_ref[:, at] = pieces[i][:, half * width : (half + 1) * width]


def assemble(where, pieces, chans):
    rows = pieces[0].shape[0]
    vmem = pl.BlockSpec(memory_space=pltpu.VMEM)
    return pl.pallas_call(
        functools.partial(assemble_kernel, len(pieces)),
        out_shape=jax.ShapeDtypeStruct((rows, chans), pieces[0].dtype),
        in_specs=[pl.BlockSpec(memory_space=pltpu.SMEM)] + [vmem] * len(pieces),
        out_specs=vmem,
        compiler_params=pltpu.CompilerParams(vmem_limit_bytes=16 << 20),
        cost_estimate=pl.CostEstimate(flops=0, bytes_accessed=4 * rows * chans, transcendentals=0),
    )(where, *pieces)


def project_kernel(count, last, where_ref, gated_ref, *refs):
    weights, refs = refs[: 2 * count], refs[2 * count :]
    width = weights[0].shape[0]
    total = None
    for i in range(count):
        left = jnp.concatenate(
            [
                gated_ref[:, pl.ds(pl.multiple_of(where_ref[2 * i + half] * width, width), width)]
                for half in range(2)
            ],
            1,
        )
        right = jnp.concatenate([weights[2 * i][...], weights[2 * i + 1][...]], 0)
        part = jnp.dot(left, right, preferred_element_type=F32)
        total = part if total is None else total + part
    if last:
        before_ref, own_ref, away_ref = refs
        total = total + before_ref[...]
        rows = own_ref.shape[0]
        own_ref[...] = total[:rows]
        away_ref[...] = total[rows:].astype(BF16)
    else:
        refs[0][...] = total


def project(where, gated, weights, before=None):
    tokens = gated.shape[0]
    depth, feats = weights[0].shape
    tile = min(512, feats)
    last = before is not None
    whole = pl.BlockSpec((tokens, tile), lambda j, where: (0, j))
    block = pl.BlockSpec((tokens // 2, tile), lambda j, where: (0, j))
    split = tuple(jax.ShapeDtypeStruct((tokens // 2, feats), kind) for kind in (F32, BF16))
    return pl.pallas_call(
        functools.partial(project_kernel, len(weights) // 2, last),
        out_shape=split if last else jax.ShapeDtypeStruct((tokens, feats), F32),
        grid_spec=pltpu.PrefetchScalarGridSpec(
            num_scalar_prefetch=1,
            grid=(feats // tile,),
            in_specs=[pl.BlockSpec(gated.shape, lambda j, where: (0, 0))]
            + [pl.BlockSpec((depth, tile), lambda j, where: (0, j))] * len(weights)
            + [whole] * last,
            out_specs=(block, block) if last else whole,
        ),
        compiler_params=pltpu.CompilerParams(vmem_limit_bytes=32 << 20),
        cost_estimate=pl.CostEstimate(
            flops=2 * tokens * depth * len(weights) * feats,
            bytes_accessed=2 * depth * feats * len(weights) + 2 * gated.size + 4 * tokens * feats,
            transcendentals=0,
        ),
    )(where, gated, *weights, *([before] if last else []))


def ring_products(gated, cotangent, w_out, place, nseq):
    rows, chans = gated.shape
    feats = cotangent.shape[1]
    size = nseq // 4
    core, pair, row = place & 1, (place >> 1) & 1, place >> 2
    at = ring_step(row, size)
    swap_core = [(i, i ^ 1) for i in range(nseq)]
    swap_pair = [(i, i ^ 2) for i in range(nseq)]
    walk = list(range(0, size, 2)) + list(range(1, size, 2))[::-1]
    ahead = [
        (4 * walk[i] + k, 4 * walk[(i + 1) % size] + k) for i in range(size) for k in range(4)
    ]
    behind = [(b, a) for a, b in ahead]
    send = functools.partial(lax.ppermute, axis_name="seq")

    half = feats // 2
    kept = pick(w_out, half, core)
    swapped = send(pick(w_out, half, 1 - core), perm=swap_core)
    first = jnp.where(core == 0, kept, swapped)
    second = jnp.where(core == 0, swapped, kept)

    cot_away = send(cotangent, perm=swap_pair)
    width = chans // (2 * size)
    gated_away = send(pick(gated, width, 1 - pair), perm=swap_pair)
    gated_pair = jnp.concatenate([pick(gated, width, pair), gated_away], 0)
    cot_pair = jnp.concatenate([cotangent, cot_away], 0)
    cot_mine, cot_other = pick(cot_pair, half, core), pick(cot_pair, half, 1 - core)

    dims = (((1,), (1,)), ((), ()))
    dot = functools.partial(lax.dot_general, dimension_numbers=dims, preferred_element_type=F32)
    mine, other, pieces, columns, places = [], [], [], [], []
    early = max(size - 2, 1)
    for step in range(size):
        first_row = ring_place(lax.rem(at - step + size, size), size)
        second_row = ring_place(lax.rem(at + step, size), size)
        columns += [2 * first_row, 2 * second_row + 1]
        for side in (pair, 1 - pair):
            places += [4 * first_row + 2 * side, 4 * second_row + 2 * side + 1]
    columns = jnp.stack(columns).astype(jnp.int32)
    for step in range(size):
        if step:
            if step >= 2:
                first, second, pieces[2 * step - 4 : 2 * step - 2] = lax.optimization_barrier(
                    (first, second, pieces[2 * step - 4 : 2 * step - 2])
                )
            if step == size - 2:
                first, second, gated_pair = lax.optimization_barrier((first, second, gated_pair))
            if step == size - 1:
                sums = [project(columns[: 2 * early], gated_pair, w[: 2 * early]) for w in (mine, other)]
                first, second, sums = lax.optimization_barrier((first, second, sums))
            first, second = send(first, perm=ahead), send(second, perm=behind)
        first_other, second_other = send(first, perm=swap_core), send(second, perm=swap_core)
        mine += [first, second]
        other += [first_other, second_other]
        first_grad = (dot(cot_mine, first) + dot(cot_other, first_other)).astype(BF16)
        second_grad = (dot(cot_mine, second) + dot(cot_other, second_other)).astype(BF16)
        grad = jnp.concatenate([first_grad, second_grad], 1)
        pieces += [grad[:rows], send(grad[rows:], perm=swap_pair)]
    grad_gated = assemble(jnp.stack(places).astype(jnp.int32), pieces, chans)

    outs = []
    for w, total in zip((mine, other), sums):
        own, away = project(columns[2 * early :], gated_pair, w[2 * early :], total)
        outs.append((own + send(away, perm=swap_pair).astype(F32)).astype(BF16))
    outputs = jnp.concatenate(
        [jnp.where(core == 0, outs[0], outs[1]), jnp.where(core == 0, outs[1], outs[0])], 1
    )
    return grad_gated, outputs


def on_device(queries, keys, values, w_out, taps, seg_ids, cotangent):
    rows, chans = queries.shape
    length = taps.shape[1]
    assert rows == length
    nseq = lax.axis_size("seq")
    place = lax.axis_index("seq")
    table, high, low = spectrum_table(length)
    table_now, high_now, low_now = table[:, length:], high[:, length:], low[:, length:]
    scale = 1.0 / length
    later = [(i, i + 1) for i in range(nseq - 1)]
    earlier = [(i + 1, i) for i in range(nseq - 1)]
    linked = links(seg_ids, place)

    product = mul(keys, values)
    before = lax.ppermute(product, "seq", later)
    before = jnp.where(linked, before, jnp.zeros_like(before))
    data = forward_dft(high, low, jnp.concatenate([before, product], 0), ((1,), (0,)))
    filt = forward_dft(high_now, low_now, taps, ((1,), (1,)))
    filtered = inverse_dft(table_now, times(filt, data), scale).astype(BF16)
    gated = mul(queries, filtered)

    if lax.axis_size("tp") == 1 and nseq % 4 == 0 and nseq > 4 and rows * nseq == chans:
        grad_gated, outputs = ring_products(gated, cotangent, w_out, place, nseq)
    else:
        grad_gated, outputs = gathered_products(gated, cotangent, w_out)
    grad_queries = mul(grad_gated, filtered)
    grad_filtered = mul(grad_gated, queries)
    grads = forward_dft(high_now, low_now, grad_filtered, ((1,), (0,)))
    back = inverse_dft(table, times_conj(grads, filt), scale)
    across = jnp.where(linked, back[:length], 0.0).astype(BF16)
    ahead = lax.ppermute(across, "seq", earlier)
    taps_part = inverse_dft(table_now, times_conj(grads, data), scale)
    taps_grad = scatter_sum(taps_part, nseq, place, (0, 2, 3, 4, 1)).T
    grad_product = (back[length:] + ahead.astype(F32)).astype(BF16)
    grad_keys = mul(grad_product, values)
    grad_values = mul(grad_product, keys)
    return (outputs, grad_queries, grad_keys, grad_values, taps_grad)


def solution(mesh):
    block = P("seq", "tp")
    return jax.shard_map(
        on_device,
        mesh=mesh,
        in_specs=(block, block, block, block, P("tp", None), P(), block),
        out_specs=(block, block, block, block, P(("tp", "seq"), None)),
        check_vma=False,
    )
```

```python
import functools

import jax
import jax.numpy as jnp
import numpy as np
from jax import lax
from jax.experimental import pallas as pl
from jax.experimental.pallas import tpu as pltpu
from jax.sharding import PartitionSpec as P

F32 = jnp.float32
BF16 = jnp.bfloat16


def spectrum_table(length):
    angles = np.pi * (2 * np.arange(length)[:, None] + 1) * np.arange(-length, length)[None, :] / (2 * length)
    table = np.concatenate([np.cos(angles), -np.sin(angles)], 0).astype(np.float32)
    high = table.astype(BF16)
    low = (table - high.astype(np.float32)).astype(BF16)
    return table, high, low


def forward_dft(high, low, data, dims):
    first = lax.dot_general(high, data, (dims, ((), ())), preferred_element_type=F32)
    second = lax.dot_general(low, data, (dims, ((), ())), preferred_element_type=F32)
    return first + second


def times(a, b):
    half = a.shape[0] // 2
    ar, ai, br, bi = a[:half], a[half:], b[:half], b[half:]
    return jnp.concatenate([ar * br - ai * bi, ar * bi + ai * br], 0)


def times_conj(a, b):
    half = a.shape[0] // 2
    ar, ai, br, bi = a[:half], a[half:], b[:half], b[half:]
    return jnp.concatenate([ar * br + ai * bi, ai * br - ar * bi], 0)


def inverse_dft(table, spectrum, scale):
    done = lax.dot_general(
        table, spectrum, (((0,), (0,)), ((), ())), precision=lax.Precision.HIGH, preferred_element_type=F32
    )
    return done * scale


def mul(a, b):
    return (a.astype(F32) * b.astype(F32)).astype(BF16)


def pick(data, width, side):
    blocks = [data[:, i : i + width] for i in range(0, data.shape[1], width)]
    return jnp.concatenate([jnp.where(side == 0, a, b) for a, b in zip(blocks[::2], blocks[1::2])], 1)


def scatter_sum(part, nseq, place, order):
    share = part.shape[1] // nseq
    bits = nseq.bit_length() - 1
    if nseq != 1 << bits:
        return lax.psum_scatter(part, "seq", scatter_dimension=1, tiled=True)
    left = list(range(bits))
    for step in [b for b in order if b < bits] + [b for b in range(bits) if b not in order]:
        width = share << sum(b < step for b in left)
        left.remove(step)
        mine = (place >> step) & 1
        away = pick(part, width, 1 - mine)
        if step:
            away = away.astype(BF16)
        away = lax.ppermute(away, "seq", [(i, i ^ (1 << step)) for i in range(nseq)])
        part = pick(part, width, mine) + away.astype(F32)
    return part


def links(seg_ids, place):
    own = lax.dynamic_index_in_dim(seg_ids, place, 0, False)
    prior = lax.dynamic_index_in_dim(seg_ids, jnp.maximum(place - 1, 0), 0, False)
    return (place > 0) & (own == prior)


def gathered_products(gated, cotangent, w_out):
    weights = lax.all_gather(w_out, "seq", axis=0, tiled=True)
    grad_gated = lax.dot_general(cotangent, weights, (((1,), (1,)), ((), ())), preferred_element_type=F32)
    grad_gated = lax.psum_scatter(grad_gated, "tp", scatter_dimension=1, tiled=True).astype(BF16)
    outputs = jnp.dot(
        lax.all_gather(gated, "tp", axis=1, tiled=True), weights, preferred_element_type=F32
    ).astype(BF16)
    return grad_gated, outputs


def ring_place(step, size):
    half = (size + 1) // 2
    return jnp.where(step < half, 2 * step, 2 * (size - 1 - step) + 1)


def ring_step(row, size):
    return jnp.where(row & 1 == 0, row >> 1, size - 1 - (row >> 1))


def split(data):
    high = data.astype(BF16)
    return high, (data - high.astype(F32)).astype(BF16)


def dot(a, b):
    return jnp.dot(a, b, preferred_element_type=F32)


def dot_three(high, low, data):
    data_high, data_low = split(data)
    return dot(high, data_high) + (dot(high, data_low) + dot(low, data_high))


def forward_kernel(linked_ref, fwd_hi, fwd_lo, inv_hi, inv_lo, before, product, taps, queries, *outs):
    data_ref, filt_ref, filtered_ref, gated_ref = outs
    length = product.shape[0]
    past = jnp.where(linked_ref[0] == 1, before[...].astype(F32), 0.0).astype(BF16)
    window = jnp.concatenate([past, product[...]], 0)
    data = dot(fwd_hi[...], window) + dot(fwd_lo[...], window)
    dims = (((1,), (1,)), ((), ()))
    filt = lax.dot_general(fwd_hi[:, length:], taps[...], dims, preferred_element_type=F32)
    filt = filt + lax.dot_general(fwd_lo[:, length:], taps[...], dims, preferred_element_type=F32)
    data_ref[...] = data
    filt_ref[...] = filt
    filtered = dot_three(inv_hi[length:], inv_lo[length:], times(filt, data)) * (1.0 / length)
    filtered = filtered.astype(BF16)
    filtered_ref[...] = filtered
    gated_ref[...] = mul(queries[...], filtered)


def tables(length):
    table, high, low = spectrum_table(length)
    return tuple(jnp.asarray(t) for t in (high, low, high.T, low.T))


def forward_filter(linked, before, product, taps, queries):
    length, chans = product.shape
    width = min(512, chans)
    fixed = pl.BlockSpec((2 * length, 2 * length), lambda j: (0, 0))
    block = pl.BlockSpec((length, width), lambda j: (0, j))
    spectrum = pl.BlockSpec((2 * length, width), lambda j: (0, j))
    wide = jax.ShapeDtypeStruct((2 * length, chans), F32)
    narrow = jax.ShapeDtypeStruct((length, chans), BF16)
    return pl.pallas_call(
        forward_kernel,
        out_shape=(wide, wide, narrow, narrow),
        grid=(chans // width,),
        in_specs=[pl.BlockSpec(memory_space=pltpu.SMEM)]
        + [fixed] * 4
        + [block, block, pl.BlockSpec((width, length), lambda j: (j, 0)), block],
        out_specs=(spectrum, spectrum, block, block),
        compiler_params=pltpu.CompilerParams(vmem_limit_bytes=32 << 20),
        cost_estimate=pl.CostEstimate(
            flops=24 * length * length * chans, bytes_accessed=28 * length * chans, transcendentals=0
        ),
    )(linked.astype(jnp.int32).reshape(1), *tables(length), before, product, taps, queries)


def grad_kernel(scalars, cot, first, first_other, second, second_other, own_ref, away_ref, total):
    @pl.when(pl.program_id(0) == 0)
    def _():
        total[...] = jnp.zeros_like(total)

    def add(refs):
        rows = jnp.concatenate([ref[...] for ref in refs], 0)
        dims = (((1,), (1,)), ((), ()))
        total[...] += lax.dot_general(cot[...], rows, dims, preferred_element_type=F32)

    @pl.when(scalars[0] == 0)
    def _():
        add((first, first_other, second, second_other))

    @pl.when(scalars[0] != 0)
    def _():
        add((first_other, first, second_other, second))

    @pl.when(pl.program_id(0) == pl.num_programs(0) - 1)
    def _():
        rows = own_ref.shape[0]
        own_ref[...] = total[:rows].astype(BF16)
        away_ref[...] = total[rows:].astype(BF16)


def grad_product(core, cot, weights):
    tokens, feats = cot.shape
    depth = weights[0].shape[0]
    tile = min(1024, feats)
    out = jax.ShapeDtypeStruct((tokens // 2, 4 * depth), BF16)
    whole = pl.BlockSpec(out.shape, lambda j, core: (0, 0))
    return pl.pallas_call(
        grad_kernel,
        out_shape=(out, out),
        grid_spec=pltpu.PrefetchScalarGridSpec(
            num_scalar_prefetch=1,
            grid=(feats // tile,),
            in_specs=[pl.BlockSpec((tokens, tile), lambda j, core: (0, j))]
            + [pl.BlockSpec((depth, tile), lambda j, core: (0, j))] * 4,
            out_specs=(whole, whole),
            scratch_shapes=[pltpu.VMEM((tokens, 4 * depth), F32)],
        ),
        compiler_params=pltpu.CompilerParams(vmem_limit_bytes=16 << 20),
        cost_estimate=pl.CostEstimate(
            flops=8 * tokens * depth * feats, bytes_accessed=(2 * tokens + 8 * depth) * feats, transcendentals=0
        ),
    )(core, cot, *weights)


def project_kernel(count, first, last, scalars, gated_ref, *refs):
    weights, refs = refs[: 4 * count], refs[4 * count :]
    width = 4 * weights[0].shape[0]
    total = refs[-1]
    total[...] = jnp.zeros_like(total) if first else refs[0][...]

    def add(order):
        for i in range(count):
            left = gated_ref[:, pl.ds(pl.multiple_of(scalars[1 + i] * width, width), width)]
            right = jnp.concatenate([weights[4 * i + k][...] for k in order], 0)
            total[...] += dot(left, right)

    @pl.when(scalars[0] == 0)
    def _():
        add((0, 1, 2, 3))

    @pl.when(scalars[0] != 0)
    def _():
        add((2, 3, 0, 1))

    if last:
        own_ref, away_ref = refs[-3:-1]
        rows = own_ref.shape[0]
        own_ref[...] = total[:rows]
        away_ref[...] = total[rows:].astype(BF16)
    else:
        refs[-2][...] = total[...]


def project(scalars, gated, groups, before=None, last=False):
    tokens = gated.shape[0]
    depth, feats = groups[0][0].shape
    tile = min(512, feats)
    weights = [w for group in groups for w in group]
    whole = pl.BlockSpec((tokens, tile), lambda j, s: (0, j))
    block = pl.BlockSpec((tokens // 2, tile), lambda j, s: (0, j))
    halves = tuple(jax.ShapeDtypeStruct((tokens // 2, feats), kind) for kind in (F32, BF16))
    return pl.pallas_call(
        functools.partial(project_kernel, len(groups), before is None, last),
        out_shape=halves if last else jax.ShapeDtypeStruct((tokens, feats), F32),
        grid_spec=pltpu.PrefetchScalarGridSpec(
            num_scalar_prefetch=1,
            grid=(feats // tile,),
            in_specs=[pl.BlockSpec(gated.shape, lambda j, s: (0, 0))]
            + [pl.BlockSpec((depth, tile), lambda j, s: (0, j))] * len(weights)
            + [whole] * (before is not None),
            out_specs=(block, block) if last else whole,
            scratch_shapes=[pltpu.VMEM((tokens, tile), F32)],
        ),
        compiler_params=pltpu.CompilerParams(vmem_limit_bytes=32 << 20),
        cost_estimate=pl.CostEstimate(
            flops=2 * tokens * depth * len(weights) * feats,
            bytes_accessed=2 * depth * feats * len(weights) + 2 * gated.size + 4 * tokens * feats,
            transcendentals=0,
        ),
    )(scalars, gated, *weights, *([] if before is None else [before]))


def backward_kernel(count, scalars, fwd_hi, fwd_lo, inv_hi, inv_lo, queries, filtered, data, filt, *refs):
    grads, refs = refs[: 4 * count], refs[-5:]
    grad_queries_ref, near_ref, across_ref, taps_ref, grad = refs
    length = queries.shape[0]
    depth = length // 2

    def side(first, second):
        return [ref[:, k * depth : (k + 1) * depth] for k in (0, 1) for ref in (first[:, : 2 * depth], second[:, 2 * depth :])]

    for i in range(count):
        own, away = [side(grads[4 * i + k], grads[4 * i + k + 2]) for k in (0, 1)]

        @pl.when((pl.program_id(0) == i) & (scalars[0] == 0))
        def _(own=own, away=away):
            grad[...] = jnp.concatenate(own + away, 1)

        @pl.when((pl.program_id(0) == i) & (scalars[0] != 0))
        def _(own=own, away=away):
            grad[...] = jnp.concatenate(away + own, 1)

    grad_gated = grad[...]
    grad_queries_ref[...] = mul(grad_gated, filtered[...])
    grad_filtered = mul(grad_gated, queries[...])
    grads = dot(fwd_hi[:, length:], grad_filtered) + dot(fwd_lo[:, length:], grad_filtered)
    back = dot_three(inv_hi[...], inv_lo[...], times_conj(grads, filt[...])) * (1.0 / length)
    across_ref[...] = jnp.where(scalars[1] == 1, back[:length], 0.0).astype(BF16)
    near_ref[...] = back[length:]
    taps_ref[...] = dot_three(inv_hi[length:], inv_lo[length:], times_conj(grads, data[...])) * (1.0 / length)


def backward_filter(scalars, groups, queries, filtered, data, filt, before=None):
    length, chans = queries.shape
    width = 4 * length
    count = len(groups)
    pieces = [p for group in groups for p in group]
    fixed = pl.BlockSpec((2 * length, 2 * length), lambda j, s: (0, 0))
    block = pl.BlockSpec((length, width), lambda j, s: (0, s[2 + j]))
    spectrum = pl.BlockSpec((2 * length, width), lambda j, s: (0, s[2 + j]))
    piece = pl.BlockSpec((length, 2 * length), lambda j, s: (0, 0))
    before = [] if before is None else list(before)
    inputs = 9 + len(pieces)
    return pl.pallas_call(
        functools.partial(backward_kernel, count),
        out_shape=tuple(jax.ShapeDtypeStruct((length, chans), kind) for kind in (BF16, F32, BF16, F32)),
        grid_spec=pltpu.PrefetchScalarGridSpec(
            num_scalar_prefetch=1,
            grid=(count,),
            in_specs=[fixed] * 4
            + [block, block, spectrum, spectrum]
            + [piece] * len(pieces)
            + [pl.BlockSpec(memory_space=pl.ANY)] * len(before),
            out_specs=(block,) * 4,
            scratch_shapes=[pltpu.VMEM((length, width), BF16)],
        ),
        input_output_aliases={inputs + i: i for i in range(len(before))},
        compiler_params=pltpu.CompilerParams(vmem_limit_bytes=32 << 20),
        cost_estimate=pl.CostEstimate(
            flops=28 * length * length * width * count, bytes_accessed=34 * length * width * count, transcendentals=0
        ),
    )(scalars, *tables(length), queries, filtered, data, filt, *pieces, *before)


def on_ring(queries, keys, values, w_out, taps, seg_ids, cotangent):
    rows, chans = queries.shape
    nseq = lax.axis_size("seq")
    place = lax.axis_index("seq")
    size = nseq // 4
    core, pair, row = place & 1, (place >> 1) & 1, place >> 2
    at = ring_step(row, size)
    swap_core = [(i, i ^ 1) for i in range(nseq)]
    swap_pair = [(i, i ^ 2) for i in range(nseq)]
    walk = list(range(0, size, 2)) + list(range(1, size, 2))[::-1]
    onward = [(4 * walk[i] + k, 4 * walk[(i + 1) % size] + k) for i in range(size) for k in range(4)]
    backward = [(b, a) for a, b in onward]
    later = [(i, i + 1) for i in range(nseq - 1)]
    earlier = [(i + 1, i) for i in range(nseq - 1)]
    send = functools.partial(lax.ppermute, axis_name="seq")
    linked = links(seg_ids, place)

    first, second = w_out[: rows // 2], w_out[rows // 2 :]
    cot_pair = jnp.concatenate([cotangent, send(cotangent, perm=swap_pair)], 0)
    product = mul(keys, values)
    before = send(product, perm=later)
    data, filt, filtered, gated = forward_filter(linked, before, product, taps, queries)
    width = 2 * rows
    gated_away = send(pick(gated, width, 1 - pair), perm=swap_pair)
    gated_pair = jnp.concatenate([pick(gated, width, pair), gated_away], 0)

    ready = [max(s, size - s) if s else 0 for s in range(size)]
    groups_at = {t: [s for s in range(size) if ready[s] == t] for t in range(size)}
    early = max(size - 3, 0)
    stages = {early: [s for s in range(size) if ready[s] <= early]}
    for t in range(early + 1, size):
        stages[t] = groups_at[t]
    block = [ring_place(lax.rem(at - s + size, size), size).astype(jnp.int32) for s in range(size)]
    core = core.astype(jnp.int32)
    core_only = core.reshape(1)
    firsts, seconds, own, away = [], [], [], []
    sums = back = None
    for step in range(size):
        if step:
            if step >= 2:
                first, second, own[step - 2], away[step - 2] = lax.optimization_barrier(
                    (first, second, own[step - 2], away[step - 2])
                )
            if step == 2:
                first, second, gated = lax.optimization_barrier((first, second, gated))
            if step - 2 in stages and step - 2 < size - 1:
                first, second, sums, back = lax.optimization_barrier((first, second, sums, back))
            first, second = send(first, perm=onward), send(second, perm=backward)
        firsts.append((first, send(first, perm=swap_core)))
        seconds.append((second, send(second, perm=swap_core)))
        mine, theirs = grad_product(core_only, cot_pair, firsts[step] + seconds[step])
        own.append(mine)
        away.append(send(theirs, perm=swap_pair))
        if step in stages and stages[step]:
            sets = stages[step]
            blocks = [block[s] for s in sets]
            mirror = [(size - s) % size for s in sets]
            groups = [
                (firsts[s][0], seconds[m][0], firsts[s][1], seconds[m][1]) for s, m in zip(sets, mirror)
            ]
            sums = project(
                jnp.stack([core] + blocks), gated_pair, groups, sums, step == size - 1
            )
            groups = [(own[s], away[s], own[m], away[m]) for s, m in zip(sets, mirror)]
            scalars = jnp.stack([pair.astype(jnp.int32), linked.astype(jnp.int32)] + blocks)
            back = backward_filter(scalars, groups, queries, filtered, data, filt, back)
    grad_queries, near, across, taps_part = back
    ahead = send(across, perm=earlier)
    taps_grad = scatter_sum(taps_part, nseq, place, (0, 2, 3, 4, 1)).T
    out_own, out_away = sums
    outputs = (out_own + send(out_away, perm=swap_pair).astype(F32)).astype(BF16)
    grad_product_ = (near + ahead.astype(F32)).astype(BF16)
    grad_keys = mul(grad_product_, values)
    grad_values = mul(grad_product_, keys)
    return (outputs, grad_queries, grad_keys, grad_values, taps_grad)


def on_device(queries, keys, values, w_out, taps, seg_ids, cotangent):
    rows, chans = queries.shape
    length = taps.shape[1]
    assert rows == length
    nseq = lax.axis_size("seq")
    place = lax.axis_index("seq")
    table, high, low = spectrum_table(length)
    table_now, high_now, low_now = table[:, length:], high[:, length:], low[:, length:]
    scale = 1.0 / length
    later = [(i, i + 1) for i in range(nseq - 1)]
    earlier = [(i + 1, i) for i in range(nseq - 1)]
    linked = links(seg_ids, place)

    product = mul(keys, values)
    before = lax.ppermute(product, "seq", later)
    before = jnp.where(linked, before, jnp.zeros_like(before))
    data = forward_dft(high, low, jnp.concatenate([before, product], 0), ((1,), (0,)))
    filt = forward_dft(high_now, low_now, taps, ((1,), (1,)))
    filtered = inverse_dft(table_now, times(filt, data), scale).astype(BF16)
    gated = mul(queries, filtered)

    grad_gated, outputs = gathered_products(gated, cotangent, w_out)
    grad_queries = mul(grad_gated, filtered)
    grad_filtered = mul(grad_gated, queries)
    grads = forward_dft(high_now, low_now, grad_filtered, ((1,), (0,)))
    back = inverse_dft(table, times_conj(grads, filt), scale)
    across = jnp.where(linked, back[:length], 0.0).astype(BF16)
    ahead = lax.ppermute(across, "seq", earlier)
    taps_part = inverse_dft(table_now, times_conj(grads, data), scale)
    taps_grad = scatter_sum(taps_part, nseq, place, (0, 2, 3, 4, 1)).T
    grad_product = (back[length:] + ahead.astype(F32)).astype(BF16)
    grad_keys = mul(grad_product, values)
    grad_values = mul(grad_product, keys)
    return (outputs, grad_queries, grad_keys, grad_values, taps_grad)


def solution(mesh):
    block = P("seq", "tp")
    ring = mesh.shape["tp"] == 1 and mesh.shape["seq"] % 4 == 0 and mesh.shape["seq"] > 4

    def run(queries, keys, values, w_out, taps, seg_ids, cotangent):
        rows, chans = queries.shape
        place = on_ring if ring and rows * lax.axis_size("seq") == chans else on_device
        return place(queries, keys, values, w_out, taps, seg_ids, cotangent)

    return jax.shard_map(
        run,
        mesh=mesh,
        in_specs=(block, block, block, block, P("tp", None), P(), block),
        out_specs=(block, block, block, block, P(("tp", "seq"), None)),
        check_vma=False,
    )
```

```python
import functools

import jax
import jax.numpy as jnp
import numpy as np
from jax import lax
from jax.experimental import pallas as pl
from jax.experimental.pallas import tpu as pltpu
from jax.sharding import PartitionSpec as P

F32 = jnp.float32
BF16 = jnp.bfloat16


def spectrum_table(length):
    angles = np.pi * (2 * np.arange(length)[:, None] + 1) * np.arange(-length, length)[None, :] / (2 * length)
    table = np.concatenate([np.cos(angles), -np.sin(angles)], 0).astype(np.float32)
    high = table.astype(BF16)
    low = (table - high.astype(np.float32)).astype(BF16)
    return table, high, low


def forward_dft(high, low, data, dims):
    first = lax.dot_general(high, data, (dims, ((), ())), preferred_element_type=F32)
    second = lax.dot_general(low, data, (dims, ((), ())), preferred_element_type=F32)
    return first + second


def times(a, b):
    half = a.shape[0] // 2
    ar, ai, br, bi = a[:half], a[half:], b[:half], b[half:]
    return jnp.concatenate([ar * br - ai * bi, ar * bi + ai * br], 0)


def times_conj(a, b):
    half = a.shape[0] // 2
    ar, ai, br, bi = a[:half], a[half:], b[:half], b[half:]
    return jnp.concatenate([ar * br + ai * bi, ai * br - ar * bi], 0)


def inverse_dft(table, spectrum, scale):
    done = lax.dot_general(
        table, spectrum, (((0,), (0,)), ((), ())), precision=lax.Precision.HIGH, preferred_element_type=F32
    )
    return done * scale


def mul(a, b):
    return (a.astype(F32) * b.astype(F32)).astype(BF16)


def scatter_sum(part, nseq, place):
    bits = nseq.bit_length() - 1
    lags = part.shape[-2]
    chans = part.shape[-1]
    for step in range(bits):
        mine = (place >> step) & 1
        part = part.reshape(-1, 2, lags, chans)
        away = lax.dynamic_index_in_dim(part, 1 - mine, 1, False)
        kept = lax.dynamic_index_in_dim(part, mine, 1, False)
        if step:
            away = away.astype(BF16)
        away = lax.ppermute(away, "seq", [(i, i ^ (1 << step)) for i in range(nseq)])
        part = kept + away.astype(F32)
    return part[0]


def sum_over_ring(part, nseq, place):
    core, pair, row = place & 1, (place >> 1) & 1, place >> 2
    four, size, lags, chans = part.shape

    def halve(part, bit, mine, kind):
        away = lax.dynamic_index_in_dim(part, 1 - mine, 1, False).astype(kind)
        away = lax.ppermute(away, "seq", [(i, i ^ bit) for i in range(nseq)])
        return lax.dynamic_index_in_dim(part, mine, 1, False) + away.astype(F32)

    part = halve(part.reshape(2, 2, size, lags, chans), 1, core, F32)
    part = halve(part.reshape(1, 2, size, lags, chans), 2, pair, BF16).reshape(size, lags, chans)
    if size & (size - 1):
        return lax.psum_scatter(
            part, "seq", scatter_dimension=0,
            axis_index_groups=[[4 * r + k for r in range(size)] for k in range(4)],
        )
    left = size
    while left > 1:
        bit = size // left
        part = halve(part.reshape(left // 2, 2, lags, chans), 4 * bit, (row // bit) & 1, BF16)
        left //= 2
    return part.reshape(lags, chans)


def links(seg_ids, place):
    own = lax.dynamic_index_in_dim(seg_ids, place, 0, False)
    prior = lax.dynamic_index_in_dim(seg_ids, jnp.maximum(place - 1, 0), 0, False)
    return (place > 0) & (own == prior)


def gathered_products(gated, cotangent, w_out):
    weights = lax.all_gather(w_out, "seq", axis=0, tiled=True)
    grad_gated = lax.dot_general(cotangent, weights, (((1,), (1,)), ((), ())), preferred_element_type=F32)
    grad_gated = lax.psum_scatter(grad_gated, "tp", scatter_dimension=1, tiled=True).astype(BF16)
    outputs = jnp.dot(
        lax.all_gather(gated, "tp", axis=1, tiled=True), weights, preferred_element_type=F32
    ).astype(BF16)
    return grad_gated, outputs


def ring_place(step, size):
    half = (size + 1) // 2
    return jnp.where(step < half, 2 * step, 2 * (size - 1 - step) + 1)


def ring_step(row, size):
    return jnp.where(row & 1 == 0, row >> 1, size - 1 - (row >> 1))


def split(data):
    high = data.astype(BF16)
    return high, (data - high.astype(F32)).astype(BF16)


def dot(a, b):
    return jnp.dot(a, b, preferred_element_type=F32)


def dot_three(high, low, data):
    data_high, data_low = split(data)
    return dot(high, data_high) + (dot(high, data_low) + dot(low, data_high))


def forward_kernel(linked_ref, fwd_hi, fwd_lo, inv_hi, inv_lo, before, product, taps, queries, *outs):
    data_ref, filt_ref, filtered_ref, gated_ref = outs
    length = product.shape[0]
    past = jnp.where(linked_ref[0] == 1, before[...].astype(F32), 0.0).astype(BF16)
    window = jnp.concatenate([past, product[...]], 0)
    data = dot(fwd_hi[...], window) + dot(fwd_lo[...], window)
    dims = (((1,), (1,)), ((), ()))
    filt = lax.dot_general(fwd_hi[:, length:], taps[...], dims, preferred_element_type=F32)
    filt = filt + lax.dot_general(fwd_lo[:, length:], taps[...], dims, preferred_element_type=F32)
    data_ref[...] = data
    filt_ref[...] = filt
    filtered = dot_three(inv_hi[length:], inv_lo[length:], times(filt, data)) * (1.0 / length)
    filtered = filtered.astype(BF16)
    filtered_ref[...] = filtered
    gated = mul(queries[...], filtered)
    half = gated.shape[1] // 2
    gated_ref[0] = gated[:, :half]
    gated_ref[1] = gated[:, half:]


def tables(length):
    table, high, low = spectrum_table(length)
    return tuple(jnp.asarray(t) for t in (high, low, high.T, low.T))


def forward_filter(linked, before, product, taps, queries):
    length, chans = product.shape
    width = 4 * length
    fixed = pl.BlockSpec((2 * length, 2 * length), lambda j: (0, 0))
    block = pl.BlockSpec((length, width), lambda j: (0, j))
    spectrum = pl.BlockSpec((2 * length, width), lambda j: (0, j))
    wide = jax.ShapeDtypeStruct((2 * length, chans), F32)
    narrow = jax.ShapeDtypeStruct((length, chans), BF16)
    return pl.pallas_call(
        forward_kernel,
        out_shape=(wide, wide, narrow, jax.ShapeDtypeStruct((2, length, chans // 2), BF16)),
        grid=(chans // width,),
        in_specs=[pl.BlockSpec(memory_space=pltpu.SMEM)]
        + [fixed] * 4
        + [block, block, pl.BlockSpec((width, length), lambda j: (j, 0)), block],
        out_specs=(spectrum, spectrum, block, pl.BlockSpec((2, length, width // 2), lambda j: (0, 0, j))),
        compiler_params=pltpu.CompilerParams(vmem_limit_bytes=12 << 20),
        cost_estimate=pl.CostEstimate(
            flops=24 * length * length * chans, bytes_accessed=28 * length * chans, transcendentals=0
        ),
    )(linked.astype(jnp.int32).reshape(1), *tables(length), before, product, taps, queries)


def grad_kernel(scalars, cot_own, cot_away, first, first_other, second, second_other, own_ref, away_ref, total):
    @pl.when(pl.program_id(0) == 0)
    def _():
        total[...] = jnp.zeros_like(total)

    def add(refs):
        rows = jnp.concatenate([ref[...] for ref in refs], 0)
        dims = (((1,), (1,)), ((), ()))
        cot = jnp.concatenate([cot_own[...], cot_away[...]], 0)
        total[...] += lax.dot_general(cot, rows, dims, preferred_element_type=F32)

    @pl.when(scalars[0] == 0)
    def _():
        add((first, first_other, second, second_other))

    @pl.when(scalars[0] != 0)
    def _():
        add((first_other, first, second_other, second))

    @pl.when(pl.program_id(0) == pl.num_programs(0) - 1)
    def _():
        rows = own_ref.shape[0]
        own_ref[...] = total[:rows].astype(BF16)
        away_ref[...] = total[rows:].astype(BF16)


def grad_product(core, cot_own, cot_away, weights):
    rows, feats = cot_own.shape
    tokens = 2 * rows
    depth = weights[0].shape[0]
    tile = min(1024, feats)
    out = jax.ShapeDtypeStruct((rows, 4 * depth), BF16)
    whole = pl.BlockSpec(out.shape, lambda j, core: (0, 0))
    return pl.pallas_call(
        grad_kernel,
        out_shape=(out, out),
        grid_spec=pltpu.PrefetchScalarGridSpec(
            num_scalar_prefetch=1,
            grid=(feats // tile,),
            in_specs=[pl.BlockSpec((rows, tile), lambda j, core: (0, j))] * 2
            + [pl.BlockSpec((depth, tile), lambda j, core: (0, j))] * 4,
            out_specs=(whole, whole),
            scratch_shapes=[pltpu.VMEM((tokens, 4 * depth), F32)],
        ),
        compiler_params=pltpu.CompilerParams(vmem_limit_bytes=8 << 20),
        cost_estimate=pl.CostEstimate(
            flops=8 * tokens * depth * feats, bytes_accessed=(2 * tokens + 8 * depth) * feats, transcendentals=0
        ),
    )(core, cot_own, cot_away, *weights)


def project_kernel(count, first, last, scalars, gated_own, gated_away, *refs):
    weights, refs = refs[: 4 * count], refs[4 * count :]
    depth = weights[0].shape[0]
    width = 4 * depth
    left, total = refs[-2:]

    @pl.when(pl.program_id(0) == 0)
    def _():
        for i in range(count):
            for part, ref in enumerate((gated_own, gated_away)):
                blocks = [
                    ref[:, pl.ds(pl.multiple_of(scalars[1 + 2 * i + way] * width, width), width)] for way in (0, 1)
                ]
                rows = ref.shape[0]
                left[i, part * rows : (part + 1) * rows] = jnp.concatenate(
                    [blocks[way][:, (2 * k + way) * depth : (2 * k + way + 1) * depth] for way in (0, 1) for k in (0, 1)],
                    1,
                )

    total[...] = jnp.zeros_like(total) if first else refs[0][...]

    def add(order):
        for i in range(count):
            right = jnp.concatenate([weights[4 * i + k][...] for k in order], 0)
            total[...] += dot(left[i], right)

    @pl.when(scalars[0] == 0)
    def _():
        add((0, 1, 2, 3))

    @pl.when(scalars[0] != 0)
    def _():
        add((1, 0, 3, 2))

    if last:
        own_ref, away_ref = refs[-4:-2]
        rows = own_ref.shape[0]
        own_ref[...] = total[:rows]
        away_ref[...] = total[rows:].astype(BF16)
    else:
        refs[-3][...] = total[...]


def project(scalars, gated_own, gated_away, groups, before=None, last=False):
    rows, chans = gated_own.shape
    depth, feats = groups[0][0].shape
    tile = min(1024, feats)
    weights = [w for group in groups for w in group]
    whole = pl.BlockSpec((2 * rows, tile), lambda j, s: (0, j))
    block = pl.BlockSpec((rows, tile), lambda j, s: (0, j))
    halves = tuple(jax.ShapeDtypeStruct((rows, feats), kind) for kind in (F32, BF16))
    return pl.pallas_call(
        functools.partial(project_kernel, len(groups), before is None, last),
        out_shape=halves if last else jax.ShapeDtypeStruct((2 * rows, feats), F32),
        grid_spec=pltpu.PrefetchScalarGridSpec(
            num_scalar_prefetch=1,
            grid=(feats // tile,),
            in_specs=[pl.BlockSpec(gated_own.shape, lambda j, s: (0, 0))] * 2
            + [pl.BlockSpec((depth, tile), lambda j, s: (0, j))] * len(weights)
            + [whole] * (before is not None),
            out_specs=(block, block) if last else whole,
            scratch_shapes=[
                pltpu.VMEM((len(groups), 2 * rows, 4 * depth), BF16),
                pltpu.VMEM((2 * rows, tile), F32),
            ],
        ),
        compiler_params=pltpu.CompilerParams(vmem_limit_bytes=16 << 20),
        cost_estimate=pl.CostEstimate(
            flops=4 * rows * depth * len(weights) * feats,
            bytes_accessed=2 * depth * feats * len(weights) + 4 * rows * chans + 8 * rows * feats,
            transcendentals=0,
        ),
    )(scalars, gated_own, gated_away, *weights, *([] if before is None else [before]))


def backward_kernel(count, scalars, fwd_hi, fwd_lo, inv_hi, inv_lo, queries, filtered, data, filt, *refs):
    grads, refs = refs[: 4 * count], refs[-5:]
    grad_queries_ref, near_ref, across_ref, taps_ref, grad = refs
    length = queries.shape[0]
    depth = length // 2

    def side(first, second):
        return [ref[:, k * depth : (k + 1) * depth] for k in (0, 1) for ref in (first[:, : 2 * depth], second[:, 2 * depth :])]

    for i in range(count):
        own, away = [side(grads[4 * i + k], grads[4 * i + k + 2]) for k in (0, 1)]

        @pl.when((pl.program_id(0) == i) & (scalars[0] == 0))
        def _(own=own, away=away):
            grad[...] = jnp.concatenate(own + away, 1)

        @pl.when((pl.program_id(0) == i) & (scalars[0] != 0))
        def _(own=own, away=away):
            grad[...] = jnp.concatenate(away + own, 1)

    grad_gated = grad[...]
    grad_queries_ref[...] = mul(grad_gated, filtered[...])
    grad_filtered = mul(grad_gated, queries[...])
    grads = dot(fwd_hi[:, length:], grad_filtered) + dot(fwd_lo[:, length:], grad_filtered)
    back = dot_three(inv_hi[...], inv_lo[...], times_conj(grads, filt[...])) * (1.0 / length)
    across_ref[0] = jnp.where(scalars[1] == 1, back[:length], 0.0).astype(BF16)
    near_ref[...] = back[length:]
    taps = dot_three(inv_hi[length:], inv_lo[length:], times_conj(grads, data[...])) * (1.0 / length)
    for k in range(4):
        taps_ref[k, 0] = taps[:, k * length : (k + 1) * length]


def backward_filter(scalars, groups, queries, filtered, data, filt, before=None):
    length, chans = queries.shape
    width = 4 * length
    count = len(groups)
    pieces = [p for group in groups for p in group]
    fixed = pl.BlockSpec((2 * length, 2 * length), lambda j, s: (0, 0))
    block = pl.BlockSpec((length, width), lambda j, s: (0, s[2 + j]))
    spectrum = pl.BlockSpec((2 * length, width), lambda j, s: (0, s[2 + j]))
    piece = pl.BlockSpec((length, 2 * length), lambda j, s: (0, 0))
    before = [] if before is None else [before[0], before[1], before[3]]
    inputs = 9 + len(pieces)
    return pl.pallas_call(
        functools.partial(backward_kernel, count),
        out_shape=(
            jax.ShapeDtypeStruct((length, chans), BF16),
            jax.ShapeDtypeStruct((length, chans), F32),
            jax.ShapeDtypeStruct((count, length, width), BF16),
            jax.ShapeDtypeStruct((4, chans // width, length, length), F32),
        ),
        grid_spec=pltpu.PrefetchScalarGridSpec(
            num_scalar_prefetch=1,
            grid=(count,),
            in_specs=[fixed] * 4
            + [block, block, spectrum, spectrum]
            + [piece] * len(pieces)
            + [pl.BlockSpec(memory_space=pl.ANY)] * len(before),
            out_specs=(
                block,
                block,
                pl.BlockSpec((1, length, width), lambda j, s: (j, 0, 0)),
                pl.BlockSpec((4, 1, length, length), lambda j, s: (0, s[2 + j], 0, 0)),
            ),
            scratch_shapes=[pltpu.VMEM((length, width), BF16)],
        ),
        input_output_aliases={inputs + i: out for i, out in zip(range(len(before)), (0, 1, 3))},
        compiler_params=pltpu.CompilerParams(vmem_limit_bytes=16 << 20),
        cost_estimate=pl.CostEstimate(
            flops=28 * length * length * width * count, bytes_accessed=34 * length * width * count, transcendentals=0
        ),
    )(scalars, *tables(length), queries, filtered, data, filt, *pieces, *before)


def join_kernel(count, scalars, near, keys, values, *refs):
    parts, (grad_keys, grad_values) = refs[:count], refs[count:]
    j = pl.program_id(0)
    total = near[...]
    for i, part in enumerate(parts):
        total = total + jnp.where(scalars[j] == i, part[0].astype(F32), 0.0)
    total = total.astype(BF16)
    grad_keys[...] = mul(total, values[...])
    grad_values[...] = mul(total, keys[...])


def join(scalars, near, keys, values, parts):
    length, chans = near.shape
    width = parts[0].shape[2]
    count = chans // width
    block = pl.BlockSpec((length, width), lambda j, s: (0, j))
    out = jax.ShapeDtypeStruct((length, chans), BF16)

    def place(i):
        return lambda j, s: (s[(1 + i) * count + j], 0, 0)

    return pl.pallas_call(
        functools.partial(join_kernel, len(parts)),
        out_shape=(out, out),
        grid_spec=pltpu.PrefetchScalarGridSpec(
            num_scalar_prefetch=1,
            grid=(count,),
            in_specs=[block] * 3 + [pl.BlockSpec((1, length, width), place(i)) for i in range(len(parts))],
            out_specs=(block, block),
        ),
        compiler_params=pltpu.CompilerParams(vmem_limit_bytes=6 << 20),
        cost_estimate=pl.CostEstimate(flops=4 * length * chans, bytes_accessed=14 * length * chans, transcendentals=0),
    )(scalars, near, keys, values, *parts)


def on_ring(queries, keys, values, w_out, taps, seg_ids, cotangent):
    rows, chans = queries.shape
    nseq = lax.axis_size("seq")
    place = lax.axis_index("seq")
    size = nseq // 4
    core, pair, row = place & 1, (place >> 1) & 1, place >> 2
    at = ring_step(row, size)
    swap_core = [(i, i ^ 1) for i in range(nseq)]
    swap_pair = [(i, i ^ 2) for i in range(nseq)]
    walk = list(range(0, size, 2)) + list(range(1, size, 2))[::-1]
    onward = [(4 * walk[i] + k, 4 * walk[(i + 1) % size] + k) for i in range(size) for k in range(4)]
    backward = [(b, a) for a, b in onward]
    later = [(i, i + 1) for i in range(nseq - 1)]
    earlier = [(i + 1, i) for i in range(nseq - 1)]
    send = functools.partial(lax.ppermute, axis_name="seq")
    tie = lax.optimization_barrier
    linked = links(seg_ids, place)

    half = rows // 2
    first, second = w_out[:half], w_out[half:]
    cot_away = send(cotangent, perm=swap_pair)
    swapped = send(w_out, perm=swap_core)
    product, cot_away = tie((mul(keys, values), cot_away))
    before = send(product, perm=later)
    data, filt, filtered, gated = forward_filter(linked, before, product, taps, queries)
    gated_own = lax.dynamic_index_in_dim(gated, pair, 0, False)
    gated_away = send(lax.dynamic_index_in_dim(gated, 1 - pair, 0, False), perm=swap_pair)

    ready = [max(s, size - s) if s else 0 for s in range(size)]
    early = max(size - 3, 0)
    stages = {early: [s for s in range(size) if ready[s] <= early]}
    for t in range(early + 1, size):
        stages[t] = [s for s in range(size) if ready[s] == t]
    stages = {t: sets for t, sets in stages.items() if sets}
    block = [ring_place(lax.rem(at - s + size, size), size).astype(jnp.int32) for s in range(size)]
    core = core.astype(jnp.int32)
    core_only = core.reshape(1)
    cut = max(size - 3, 1)
    firsts, seconds, own, away, parts = [], [], [], [], []
    sums = back = None
    kept = {}

    def projected(steps, sums, last):
        groups = [firsts[s] + seconds[s] for s in steps]
        places = [b for s in steps for b in (block[s], block[(size - s) % size])]
        return project(jnp.stack([core] + places), gated_own, gated_away, groups, sums, last)

    for step in range(size):
        if step:
            if step >= 2:
                first, second, own[step - 2], away[step - 2] = tie((first, second, own[step - 2], away[step - 2]))
            if step == 3:
                first, second, gated_away = tie((first, second, gated_away))
            if step == cut + 1 and sums is not None:
                first, second, sums = tie((first, second, sums))
            if step - 2 in stages:
                first, second, kept[step - 2] = tie((first, second, kept[step - 2]))
            first, second = send(first, perm=onward), send(second, perm=backward)
            firsts.append((first, send(first, perm=swap_core)))
            seconds.append((second, send(second, perm=swap_core)))
        else:
            firsts.append((first, swapped[:half]))
            seconds.append((second, swapped[half:]))
        if step == size - 1 and back is not None:
            firsts[step], seconds[step], back, parts[0] = tie((firsts[step], seconds[step], back, parts[0]))
        mine, theirs = grad_product(core_only, cotangent, cot_away, firsts[step] + seconds[step])
        own.append(mine)
        away.append(send(theirs, perm=swap_pair))
        if step == cut - 1:
            sums = projected(range(cut), None, False)
        if step == size - 1:
            sums = projected(range(cut, size), sums, True)
        if step in stages:
            sets = stages[step]
            mirror = [(size - s) % size for s in sets]
            groups = [(own[s], away[s], own[m], away[m]) for s, m in zip(sets, mirror)]
            scalars = jnp.stack([pair.astype(jnp.int32), linked.astype(jnp.int32)] + [block[s] for s in sets])
            back = backward_filter(scalars, groups, queries, filtered, data, filt, back)
            kept[step] = back[2]
            parts.append(send(back[2], perm=earlier))
    grad_queries, near, _, taps_part = back
    taps_grad = sum_over_ring(taps_part, nseq, place).T
    out_own, out_away = sums
    outputs = (out_own + send(out_away, perm=swap_pair).astype(F32)).astype(BF16)

    source = ring_step(jnp.minimum(place + 1, nseq - 1) >> 2, size)
    stage_of, place_in = np.zeros(size, np.int32), np.zeros((len(stages), size), np.int32)
    for i, sets in enumerate(stages.values()):
        for k, s in enumerate(sets):
            stage_of[s], place_in[i, s] = i, k
    table = np.concatenate([stage_of[None], place_in], 0)
    steps = jnp.stack([lax.rem(source - ring_step(jnp.int32(r), size) + size, size) for r in range(size)])
    scalars = jnp.take(jnp.asarray(table), steps, axis=1).reshape(-1)
    grad_keys, grad_values = join(scalars, near, keys, values, parts)
    return (outputs, grad_queries, grad_keys, grad_values, taps_grad)


def on_device(queries, keys, values, w_out, taps, seg_ids, cotangent):
    rows, chans = queries.shape
    length = taps.shape[1]
    assert rows == length
    nseq = lax.axis_size("seq")
    place = lax.axis_index("seq")
    table, high, low = spectrum_table(length)
    table_now, high_now, low_now = table[:, length:], high[:, length:], low[:, length:]
    scale = 1.0 / length
    later = [(i, i + 1) for i in range(nseq - 1)]
    earlier = [(i + 1, i) for i in range(nseq - 1)]
    linked = links(seg_ids, place)

    product = mul(keys, values)
    before = lax.ppermute(product, "seq", later)
    before = jnp.where(linked, before, jnp.zeros_like(before))
    data = forward_dft(high, low, jnp.concatenate([before, product], 0), ((1,), (0,)))
    filt = forward_dft(high_now, low_now, taps, ((1,), (1,)))
    filtered = inverse_dft(table_now, times(filt, data), scale).astype(BF16)
    gated = mul(queries, filtered)

    grad_gated, outputs = gathered_products(gated, cotangent, w_out)
    grad_queries = mul(grad_gated, filtered)
    grad_filtered = mul(grad_gated, queries)
    grads = forward_dft(high_now, low_now, grad_filtered, ((1,), (0,)))
    back = inverse_dft(table, times_conj(grads, filt), scale)
    across = jnp.where(linked, back[:length], 0.0).astype(BF16)
    ahead = lax.ppermute(across, "seq", earlier)
    taps_part = inverse_dft(table_now, times_conj(grads, data), scale)
    if nseq & (nseq - 1):
        taps_grad = lax.psum_scatter(taps_part.T, "seq", scatter_dimension=0, tiled=True)
    else:
        blocks = taps_part.reshape(length, nseq, -1).transpose(1, 0, 2)
        taps_grad = scatter_sum(blocks, nseq, place).T
    grad_product = (back[length:] + ahead.astype(F32)).astype(BF16)
    grad_keys = mul(grad_product, values)
    grad_values = mul(grad_product, keys)
    return (outputs, grad_queries, grad_keys, grad_values, taps_grad)


def solution(mesh):
    block = P("seq", "tp")
    ring = mesh.shape["tp"] == 1 and mesh.shape["seq"] % 4 == 0 and mesh.shape["seq"] > 4

    def run(queries, keys, values, w_out, taps, seg_ids, cotangent):
        rows, chans = queries.shape
        place = on_ring if ring and rows * lax.axis_size("seq") == chans else on_device
        return place(queries, keys, values, w_out, taps, seg_ids, cotangent)

    return jax.shard_map(
        run,
        mesh=mesh,
        in_specs=(block, block, block, block, P("tp", None), P(), block),
        out_specs=(block, block, block, block, P(("tp", "seq"), None)),
        check_vma=False,
    )
```

```python
import functools

import jax
import jax.numpy as jnp
import numpy as np
from jax import lax
from jax.experimental import pallas as pl
from jax.experimental.pallas import tpu as pltpu
from jax.sharding import PartitionSpec as P

F32 = jnp.float32
BF16 = jnp.bfloat16


def spectrum_table(length):
    angles = np.pi * (2 * np.arange(length)[:, None] + 1) * np.arange(-length, length)[None, :] / (2 * length)
    table = np.concatenate([np.cos(angles), -np.sin(angles)], 0).astype(np.float32)
    high = table.astype(BF16)
    low = (table - high.astype(np.float32)).astype(BF16)
    return table, high, low


def forward_dft(high, low, data, dims):
    first = lax.dot_general(high, data, (dims, ((), ())), preferred_element_type=F32)
    second = lax.dot_general(low, data, (dims, ((), ())), preferred_element_type=F32)
    return first + second


def times(a, b):
    half = a.shape[0] // 2
    ar, ai, br, bi = a[:half], a[half:], b[:half], b[half:]
    return jnp.concatenate([ar * br - ai * bi, ar * bi + ai * br], 0)


def times_conj(a, b):
    half = a.shape[0] // 2
    ar, ai, br, bi = a[:half], a[half:], b[:half], b[half:]
    return jnp.concatenate([ar * br + ai * bi, ai * br - ar * bi], 0)


def inverse_dft(table, spectrum, scale):
    done = lax.dot_general(
        table, spectrum, (((0,), (0,)), ((), ())), precision=lax.Precision.HIGH, preferred_element_type=F32
    )
    return done * scale


def mul(a, b):
    return (a.astype(F32) * b.astype(F32)).astype(BF16)


def scatter_sum(part, nseq, place):
    bits = nseq.bit_length() - 1
    lags = part.shape[-2]
    chans = part.shape[-1]
    for step in range(bits):
        mine = (place >> step) & 1
        part = part.reshape(-1, 2, lags, chans)
        away = lax.dynamic_index_in_dim(part, 1 - mine, 1, False)
        kept = lax.dynamic_index_in_dim(part, mine, 1, False)
        if step:
            away = away.astype(BF16)
        away = lax.ppermute(away, "seq", [(i, i ^ (1 << step)) for i in range(nseq)])
        part = kept + away.astype(F32)
    return part[0]


def sum_over_ring(part, nseq, place):
    core, pair, row = place & 1, (place >> 1) & 1, place >> 2
    four, size, lags, chans = part.shape

    def halve(part, bit, mine, kind):
        away = lax.dynamic_index_in_dim(part, 1 - mine, 1, False).astype(kind)
        away = lax.ppermute(away, "seq", [(i, i ^ bit) for i in range(nseq)])
        return lax.dynamic_index_in_dim(part, mine, 1, False) + away.astype(F32)

    part = halve(part.reshape(2, 2, size, lags, chans), 1, core, F32)
    part = halve(part.reshape(1, 2, size, lags, chans), 2, pair, BF16).reshape(size, lags, chans)
    left = size
    while left > 1:
        bit = size // left
        part = halve(part.reshape(left // 2, 2, lags, chans), 4 * bit, (row // bit) & 1, BF16)
        left //= 2
    return part.reshape(lags, chans)


def links(seg_ids, place):
    own = lax.dynamic_index_in_dim(seg_ids, place, 0, False)
    prior = lax.dynamic_index_in_dim(seg_ids, jnp.maximum(place - 1, 0), 0, False)
    return (place > 0) & (own == prior)


def gathered_products(gated, cotangent, w_out):
    weights = lax.all_gather(w_out, "seq", axis=0, tiled=True)
    grad_gated = lax.dot_general(cotangent, weights, (((1,), (1,)), ((), ())), preferred_element_type=F32)
    grad_gated = lax.psum_scatter(grad_gated, "tp", scatter_dimension=1, tiled=True).astype(BF16)
    outputs = jnp.dot(
        lax.all_gather(gated, "tp", axis=1, tiled=True), weights, preferred_element_type=F32
    ).astype(BF16)
    return grad_gated, outputs


def ring_place(step, size):
    half = (size + 1) // 2
    return jnp.where(step < half, 2 * step, 2 * (size - 1 - step) + 1)


def ring_step(row, size):
    return jnp.where(row & 1 == 0, row >> 1, size - 1 - (row >> 1))


def split(data):
    high = data.astype(BF16)
    return high, (data - high.astype(F32)).astype(BF16)


def dot(a, b):
    return jnp.dot(a, b, preferred_element_type=F32)


def dot_three(high, low, data):
    data_high, data_low = split(data)
    return dot(high, data_high) + (dot(high, data_low) + dot(low, data_high))


def forward_kernel(linked_ref, fwd_hi, fwd_lo, inv_hi, inv_lo, before, product, taps, queries, *outs):
    data_ref, filt_ref, filtered_ref, gated_ref = outs
    length = product.shape[0]
    past = jnp.where(linked_ref[0] == 1, before[...].astype(F32), 0.0).astype(BF16)
    window = jnp.concatenate([past, product[...]], 0)
    data = dot(fwd_hi[...], window) + dot(fwd_lo[...], window)
    dims = (((1,), (1,)), ((), ()))
    filt = lax.dot_general(fwd_hi[:, length:], taps[...], dims, preferred_element_type=F32)
    filt = filt + lax.dot_general(fwd_lo[:, length:], taps[...], dims, preferred_element_type=F32)
    data_ref[...] = data
    filt_ref[...] = filt
    filtered = dot_three(inv_hi[length:], inv_lo[length:], times(filt, data)) * (1.0 / length)
    filtered = filtered.astype(BF16)
    filtered_ref[...] = filtered
    gated = mul(queries[...], filtered)
    half = gated.shape[1] // 2
    gated_ref[0] = gated[:, :half]
    gated_ref[1] = gated[:, half:]


def tables(length):
    table, high, low = spectrum_table(length)
    return tuple(jnp.asarray(t) for t in (high, low, high.T, low.T))


def forward_filter(linked, before, product, taps, queries):
    length, chans = product.shape
    width = 4 * length
    fixed = pl.BlockSpec((2 * length, 2 * length), lambda j: (0, 0))
    block = pl.BlockSpec((length, width), lambda j: (0, j))
    spectrum = pl.BlockSpec((2 * length, width), lambda j: (0, j))
    wide = jax.ShapeDtypeStruct((2 * length, chans), F32)
    narrow = jax.ShapeDtypeStruct((length, chans), BF16)
    return pl.pallas_call(
        forward_kernel,
        out_shape=(wide, wide, narrow, jax.ShapeDtypeStruct((2, length, chans // 2), BF16)),
        grid=(chans // width,),
        in_specs=[pl.BlockSpec(memory_space=pltpu.SMEM)]
        + [fixed] * 4
        + [block, block, pl.BlockSpec((width, length), lambda j: (j, 0)), block],
        out_specs=(spectrum, spectrum, block, pl.BlockSpec((2, length, width // 2), lambda j: (0, 0, j))),
        compiler_params=pltpu.CompilerParams(vmem_limit_bytes=56 << 20),
        cost_estimate=pl.CostEstimate(
            flops=24 * length * length * chans, bytes_accessed=28 * length * chans, transcendentals=0
        ),
    )(linked.astype(jnp.int32).reshape(1), *tables(length), before, product, taps, queries)


def grad_kernel(scalars, cot_own, cot_away, first, first_other, second, second_other, own_ref, away_ref, total):
    @pl.when(pl.program_id(0) == 0)
    def _():
        total[...] = jnp.zeros_like(total)

    def add(refs):
        rows = jnp.concatenate([ref[...] for ref in refs], 0)
        dims = (((1,), (1,)), ((), ()))
        cot = jnp.concatenate([cot_own[...], cot_away[...]], 0)
        total[...] += lax.dot_general(cot, rows, dims, preferred_element_type=F32)

    @pl.when(scalars[0] == 0)
    def _():
        add((first, first_other, second, second_other))

    @pl.when(scalars[0] != 0)
    def _():
        add((first_other, first, second_other, second))

    @pl.when(pl.program_id(0) == pl.num_programs(0) - 1)
    def _():
        rows = own_ref.shape[0]
        own_ref[...] = total[:rows].astype(BF16)
        away_ref[...] = total[rows:].astype(BF16)


def grad_product(core, cot_own, cot_away, weights):
    rows, feats = cot_own.shape
    tokens = 2 * rows
    depth = weights[0].shape[0]
    tile = min(1024, feats)
    out = jax.ShapeDtypeStruct((rows, 4 * depth), BF16)
    whole = pl.BlockSpec(out.shape, lambda j, core: (0, 0))
    return pl.pallas_call(
        grad_kernel,
        out_shape=(out, out),
        grid_spec=pltpu.PrefetchScalarGridSpec(
            num_scalar_prefetch=1,
            grid=(feats // tile,),
            in_specs=[pl.BlockSpec((rows, tile), lambda j, core: (0, j))] * 2
            + [pl.BlockSpec((depth, tile), lambda j, core: (0, j))] * 4,
            out_specs=(whole, whole),
            scratch_shapes=[pltpu.VMEM((tokens, 4 * depth), F32)],
        ),
        compiler_params=pltpu.CompilerParams(vmem_limit_bytes=56 << 20),
        cost_estimate=pl.CostEstimate(
            flops=8 * tokens * depth * feats, bytes_accessed=(2 * tokens + 8 * depth) * feats, transcendentals=0
        ),
    )(core, cot_own, cot_away, *weights)


def project_kernel(count, first, last, scalars, gated_own, gated_away, *refs):
    weights, refs = refs[: 4 * count], refs[4 * count :]
    depth = weights[0].shape[0]
    width = 4 * depth
    left, total = refs[-2:]

    @pl.when(pl.program_id(0) == 0)
    def _():
        for i in range(count):
            for part, ref in enumerate((gated_own, gated_away)):
                blocks = [
                    ref[:, pl.ds(pl.multiple_of(scalars[1 + 2 * i + way] * width, width), width)] for way in (0, 1)
                ]
                rows = ref.shape[0]
                left[i, part * rows : (part + 1) * rows] = jnp.concatenate(
                    [blocks[way][:, (2 * k + way) * depth : (2 * k + way + 1) * depth] for way in (0, 1) for k in (0, 1)],
                    1,
                )

    total[...] = jnp.zeros_like(total) if first else refs[0][...]

    def add(order):
        for i in range(count):
            right = jnp.concatenate([weights[4 * i + k][...] for k in order], 0)
            total[...] += dot(left[i], right)

    @pl.when(scalars[0] == 0)
    def _():
        add((0, 1, 2, 3))

    @pl.when(scalars[0] != 0)
    def _():
        add((1, 0, 3, 2))

    if last:
        own_ref, away_ref = refs[-4:-2]
        rows = own_ref.shape[0]
        own_ref[...] = total[:rows]
        away_ref[...] = total[rows:].astype(BF16)
    else:
        refs[-3][...] = total[...]


def project(scalars, gated_own, gated_away, groups, before=None, last=False):
    rows, chans = gated_own.shape
    depth, feats = groups[0][0].shape
    tile = min(1024, feats)
    weights = [w for group in groups for w in group]
    whole = pl.BlockSpec((2 * rows, tile), lambda j, s: (0, j))
    block = pl.BlockSpec((rows, tile), lambda j, s: (0, j))
    halves = tuple(jax.ShapeDtypeStruct((rows, feats), kind) for kind in (F32, BF16))
    return pl.pallas_call(
        functools.partial(project_kernel, len(groups), before is None, last),
        out_shape=halves if last else jax.ShapeDtypeStruct((2 * rows, feats), F32),
        grid_spec=pltpu.PrefetchScalarGridSpec(
            num_scalar_prefetch=1,
            grid=(feats // tile,),
            in_specs=[pl.BlockSpec(gated_own.shape, lambda j, s: (0, 0))] * 2
            + [pl.BlockSpec((depth, tile), lambda j, s: (0, j))] * len(weights)
            + [whole] * (before is not None),
            out_specs=(block, block) if last else whole,
            scratch_shapes=[
                pltpu.VMEM((len(groups), 2 * rows, 4 * depth), BF16),
                pltpu.VMEM((2 * rows, tile), F32),
            ],
        ),
        compiler_params=pltpu.CompilerParams(vmem_limit_bytes=56 << 20),
        cost_estimate=pl.CostEstimate(
            flops=4 * rows * depth * len(weights) * feats,
            bytes_accessed=2 * depth * feats * len(weights) + 4 * rows * chans + 8 * rows * feats,
            transcendentals=0,
        ),
    )(scalars, gated_own, gated_away, *weights, *([] if before is None else [before]))


def backward_kernel(count, scalars, fwd_hi, fwd_lo, inv_hi, inv_lo, queries, filtered, data, filt, *refs):
    grads, refs = refs[: 4 * count], refs[-5:]
    grad_queries_ref, near_ref, across_ref, taps_ref, grad = refs
    length = queries.shape[0]
    depth = length // 2

    def side(first, second):
        return [ref[:, k * depth : (k + 1) * depth] for k in (0, 1) for ref in (first[:, : 2 * depth], second[:, 2 * depth :])]

    for i in range(count):
        own, away = [side(grads[4 * i + k], grads[4 * i + k + 2]) for k in (0, 1)]

        @pl.when((pl.program_id(0) == i) & (scalars[0] == 0))
        def _(own=own, away=away):
            grad[...] = jnp.concatenate(own + away, 1)

        @pl.when((pl.program_id(0) == i) & (scalars[0] != 0))
        def _(own=own, away=away):
            grad[...] = jnp.concatenate(away + own, 1)

    grad_gated = grad[...]
    grad_queries_ref[...] = mul(grad_gated, filtered[...])
    grad_filtered = mul(grad_gated, queries[...])
    grads = dot(fwd_hi[:, length:], grad_filtered) + dot(fwd_lo[:, length:], grad_filtered)
    back = dot_three(inv_hi[...], inv_lo[...], times_conj(grads, filt[...])) * (1.0 / length)
    across_ref[0] = jnp.where(scalars[1] == 1, back[:length], 0.0).astype(BF16)
    near_ref[...] = back[length:]
    taps = dot_three(inv_hi[length:], inv_lo[length:], times_conj(grads, data[...])) * (1.0 / length)
    for k in range(4):
        taps_ref[k, 0] = taps[:, k * length : (k + 1) * length]


def backward_filter(scalars, groups, queries, filtered, data, filt, before=None):
    length, chans = queries.shape
    width = 4 * length
    count = len(groups)
    pieces = [p for group in groups for p in group]
    fixed = pl.BlockSpec((2 * length, 2 * length), lambda j, s: (0, 0))
    block = pl.BlockSpec((length, width), lambda j, s: (0, s[2 + j]))
    spectrum = pl.BlockSpec((2 * length, width), lambda j, s: (0, s[2 + j]))
    piece = pl.BlockSpec((length, 2 * length), lambda j, s: (0, 0))
    before = [] if before is None else [before[0], before[1], before[3]]
    inputs = 9 + len(pieces)
    return pl.pallas_call(
        functools.partial(backward_kernel, count),
        out_shape=(
            jax.ShapeDtypeStruct((length, chans), BF16),
            jax.ShapeDtypeStruct((length, chans), F32),
            jax.ShapeDtypeStruct((count, length, width), BF16),
            jax.ShapeDtypeStruct((4, chans // width, length, length), F32),
        ),
        grid_spec=pltpu.PrefetchScalarGridSpec(
            num_scalar_prefetch=1,
            grid=(count,),
            in_specs=[fixed] * 4
            + [block, block, spectrum, spectrum]
            + [piece] * len(pieces)
            + [pl.BlockSpec(memory_space=pl.ANY)] * len(before),
            out_specs=(
                block,
                block,
                pl.BlockSpec((1, length, width), lambda j, s: (j, 0, 0)),
                pl.BlockSpec((4, 1, length, length), lambda j, s: (0, s[2 + j], 0, 0)),
            ),
            scratch_shapes=[pltpu.VMEM((length, width), BF16)],
        ),
        input_output_aliases={inputs + i: out for i, out in zip(range(len(before)), (0, 1, 3))},
        compiler_params=pltpu.CompilerParams(vmem_limit_bytes=56 << 20),
        cost_estimate=pl.CostEstimate(
            flops=28 * length * length * width * count, bytes_accessed=34 * length * width * count, transcendentals=0
        ),
    )(scalars, *tables(length), queries, filtered, data, filt, *pieces, *before)


def join_kernel(count, scalars, near, keys, values, *refs):
    parts, (grad_keys, grad_values) = refs[:count], refs[count:]
    j = pl.program_id(0)
    total = near[...]
    for i, part in enumerate(parts):
        total = total + jnp.where(scalars[j] == i, part[0].astype(F32), 0.0)
    total = total.astype(BF16)
    grad_keys[...] = mul(total, values[...])
    grad_values[...] = mul(total, keys[...])


def join(scalars, near, keys, values, parts):
    length, chans = near.shape
    width = parts[0].shape[2]
    count = chans // width
    block = pl.BlockSpec((length, width), lambda j, s: (0, j))
    out = jax.ShapeDtypeStruct((length, chans), BF16)

    def place(i):
        return lambda j, s: (s[(1 + i) * count + j], 0, 0)

    return pl.pallas_call(
        functools.partial(join_kernel, len(parts)),
        out_shape=(out, out),
        grid_spec=pltpu.PrefetchScalarGridSpec(
            num_scalar_prefetch=1,
            grid=(count,),
            in_specs=[block] * 3 + [pl.BlockSpec((1, length, width), place(i)) for i in range(len(parts))],
            out_specs=(block, block),
        ),
        compiler_params=pltpu.CompilerParams(vmem_limit_bytes=56 << 20),
        cost_estimate=pl.CostEstimate(flops=4 * length * chans, bytes_accessed=14 * length * chans, transcendentals=0),
    )(scalars, near, keys, values, *parts)


def on_ring(queries, keys, values, w_out, taps, seg_ids, cotangent):
    rows, chans = queries.shape
    nseq = lax.axis_size("seq")
    place = lax.axis_index("seq")
    size = nseq // 4
    core, pair, row = place & 1, (place >> 1) & 1, place >> 2
    at = ring_step(row, size)
    swap_core = [(i, i ^ 1) for i in range(nseq)]
    swap_pair = [(i, i ^ 2) for i in range(nseq)]
    walk = list(range(0, size, 2)) + list(range(1, size, 2))[::-1]
    onward = [(4 * walk[i] + k, 4 * walk[(i + 1) % size] + k) for i in range(size) for k in range(4)]
    backward = [(b, a) for a, b in onward]
    later = [(i, i + 1) for i in range(nseq - 1)]
    earlier = [(i + 1, i) for i in range(nseq - 1)]
    send = functools.partial(lax.ppermute, axis_name="seq")
    tie = lax.optimization_barrier
    linked = links(seg_ids, place)

    half = rows // 2
    first, second = w_out[:half], w_out[half:]
    cot_away = send(cotangent, perm=swap_pair)
    swapped = send(w_out, perm=swap_core)
    product, cot_away = tie((mul(keys, values), cot_away))
    before = send(product, perm=later)

    ready = [max(s, size - s) if s else 0 for s in range(size)]
    early = max(size - 3, 1)
    stages = {early: [s for s in range(size) if ready[s] <= early]}
    for t in range(early + 1, size):
        stages[t] = [s for s in range(size) if ready[s] == t]
    stages = {t: sets for t, sets in stages.items() if sets}
    block = [ring_place(lax.rem(at - s + size, size), size).astype(jnp.int32) for s in range(size)]
    core = core.astype(jnp.int32)
    core_only = core.reshape(1)
    cut = max(size - 3, 1)
    firsts, seconds, own, away, parts = [], [], [], [], []
    sums = back = None
    kept = {}

    def projected(steps, sums, last):
        groups = [firsts[s] + seconds[s] for s in steps]
        places = [b for s in steps for b in (block[s], block[(size - s) % size])]
        return project(jnp.stack([core] + places), gated_own, gated_away, groups, sums, last)

    for step in range(size):
        if step:
            if step >= 3:
                for s in (0, 1) if step == 3 else (step - 2,):
                    first, second, own[s], away[s] = tie((first, second, own[s], away[s]))
            if step == cut + 1 and sums is not None:
                first, second, sums = tie((first, second, sums))
            if step - 2 in stages:
                first, second, kept[step - 2] = tie((first, second, kept[step - 2]))
            first, second = send(first, perm=onward), send(second, perm=backward)
            firsts.append((first, send(first, perm=swap_core)))
            seconds.append((second, send(second, perm=swap_core)))
            if step == 1:
                _, _, cot_away = tie((first, second, cot_away))
                mine, theirs = grad_product(core_only, cotangent, cot_away, firsts[0] + seconds[0])
                own.append(mine)
                away.append(send(theirs, perm=swap_pair))
            if step == max(min(2, early), 1):
                _, _, before = tie((first, second, before))
                data, filt, filtered, gated = forward_filter(linked, before, product, taps, queries)
                gated_own = lax.dynamic_index_in_dim(gated, pair, 0, False)
                gated_away = send(lax.dynamic_index_in_dim(gated, 1 - pair, 0, False), perm=swap_pair)
        else:
            firsts.append((first, swapped[:half]))
            seconds.append((second, swapped[half:]))
            continue
        if step == size - 1 and back is not None:
            firsts[step], seconds[step], back, parts[0] = tie((firsts[step], seconds[step], back, parts[0]))
        mine, theirs = grad_product(core_only, cotangent, cot_away, firsts[step] + seconds[step])
        own.append(mine)
        away.append(send(theirs, perm=swap_pair))
        if step == max(cut - 1, 1) and step < size - 1:
            sums = projected(range(cut), None, False)
        if step == size - 1:
            sums = projected(range(0 if sums is None else cut, size), sums, True)
            away[step], sums = tie((away[step], sums))
        if step in stages:
            sets = stages[step]
            mirror = [(size - s) % size for s in sets]
            groups = [(own[s], away[s], own[m], away[m]) for s, m in zip(sets, mirror)]
            scalars = jnp.stack([pair.astype(jnp.int32), linked.astype(jnp.int32)] + [block[s] for s in sets])
            back = backward_filter(scalars, groups, queries, filtered, data, filt, back)
            kept[step] = back[2]
            parts.append(send(back[2], perm=earlier))
    grad_queries, near, _, taps_part = back
    taps_grad = sum_over_ring(taps_part, nseq, place).T
    out_own, out_away = sums
    outputs = (out_own + send(out_away, perm=swap_pair).astype(F32)).astype(BF16)

    source = ring_step(jnp.minimum(place + 1, nseq - 1) >> 2, size)
    stage_of, place_in = np.zeros(size, np.int32), np.zeros((len(stages), size), np.int32)
    for i, sets in enumerate(stages.values()):
        for k, s in enumerate(sets):
            stage_of[s], place_in[i, s] = i, k
    table = np.concatenate([stage_of[None], place_in], 0)
    steps = jnp.stack([lax.rem(source - ring_step(jnp.int32(r), size) + size, size) for r in range(size)])
    scalars = jnp.take(jnp.asarray(table), steps, axis=1).reshape(-1)
    grad_keys, grad_values = join(scalars, near, keys, values, parts)
    return (outputs, grad_queries, grad_keys, grad_values, taps_grad)


def on_device(queries, keys, values, w_out, taps, seg_ids, cotangent):
    rows, chans = queries.shape
    length = taps.shape[1]
    assert rows == length
    nseq = lax.axis_size("seq")
    place = lax.axis_index("seq")
    table, high, low = spectrum_table(length)
    table_now, high_now, low_now = table[:, length:], high[:, length:], low[:, length:]
    scale = 1.0 / length
    later = [(i, i + 1) for i in range(nseq - 1)]
    earlier = [(i + 1, i) for i in range(nseq - 1)]
    linked = links(seg_ids, place)

    product = mul(keys, values)
    before = lax.ppermute(product, "seq", later)
    before = jnp.where(linked, before, jnp.zeros_like(before))
    data = forward_dft(high, low, jnp.concatenate([before, product], 0), ((1,), (0,)))
    filt = forward_dft(high_now, low_now, taps, ((1,), (1,)))
    filtered = inverse_dft(table_now, times(filt, data), scale).astype(BF16)
    gated = mul(queries, filtered)

    grad_gated, outputs = gathered_products(gated, cotangent, w_out)
    grad_queries = mul(grad_gated, filtered)
    grad_filtered = mul(grad_gated, queries)
    grads = forward_dft(high_now, low_now, grad_filtered, ((1,), (0,)))
    back = inverse_dft(table, times_conj(grads, filt), scale)
    across = jnp.where(linked, back[:length], 0.0).astype(BF16)
    ahead = lax.ppermute(across, "seq", earlier)
    taps_part = inverse_dft(table_now, times_conj(grads, data), scale)
    if nseq & (nseq - 1):
        taps_grad = lax.psum_scatter(taps_part.T, "seq", scatter_dimension=0, tiled=True)
    else:
        blocks = taps_part.reshape(length, nseq, -1).transpose(1, 0, 2)
        taps_grad = scatter_sum(blocks, nseq, place).T
    grad_product = (back[length:] + ahead.astype(F32)).astype(BF16)
    grad_keys = mul(grad_product, values)
    grad_values = mul(grad_product, keys)
    return (outputs, grad_queries, grad_keys, grad_values, taps_grad)


def solution(mesh):
    block = P("seq", "tp")
    count = mesh.shape["seq"]
    ring = mesh.shape["tp"] == 1 and count & (count - 1) == 0 and count >= 8

    def run(queries, keys, values, w_out, taps, seg_ids, cotangent):
        rows, chans = queries.shape
        place = on_ring if ring and rows * count == chans else on_device
        return place(queries, keys, values, w_out, taps, seg_ids, cotangent)

    return jax.shard_map(
        run,
        mesh=mesh,
        in_specs=(block, block, block, block, P("tp", None), P(), block),
        out_specs=(block, block, block, block, P(("tp", "seq"), None)),
        check_vma=False,
    )
```

```python
import functools

import jax
import jax.numpy as jnp
import numpy as np
from jax import lax
from jax.experimental import pallas as pl
from jax.experimental.pallas import tpu as pltpu
from jax.sharding import PartitionSpec as P

F32 = jnp.float32
BF16 = jnp.bfloat16
GRANT = 16 << 20


def spectrum_table(length):
    angles = np.pi * (2 * np.arange(length)[:, None] + 1) * np.arange(-length, length)[None, :] / (2 * length)
    table = np.concatenate([np.cos(angles), -np.sin(angles)], 0).astype(np.float32)
    high = table.astype(BF16)
    low = (table - high.astype(np.float32)).astype(BF16)
    return table, high, low


def forward_dft(high, low, data, dims):
    first = lax.dot_general(high, data, (dims, ((), ())), preferred_element_type=F32)
    second = lax.dot_general(low, data, (dims, ((), ())), preferred_element_type=F32)
    return first + second


def times(a, b):
    half = a.shape[0] // 2
    ar, ai, br, bi = a[:half], a[half:], b[:half], b[half:]
    return jnp.concatenate([ar * br - ai * bi, ar * bi + ai * br], 0)


def times_conj(a, b):
    half = a.shape[0] // 2
    ar, ai, br, bi = a[:half], a[half:], b[:half], b[half:]
    return jnp.concatenate([ar * br + ai * bi, ai * br - ar * bi], 0)


def inverse_dft(table, spectrum, scale):
    done = lax.dot_general(
        table, spectrum, (((0,), (0,)), ((), ())), precision=lax.Precision.HIGH, preferred_element_type=F32
    )
    return done * scale


def mul(a, b):
    return (a.astype(F32) * b.astype(F32)).astype(BF16)


def scatter_sum(part, nseq, place):
    bits = nseq.bit_length() - 1
    lags = part.shape[-2]
    chans = part.shape[-1]
    for step in range(bits):
        mine = (place >> step) & 1
        part = part.reshape(-1, 2, lags, chans)
        away = lax.dynamic_index_in_dim(part, 1 - mine, 1, False)
        kept = lax.dynamic_index_in_dim(part, mine, 1, False)
        if step:
            away = away.astype(BF16)
        away = lax.ppermute(away, "seq", [(i, i ^ (1 << step)) for i in range(nseq)])
        part = kept + away.astype(F32)
    return part[0]


def sum_over_ring(part, nseq, place):
    core, pair, row = place & 1, (place >> 1) & 1, place >> 2
    four, size, lags, chans = part.shape

    def halve(part, bit, mine, kind):
        away = lax.dynamic_index_in_dim(part, 1 - mine, 1, False).astype(kind)
        away = lax.ppermute(away, "seq", [(i, i ^ bit) for i in range(nseq)])
        return lax.dynamic_index_in_dim(part, mine, 1, False) + away.astype(F32)

    part = halve(part.reshape(2, 2, size, lags, chans), 1, core, F32)
    part = halve(part.reshape(1, 2, size, lags, chans), 2, pair, BF16).reshape(size, lags, chans)
    left = size
    while left > 1:
        bit = size // left
        part = halve(part.reshape(left // 2, 2, lags, chans), 4 * bit, (row // bit) & 1, BF16)
        left //= 2
    return part.reshape(lags, chans)


def links(seg_ids, place):
    own = lax.dynamic_index_in_dim(seg_ids, place, 0, False)
    prior = lax.dynamic_index_in_dim(seg_ids, jnp.maximum(place - 1, 0), 0, False)
    return (place > 0) & (own == prior)


def gathered_products(gated, cotangent, w_out):
    weights = lax.all_gather(w_out, "seq", axis=0, tiled=True)
    grad_gated = lax.dot_general(cotangent, weights, (((1,), (1,)), ((), ())), preferred_element_type=F32)
    grad_gated = lax.psum_scatter(grad_gated, "tp", scatter_dimension=1, tiled=True).astype(BF16)
    outputs = jnp.dot(
        lax.all_gather(gated, "tp", axis=1, tiled=True), weights, preferred_element_type=F32
    ).astype(BF16)
    return grad_gated, outputs


def ring_place(step, size):
    half = (size + 1) // 2
    return jnp.where(step < half, 2 * step, 2 * (size - 1 - step) + 1)


def ring_step(row, size):
    return jnp.where(row & 1 == 0, row >> 1, size - 1 - (row >> 1))


def pinned(space, *arrays):
    return [pltpu.with_memory_space_constraint(a, space) for a in arrays]


def split(data):
    high = data.astype(BF16)
    return high, (data - high.astype(F32)).astype(BF16)


def dot(a, b):
    return jnp.dot(a, b, preferred_element_type=F32)


def dot_three(high, low, data):
    data_high, data_low = split(data)
    return dot(high, data_high) + (dot(high, data_low) + dot(low, data_high))


def forward_kernel(linked_ref, fwd_hi, fwd_lo, inv_hi, inv_lo, before, product, taps, queries, *outs):
    data_ref, filt_ref, filtered_ref, gated_ref = outs
    length = product.shape[0]
    past = jnp.where(linked_ref[0] == 1, before[...].astype(F32), 0.0).astype(BF16)
    window = jnp.concatenate([past, product[...]], 0)
    data = dot(fwd_hi[...], window) + dot(fwd_lo[...], window)
    dims = (((1,), (1,)), ((), ()))
    filt = lax.dot_general(fwd_hi[:, length:], taps[...], dims, preferred_element_type=F32)
    filt = filt + lax.dot_general(fwd_lo[:, length:], taps[...], dims, preferred_element_type=F32)
    data_ref[...] = data
    filt_ref[...] = filt
    filtered = dot_three(inv_hi[length:], inv_lo[length:], times(filt, data)) * (1.0 / length)
    filtered = filtered.astype(BF16)
    filtered_ref[...] = filtered
    gated = mul(queries[...], filtered)
    half = gated.shape[1] // 2
    gated_ref[0] = gated[:, :half]
    gated_ref[1] = gated[:, half:]


def tables(length):
    table, high, low = spectrum_table(length)
    return tuple(jnp.asarray(t) for t in (high, low, high.T, low.T))


def forward_filter(linked, before, product, taps, queries):
    length, chans = product.shape
    width = 4 * length
    fixed = pl.BlockSpec((2 * length, 2 * length), lambda j: (0, 0))
    block = pl.BlockSpec((length, width), lambda j: (0, j))
    spectrum = pl.BlockSpec((2 * length, width), lambda j: (0, j))
    wide = pltpu.HBM((2 * length, chans), F32)
    narrow = pltpu.HBM((length, chans), BF16)
    return pl.pallas_call(
        forward_kernel,
        out_shape=(wide, wide, narrow, pltpu.HBM((2, length, chans // 2), BF16)),
        grid=(chans // width,),
        in_specs=[pl.BlockSpec(memory_space=pltpu.SMEM)]
        + [fixed] * 4
        + [block, block, pl.BlockSpec((width, length), lambda j: (j, 0)), block],
        out_specs=(spectrum, spectrum, block, pl.BlockSpec((2, length, width // 2), lambda j: (0, 0, j))),
        compiler_params=pltpu.CompilerParams(vmem_limit_bytes=GRANT),
        cost_estimate=pl.CostEstimate(
            flops=24 * length * length * chans, bytes_accessed=28 * length * chans, transcendentals=0
        ),
    )(linked.astype(jnp.int32).reshape(1), *tables(length), *pinned(pltpu.HBM, before, product, taps, queries))


def grad_kernel(scalars, cot_own, cot_away, first, first_other, second, second_other, own_ref, away_ref):
    rows, feats = cot_own.shape
    tile = min(512, feats)
    depth = first.shape[0]
    dims = (((1,), (1,)), ((), ()))

    def add(refs):
        def step(j, total):
            at = pl.ds(pl.multiple_of(j * tile, tile), tile)
            left = jnp.concatenate([cot_own[:, at], cot_away[:, at]], 0)
            right = jnp.concatenate([ref[:, at] for ref in refs], 0)
            return total + lax.dot_general(left, right, dims, preferred_element_type=F32)

        total = lax.fori_loop(0, feats // tile, step, jnp.zeros((2 * rows, 4 * depth), F32))
        own_ref[...] = total[:rows].astype(BF16)
        away_ref[...] = total[rows:].astype(BF16)

    @pl.when(scalars[0] == 0)
    def _():
        add((first, first_other, second, second_other))

    @pl.when(scalars[0] != 0)
    def _():
        add((first_other, first, second_other, second))


def grad_product(core, cot_own, cot_away, weights):
    rows, feats = cot_own.shape
    depth = weights[0].shape[0]
    out = jax.ShapeDtypeStruct((rows, 4 * depth), BF16)
    vmem = pl.BlockSpec(memory_space=pltpu.VMEM)
    return pl.pallas_call(
        grad_kernel,
        out_shape=(out, out),
        in_specs=[pl.BlockSpec(memory_space=pltpu.SMEM)] + [vmem] * 6,
        out_specs=(vmem, vmem),
        compiler_params=pltpu.CompilerParams(vmem_limit_bytes=GRANT),
        cost_estimate=pl.CostEstimate(
            flops=16 * rows * depth * feats, bytes_accessed=(4 * rows + 8 * depth) * feats, transcendentals=0
        ),
    )(core, cot_own, cot_away, *weights)


def project_kernel(count, first, last, scalars, gated_own, gated_away, *refs):
    weights, refs = refs[: 4 * count], refs[4 * count :]
    depth = weights[0].shape[0]
    width = 4 * depth
    left, total = refs[-2:]

    @pl.when(pl.program_id(0) == 0)
    def _():
        for i in range(count):
            for part, ref in enumerate((gated_own, gated_away)):
                blocks = [
                    ref[:, pl.ds(pl.multiple_of(scalars[1 + 2 * i + way] * width, width), width)] for way in (0, 1)
                ]
                rows = ref.shape[0]
                left[i, part * rows : (part + 1) * rows] = jnp.concatenate(
                    [blocks[way][:, (2 * k + way) * depth : (2 * k + way + 1) * depth] for way in (0, 1) for k in (0, 1)],
                    1,
                )

    total[...] = jnp.zeros_like(total) if first else refs[0][...]

    def add(order):
        for i in range(count):
            right = jnp.concatenate([weights[4 * i + k][...] for k in order], 0)
            total[...] += dot(left[i], right)

    @pl.when(scalars[0] == 0)
    def _():
        add((0, 1, 2, 3))

    @pl.when(scalars[0] != 0)
    def _():
        add((1, 0, 3, 2))

    if last:
        own_ref, away_ref = refs[-4:-2]
        rows = own_ref.shape[0]
        own_ref[...] = total[:rows]
        away_ref[...] = total[rows:].astype(BF16)
    else:
        refs[-3][...] = total[...]


def project(scalars, gated_own, gated_away, groups, before=None, last=False):
    rows, chans = gated_own.shape
    depth, feats = groups[0][0].shape
    tile = min(1024, feats)
    weights = [w for group in groups for w in group]
    whole = pl.BlockSpec((2 * rows, tile), lambda j, s: (0, j))
    block = pl.BlockSpec((rows, tile), lambda j, s: (0, j))
    halves = tuple(pltpu.HBM((rows, feats), kind) for kind in (F32, BF16))
    return pl.pallas_call(
        functools.partial(project_kernel, len(groups), before is None, last),
        out_shape=halves if last else pltpu.HBM((2 * rows, feats), F32),
        grid_spec=pltpu.PrefetchScalarGridSpec(
            num_scalar_prefetch=1,
            grid=(feats // tile,),
            in_specs=[pl.BlockSpec(gated_own.shape, lambda j, s: (0, 0))] * 2
            + [pl.BlockSpec((depth, tile), lambda j, s: (0, j))] * len(weights)
            + [whole] * (before is not None),
            out_specs=(block, block) if last else whole,
            scratch_shapes=[
                pltpu.VMEM((len(groups), 2 * rows, 4 * depth), BF16),
                pltpu.VMEM((2 * rows, tile), F32),
            ],
        ),
        compiler_params=pltpu.CompilerParams(vmem_limit_bytes=GRANT),
        cost_estimate=pl.CostEstimate(
            flops=4 * rows * depth * len(weights) * feats,
            bytes_accessed=2 * depth * feats * len(weights) + 4 * rows * chans + 8 * rows * feats,
            transcendentals=0,
        ),
    )(
        scalars,
        *pinned(pltpu.HBM, gated_own, gated_away),
        *pinned(pltpu.VMEM, *weights),
        *([] if before is None else pinned(pltpu.HBM, before)),
    )


def backward_kernel(count, scalars, fwd_hi, fwd_lo, inv_hi, inv_lo, queries, filtered, data, filt, *refs):
    grads, refs = refs[: 4 * count], refs[-5:]
    grad_queries_ref, near_ref, across_ref, taps_ref, grad = refs
    length = queries.shape[0]
    depth = length // 2

    def side(first, second):
        return [ref[:, k * depth : (k + 1) * depth] for k in (0, 1) for ref in (first[:, : 2 * depth], second[:, 2 * depth :])]

    for i in range(count):
        own, away = [side(grads[4 * i + k], grads[4 * i + k + 2]) for k in (0, 1)]

        @pl.when((pl.program_id(0) == i) & (scalars[0] == 0))
        def _(own=own, away=away):
            grad[...] = jnp.concatenate(own + away, 1)

        @pl.when((pl.program_id(0) == i) & (scalars[0] != 0))
        def _(own=own, away=away):
            grad[...] = jnp.concatenate(away + own, 1)

    grad_gated = grad[...]
    grad_queries_ref[...] = mul(grad_gated, filtered[...])
    grad_filtered = mul(grad_gated, queries[...])
    grads = dot(fwd_hi[:, length:], grad_filtered) + dot(fwd_lo[:, length:], grad_filtered)
    back = dot_three(inv_hi[...], inv_lo[...], times_conj(grads, filt[...])) * (1.0 / length)
    across_ref[0] = jnp.where(scalars[1] == 1, back[:length], 0.0).astype(BF16)
    near_ref[...] = back[length:]
    taps = dot_three(inv_hi[length:], inv_lo[length:], times_conj(grads, data[...])) * (1.0 / length)
    for k in range(4):
        taps_ref[k, 0] = taps[:, k * length : (k + 1) * length]


def backward_filter(scalars, groups, queries, filtered, data, filt, before=None):
    length, chans = queries.shape
    width = 4 * length
    count = len(groups)
    pieces = [p for group in groups for p in group]
    fixed = pl.BlockSpec((2 * length, 2 * length), lambda j, s: (0, 0))
    block = pl.BlockSpec((length, width), lambda j, s: (0, s[2 + j]))
    spectrum = pl.BlockSpec((2 * length, width), lambda j, s: (0, s[2 + j]))
    piece = pl.BlockSpec((length, 2 * length), lambda j, s: (0, 0))
    before = [] if before is None else [before[0], before[1], before[3]]
    inputs = 9 + len(pieces)
    return pl.pallas_call(
        functools.partial(backward_kernel, count),
        out_shape=(
            pltpu.HBM((length, chans), BF16),
            pltpu.HBM((length, chans), F32),
            pltpu.HBM((count, length, width), BF16),
            pltpu.HBM((4, chans // width, length, length), F32),
        ),
        grid_spec=pltpu.PrefetchScalarGridSpec(
            num_scalar_prefetch=1,
            grid=(count,),
            in_specs=[fixed] * 4
            + [block, block, spectrum, spectrum]
            + [piece] * len(pieces)
            + [pl.BlockSpec(memory_space=pl.ANY)] * len(before),
            out_specs=(
                block,
                block,
                pl.BlockSpec((1, length, width), lambda j, s: (j, 0, 0)),
                pl.BlockSpec((4, 1, length, length), lambda j, s: (0, s[2 + j], 0, 0)),
            ),
            scratch_shapes=[pltpu.VMEM((length, width), BF16)],
        ),
        input_output_aliases={inputs + i: out for i, out in zip(range(len(before)), (0, 1, 3))},
        compiler_params=pltpu.CompilerParams(vmem_limit_bytes=GRANT),
        cost_estimate=pl.CostEstimate(
            flops=28 * length * length * width * count, bytes_accessed=34 * length * width * count, transcendentals=0
        ),
    )(
        scalars,
        *tables(length),
        *pinned(pltpu.HBM, queries, filtered, data, filt),
        *pinned(pltpu.VMEM, *pieces),
        *pinned(pltpu.HBM, *before),
    )


def join_kernel(count, scalars, near, keys, values, *refs):
    parts, (grad_keys, grad_values) = refs[:count], refs[count:]
    j = pl.program_id(0)
    total = near[...]
    for i, part in enumerate(parts):
        total = total + jnp.where(scalars[j] == i, part[0].astype(F32), 0.0)
    total = total.astype(BF16)
    grad_keys[...] = mul(total, values[...])
    grad_values[...] = mul(total, keys[...])


def join(scalars, near, keys, values, parts):
    length, chans = near.shape
    width = parts[0].shape[2]
    count = chans // width
    block = pl.BlockSpec((length, width), lambda j, s: (0, j))
    out = jax.ShapeDtypeStruct((length, chans), BF16)

    def place(i):
        return lambda j, s: (s[(1 + i) * count + j], 0, 0)

    return pl.pallas_call(
        functools.partial(join_kernel, len(parts)),
        out_shape=(out, out),
        grid_spec=pltpu.PrefetchScalarGridSpec(
            num_scalar_prefetch=1,
            grid=(count,),
            in_specs=[block] * 3 + [pl.BlockSpec((1, length, width), place(i)) for i in range(len(parts))],
            out_specs=(block, block),
        ),
        compiler_params=pltpu.CompilerParams(vmem_limit_bytes=GRANT),
        cost_estimate=pl.CostEstimate(flops=4 * length * chans, bytes_accessed=14 * length * chans, transcendentals=0),
    )(scalars, *pinned(pltpu.HBM, near, keys, values), *pinned(pltpu.VMEM, *parts))


def on_ring(queries, keys, values, w_out, taps, seg_ids, cotangent):
    rows, chans = queries.shape
    nseq = lax.axis_size("seq")
    place = lax.axis_index("seq")
    size = nseq // 4
    core, pair, row = place & 1, (place >> 1) & 1, place >> 2
    at = ring_step(row, size)
    swap_core = [(i, i ^ 1) for i in range(nseq)]
    swap_pair = [(i, i ^ 2) for i in range(nseq)]
    walk = list(range(0, size, 2)) + list(range(1, size, 2))[::-1]
    onward = [(4 * walk[i] + k, 4 * walk[(i + 1) % size] + k) for i in range(size) for k in range(4)]
    backward = [(b, a) for a, b in onward]
    later = [(i, i + 1) for i in range(nseq - 1)]
    earlier = [(i + 1, i) for i in range(nseq - 1)]
    send = functools.partial(lax.ppermute, axis_name="seq")
    tie = lax.optimization_barrier
    linked = links(seg_ids, place)

    half = rows // 2
    first, second = w_out[:half], w_out[half:]
    cot_away = send(cotangent, perm=swap_pair)
    swapped = send(w_out, perm=swap_core)
    product, cot_away = tie((mul(keys, values), cot_away))
    before = send(product, perm=later)

    ready = [max(s, size - s) if s else 0 for s in range(size)]
    early = max(size - 3, 1)
    stages = {early: [s for s in range(size) if ready[s] <= early]}
    for t in range(early + 1, size):
        stages[t] = [s for s in range(size) if ready[s] == t]
    stages = {t: sets for t, sets in stages.items() if sets}
    block = [ring_place(lax.rem(at - s + size, size), size).astype(jnp.int32) for s in range(size)]
    core = core.astype(jnp.int32)
    core_only = core.reshape(1)
    cut = max(size - 3, 1)
    firsts, seconds, own, away, parts = [], [], [], [], []
    sums = back = None
    kept = {}

    def projected(steps, sums, last):
        groups = [firsts[s] + seconds[s] for s in steps]
        places = [b for s in steps for b in (block[s], block[(size - s) % size])]
        return project(jnp.stack([core] + places), gated_own, gated_away, groups, sums, last)

    for step in range(size):
        if step:
            if step >= 3:
                for s in (0, 1) if step == 3 else (step - 2,):
                    first, second, own[s], away[s] = tie((first, second, own[s], away[s]))
            if step == cut + 1 and sums is not None:
                first, second, sums = tie((first, second, sums))
            if step - 2 in stages:
                first, second, kept[step - 2] = tie((first, second, kept[step - 2]))
            first, second = send(first, perm=onward), send(second, perm=backward)
            firsts.append((first, send(first, perm=swap_core)))
            seconds.append((second, send(second, perm=swap_core)))
            if step == 1:
                _, _, cot_away = tie((first, second, cot_away))
                mine, theirs = grad_product(core_only, cotangent, cot_away, firsts[0] + seconds[0])
                own.append(mine)
                away.append(send(theirs, perm=swap_pair))
            if step == max(min(2, early), 1):
                _, _, before = tie((first, second, before))
                data, filt, filtered, gated = forward_filter(linked, before, product, taps, queries)
                gated_own = lax.dynamic_index_in_dim(gated, pair, 0, False)
                gated_away = send(lax.dynamic_index_in_dim(gated, 1 - pair, 0, False), perm=swap_pair)
        else:
            firsts.append((first, swapped[:half]))
            seconds.append((second, swapped[half:]))
            continue
        if step == size - 1 and back is not None:
            firsts[step], seconds[step], back, parts[0] = tie((firsts[step], seconds[step], back, parts[0]))
        mine, theirs = grad_product(core_only, cotangent, cot_away, firsts[step] + seconds[step])
        own.append(mine)
        away.append(send(theirs, perm=swap_pair))
        if step == max(cut - 1, 1) and step < size - 1:
            sums = projected(range(cut), None, False)
        if step == size - 1:
            sums = projected(range(0 if sums is None else cut, size), sums, True)
            away[step], sums = tie((away[step], sums))
        if step in stages:
            sets = stages[step]
            mirror = [(size - s) % size for s in sets]
            groups = [(own[s], away[s], own[m], away[m]) for s, m in zip(sets, mirror)]
            scalars = jnp.stack([pair.astype(jnp.int32), linked.astype(jnp.int32)] + [block[s] for s in sets])
            back = backward_filter(scalars, groups, queries, filtered, data, filt, back)
            kept[step] = back[2]
            parts.append(send(back[2], perm=earlier))
    grad_queries, near, _, taps_part = back
    taps_grad = sum_over_ring(taps_part, nseq, place).T
    out_own, out_away = sums
    outputs = (out_own + send(out_away, perm=swap_pair).astype(F32)).astype(BF16)

    source = ring_step(jnp.minimum(place + 1, nseq - 1) >> 2, size)
    stage_of, place_in = np.zeros(size, np.int32), np.zeros((len(stages), size), np.int32)
    for i, sets in enumerate(stages.values()):
        for k, s in enumerate(sets):
            stage_of[s], place_in[i, s] = i, k
    table = np.concatenate([stage_of[None], place_in], 0)
    steps = jnp.stack([lax.rem(source - ring_step(jnp.int32(r), size) + size, size) for r in range(size)])
    scalars = jnp.take(jnp.asarray(table), steps, axis=1).reshape(-1)
    grad_keys, grad_values = join(scalars, near, keys, values, parts)
    return (outputs, grad_queries, grad_keys, grad_values, taps_grad)


def on_device(queries, keys, values, w_out, taps, seg_ids, cotangent):
    rows, chans = queries.shape
    length = taps.shape[1]
    assert rows == length
    nseq = lax.axis_size("seq")
    place = lax.axis_index("seq")
    table, high, low = spectrum_table(length)
    table_now, high_now, low_now = table[:, length:], high[:, length:], low[:, length:]
    scale = 1.0 / length
    later = [(i, i + 1) for i in range(nseq - 1)]
    earlier = [(i + 1, i) for i in range(nseq - 1)]
    linked = links(seg_ids, place)

    product = mul(keys, values)
    before = lax.ppermute(product, "seq", later)
    before = jnp.where(linked, before, jnp.zeros_like(before))
    data = forward_dft(high, low, jnp.concatenate([before, product], 0), ((1,), (0,)))
    filt = forward_dft(high_now, low_now, taps, ((1,), (1,)))
    filtered = inverse_dft(table_now, times(filt, data), scale).astype(BF16)
    gated = mul(queries, filtered)

    grad_gated, outputs = gathered_products(gated, cotangent, w_out)
    grad_queries = mul(grad_gated, filtered)
    grad_filtered = mul(grad_gated, queries)
    grads = forward_dft(high_now, low_now, grad_filtered, ((1,), (0,)))
    back = inverse_dft(table, times_conj(grads, filt), scale)
    across = jnp.where(linked, back[:length], 0.0).astype(BF16)
    ahead = lax.ppermute(across, "seq", earlier)
    taps_part = inverse_dft(table_now, times_conj(grads, data), scale)
    if nseq & (nseq - 1):
        taps_grad = lax.psum_scatter(taps_part.T, "seq", scatter_dimension=0, tiled=True)
    else:
        blocks = taps_part.reshape(length, nseq, -1).transpose(1, 0, 2)
        taps_grad = scatter_sum(blocks, nseq, place).T
    grad_product = (back[length:] + ahead.astype(F32)).astype(BF16)
    grad_keys = mul(grad_product, values)
    grad_values = mul(grad_product, keys)
    return (outputs, grad_queries, grad_keys, grad_values, taps_grad)


def solution(mesh):
    block = P("seq", "tp")
    count = mesh.shape["seq"]
    ring = mesh.shape["tp"] == 1 and count & (count - 1) == 0 and count >= 8

    def run(queries, keys, values, w_out, taps, seg_ids, cotangent):
        rows, chans = queries.shape
        place = on_ring if ring and rows * count == chans else on_device
        return place(queries, keys, values, w_out, taps, seg_ids, cotangent)

    return jax.shard_map(
        run,
        mesh=mesh,
        in_specs=(block, block, block, block, P("tp", None), P(), block),
        out_specs=(block, block, block, block, P(("tp", "seq"), None)),
        check_vma=False,
    )
```

```python
import functools

import jax
import jax.numpy as jnp
import numpy as np
from jax import lax
from jax.experimental import pallas as pl
from jax.experimental.pallas import tpu as pltpu
from jax.sharding import PartitionSpec as P

F32 = jnp.float32
BF16 = jnp.bfloat16
GRANT = 16 << 20


def spectrum_table(length):
    angles = np.pi * (2 * np.arange(length)[:, None] + 1) * np.arange(-length, length)[None, :] / (2 * length)
    table = np.concatenate([np.cos(angles), -np.sin(angles)], 0).astype(np.float32)
    high = table.astype(BF16)
    low = (table - high.astype(np.float32)).astype(BF16)
    return table, high, low


def forward_dft(high, low, data, dims):
    first = lax.dot_general(high, data, (dims, ((), ())), preferred_element_type=F32)
    second = lax.dot_general(low, data, (dims, ((), ())), preferred_element_type=F32)
    return first + second


def times(a, b):
    half = a.shape[0] // 2
    ar, ai, br, bi = a[:half], a[half:], b[:half], b[half:]
    return jnp.concatenate([ar * br - ai * bi, ar * bi + ai * br], 0)


def times_conj(a, b):
    half = a.shape[0] // 2
    ar, ai, br, bi = a[:half], a[half:], b[:half], b[half:]
    return jnp.concatenate([ar * br + ai * bi, ai * br - ar * bi], 0)


def inverse_dft(table, spectrum, scale):
    done = lax.dot_general(
        table, spectrum, (((0,), (0,)), ((), ())), precision=lax.Precision.HIGH, preferred_element_type=F32
    )
    return done * scale


def mul(a, b):
    return (a.astype(F32) * b.astype(F32)).astype(BF16)


def pick(data, width, side):
    blocks = [data[:, i : i + width] for i in range(0, data.shape[1], width)]
    return jnp.concatenate([jnp.where(side == 0, a, b) for a, b in zip(blocks[::2], blocks[1::2])], 1)


def scatter_sum(part, nseq, place, order):
    share = part.shape[1] // nseq
    bits = nseq.bit_length() - 1
    if nseq != 1 << bits:
        return lax.psum_scatter(part, "seq", scatter_dimension=1, tiled=True)
    left = list(range(bits))
    for step in [b for b in order if b < bits] + [b for b in range(bits) if b not in order]:
        width = share << sum(b < step for b in left)
        left.remove(step)
        mine = (place >> step) & 1
        away = pick(part, width, 1 - mine)
        if step:
            away = away.astype(BF16)
        away = lax.ppermute(away, "seq", [(i, i ^ (1 << step)) for i in range(nseq)])
        part = pick(part, width, mine) + away.astype(F32)
    return part


def sum_over_ring(part, nseq, place):
    core, pair, row = place & 1, (place >> 1) & 1, place >> 2
    lags, chans = part.shape
    size, chans = nseq // 4, chans // nseq

    def halve(part, bit, mine, kind):
        away = lax.dynamic_index_in_dim(part, 1 - mine, 1, False).astype(kind)
        away = lax.ppermute(away, "seq", [(i, i ^ bit) for i in range(nseq)])
        return lax.dynamic_index_in_dim(part, mine, 1, False) + away.astype(F32)

    kept, away = deal(core.astype(jnp.int32), part, chans, 2)
    part = kept + lax.ppermute(away, "seq", [(i, i ^ 1) for i in range(nseq)])
    part = halve(part.reshape(1, 2, size, lags, chans), 2, pair, BF16).reshape(size, lags, chans)
    left = size
    while left > 1:
        bit = size // left
        part = halve(part.reshape(left // 2, 2, lags, chans), 4 * bit, (row // bit) & 1, BF16)
        left //= 2
    return part.reshape(lags, chans)


def links(seg_ids, place):
    own = lax.dynamic_index_in_dim(seg_ids, place, 0, False)
    prior = lax.dynamic_index_in_dim(seg_ids, jnp.maximum(place - 1, 0), 0, False)
    return (place > 0) & (own == prior)


def gathered_products(gated, cotangent, w_out):
    weights = lax.all_gather(w_out, "seq", axis=0, tiled=True)
    grad_gated = lax.dot_general(cotangent, weights, (((1,), (1,)), ((), ())), preferred_element_type=F32)
    grad_gated = lax.psum_scatter(grad_gated, "tp", scatter_dimension=1, tiled=True).astype(BF16)
    outputs = jnp.dot(
        lax.all_gather(gated, "tp", axis=1, tiled=True), weights, preferred_element_type=F32
    ).astype(BF16)
    return grad_gated, outputs


def ring_place(step, size):
    half = (size + 1) // 2
    return jnp.where(step < half, 2 * step, 2 * (size - 1 - step) + 1)


def ring_step(row, size):
    return jnp.where(row & 1 == 0, row >> 1, size - 1 - (row >> 1))


def place_kernel(count, scalars, *refs):
    pieces, out_ref = refs[: 4 * count], refs[-1]
    width = out_ref.shape[0]
    half = width // 2
    for i in range(4 * count):
        if i % 4 < 2:
            first, second = pieces[i], pieces[i + 2]
            for k in (0, 1):
                at = pl.ds(pl.multiple_of(scalars[4 * (i // 4) + 2 * (i % 4) + k] * width, width), width)
                out_ref[:, at] = jnp.concatenate(
                    [first[:, k * half : (k + 1) * half], second[:, (2 + k) * half : (3 + k) * half]], 1
                )


def place_pieces(scalars, groups, chans):
    pieces = [p for group in groups for p in group]
    rows = pieces[0].shape[0]
    vmem = pl.BlockSpec(memory_space=pltpu.VMEM)
    return pl.pallas_call(
        functools.partial(place_kernel, len(groups)),
        out_shape=jax.ShapeDtypeStruct((rows, chans), BF16),
        in_specs=[pl.BlockSpec(memory_space=pltpu.SMEM)] + [vmem] * len(pieces),
        out_specs=vmem,
        compiler_params=pltpu.CompilerParams(vmem_limit_bytes=16 << 20),
        cost_estimate=pl.CostEstimate(flops=0, bytes_accessed=4 * rows * chans, transcendentals=0),
    )(scalars, *pieces)


def deal_kernel(sides, scalars, data, kept, away):
    width = kept.shape[-1]
    for i in range(data.shape[1] // (2 * width)):
        for ref, side in ((kept, scalars[0]), (away, 1 - scalars[0])):
            block = data[:, pl.ds(pl.multiple_of((2 * i + side) * width, width), width)]
            if sides:
                ref[i % sides, i // sides] = block
            else:
                ref[i] = block


def deal(side, data, width, sides=0):
    rows, chans = data.shape
    count = chans // (2 * width)
    lead = (sides, count // sides) if sides else (count,)
    out = jax.ShapeDtypeStruct(lead + (rows, width), data.dtype)
    vmem = pl.BlockSpec(memory_space=pltpu.VMEM)
    return pl.pallas_call(
        functools.partial(deal_kernel, sides),
        out_shape=(out, out),
        in_specs=[pl.BlockSpec(memory_space=pltpu.SMEM), vmem],
        out_specs=(vmem, vmem),
        compiler_params=pltpu.CompilerParams(vmem_limit_bytes=GRANT),
        cost_estimate=pl.CostEstimate(flops=0, bytes_accessed=8 * rows * chans, transcendentals=0),
    )(side.reshape(1), data)


def dot(a, b):
    return jnp.dot(a, b, preferred_element_type=F32)


def project_kernel(count, first, last, scalars, gated_own, gated_away, *refs):
    weights, refs = refs[:count], refs[count:]
    width = weights[0].shape[0]
    depth = width // 4
    left, total = refs[-2:]

    def arrange(order):
        for i in range(count):
            for part, ref in enumerate((gated_own, gated_away)):
                blocks = [ref[scalars[1 + 2 * i + way]] for way in (0, 1)]
                rows = ref.shape[1]
                left[i, part * rows : (part + 1) * rows] = jnp.concatenate(
                    [blocks[way][:, (2 * k + way) * depth : (2 * k + way + 1) * depth] for way in (0, 1) for k in order],
                    1,
                )

    @pl.when((pl.program_id(0) == 0) & (scalars[0] == 0))
    def _():
        arrange((0, 1))

    @pl.when((pl.program_id(0) == 0) & (scalars[0] != 0))
    def _():
        arrange((1, 0))

    total[...] = dot(left[0], weights[0][...]) + (0.0 if first else refs[0][...])
    for i in range(1, count):
        total[...] += dot(left[i], weights[i][...])
    if last:
        own_ref, away_ref = refs[-4:-2]
        rows = own_ref.shape[0]
        own_ref[...] = total[:rows]
        away_ref[...] = total[rows:].astype(BF16)
    else:
        refs[-3][...] = total[...]


def project(scalars, gated_own, gated_away, weights, before=None, last=False):
    rows = gated_own.shape[1]
    depth, feats = weights[0].shape
    tile = min(1024, feats)
    whole = pl.BlockSpec((2 * rows, tile), lambda j, s: (0, j))
    block = pl.BlockSpec((rows, tile), lambda j, s: (0, j))
    halves = tuple(jax.ShapeDtypeStruct((rows, feats), kind) for kind in (F32, BF16))
    return pl.pallas_call(
        functools.partial(project_kernel, len(weights), before is None, last),
        out_shape=halves if last else jax.ShapeDtypeStruct((2 * rows, feats), F32),
        grid_spec=pltpu.PrefetchScalarGridSpec(
            num_scalar_prefetch=1,
            grid=(feats // tile,),
            in_specs=[pl.BlockSpec(gated_own.shape, lambda j, s: (0, 0, 0))] * 2
            + [pl.BlockSpec((depth, tile), lambda j, s: (0, j))] * len(weights)
            + [whole] * (before is not None),
            out_specs=(block, block) if last else whole,
            scratch_shapes=[
                pltpu.VMEM((len(weights), 2 * rows, depth), BF16),
                pltpu.VMEM((2 * rows, tile), F32),
            ],
        ),
        compiler_params=pltpu.CompilerParams(vmem_limit_bytes=GRANT),
        cost_estimate=pl.CostEstimate(
            flops=4 * rows * depth * len(weights) * feats,
            bytes_accessed=2 * depth * feats * len(weights) + 4 * gated_own.size + 8 * rows * feats,
            transcendentals=0,
        ),
    )(scalars, gated_own, gated_away, *weights, *([] if before is None else [before]))


def on_ring(queries, keys, values, w_out, taps, seg_ids, cotangent):
    rows, chans = queries.shape
    length = rows
    nseq = lax.axis_size("seq")
    place = lax.axis_index("seq")
    size = nseq // 4
    core, pair, row = [i.astype(jnp.int32) for i in (place & 1, (place >> 1) & 1, place >> 2)]
    at = ring_step(row, size)
    swap_core = [(i, i ^ 1) for i in range(nseq)]
    swap_pair = [(i, i ^ 2) for i in range(nseq)]
    walk = list(range(0, size, 2)) + list(range(1, size, 2))[::-1]
    onward = [(4 * walk[i] + k, 4 * walk[(i + 1) % size] + k) for i in range(size) for k in range(4)]
    backward = [(b, a) for a, b in onward]
    later = [(i, i + 1) for i in range(nseq - 1)]
    earlier = [(i + 1, i) for i in range(nseq - 1)]
    send = functools.partial(lax.ppermute, axis_name="seq")
    tie = lax.optimization_barrier
    linked = links(seg_ids, place)
    table, high, low = spectrum_table(length)
    table_now, high_now, low_now = table[:, length:], high[:, length:], low[:, length:]
    scale = 1.0 / length

    half = rows // 2
    first, second = w_out[:half], w_out[half:]
    cot_away = send(cotangent, perm=swap_pair)
    swapped = send(w_out, perm=swap_core)
    product, cot_away = tie((mul(keys, values), cot_away))
    before = send(product, perm=later)
    filt = forward_dft(high_now, low_now, tie(taps.T), ((1,), (0,)))

    block = [ring_place(lax.rem(at - s + size, size), size) for s in range(size)]
    middle = min(2, size - 1)
    cuts = [range(0, max(size // 2, 1)), range(max(size // 2, 1), size - 1), range(size - 1, size)]
    weights, own, away = [None] * size, [None] * size, [None] * size
    fresh = []
    sums = None
    dims = (((1,), (1,)), ((), ()))

    def product_of(step, parts):
        weights[step] = jnp.concatenate(parts, 0)
        grad = lax.dot_general(cot_pair, weights[step], dims, preferred_element_type=F32).astype(BF16)
        own[step], away[step] = grad[:rows], send(grad[rows:], perm=swap_pair)
        fresh.append(step)

    def projected(steps, sums, last):
        places = [b for s in steps for b in (block[s], block[(size - s) % size])]
        scalars = jnp.stack([core] + places)
        return project(scalars, gated_own, gated_away, [weights[s] for s in steps], sums, last)

    waiting = [(first, swapped[:half], second, swapped[half:])]
    for step in range(1, size):
        due = fresh[:-1] if step < size - 1 else fresh[:]
        for s in due:
            first, second, own[s], away[s] = tie((first, second, own[s], away[s]))
        fresh = fresh[len(due) :]
        if step == size - 1 and sums is not None:
            first, second, sums = tie((first, second, sums))
        first, second = send(first, perm=onward), send(second, perm=backward)
        waiting.append((first, send(first, perm=swap_core), second, send(second, perm=swap_core)))
        if step < middle:
            continue
        if step == middle:
            _, _, cot_away, before = tie((first, second, cot_away, before))
            cot_pair = jnp.concatenate([cotangent, cot_away], 0)
        if step == size - 1 and sums is not None and len(cuts[1]):
            sums = projected(cuts[1], sums, False)
            waiting[-1], sums = tie((waiting[-1], sums))
        for s, parts in enumerate(waiting, step + 1 - len(waiting)):
            product_of(s, parts if s < step else tie(parts))
        waiting = []
        if step == middle:
            before = jnp.where(linked, before, jnp.zeros_like(before))
            data = forward_dft(high, low, jnp.concatenate([before, product], 0), ((1,), (0,)))
            filtered = inverse_dft(table_now, times(filt, data), scale).astype(BF16)
            gated = mul(queries, filtered)
            width = chans // (2 * size)
            gated_own, gated_away = deal(pair, gated, width)
            gated_away = send(gated_away, perm=swap_pair)
        if step == max(cuts[0][-1] + 1, middle) and step < size - 1:
            sums = projected(cuts[0], None, False)
        if step == size - 1:
            sums = projected(cuts[2] if sums is not None else range(size), sums, True)
            away[step], sums = tie((away[step], sums))

    out_own, out_away = sums
    out_away = send(out_away, perm=swap_pair)
    groups, places = [], []
    for s in range(size):
        m = (size - s) % size
        groups.append((own[s], away[s], own[m], away[m]))
        for side in (pair, 1 - pair):
            places += [4 * block[s] + 2 * side + core, 4 * block[s] + 2 * side + 1 - core]
    grad_gated = place_pieces(jnp.stack(places), groups, chans)
    grad_queries = mul(grad_gated, filtered)
    grad_filtered = mul(grad_gated, queries)
    grads = forward_dft(high_now, low_now, grad_filtered, ((1,), (0,)))
    back = inverse_dft(table, times_conj(grads, filt), scale)
    across = jnp.where(linked, back[:length], 0.0).astype(BF16)
    ahead = send(across, perm=earlier)
    taps_part = inverse_dft(table_now, times_conj(grads, data), scale)
    taps_grad = sum_over_ring(taps_part, nseq, place).T
    outputs = (out_own + out_away.astype(F32)).astype(BF16)
    grad_product = (back[length:] + ahead.astype(F32)).astype(BF16)
    grad_keys = mul(grad_product, values)
    grad_values = mul(grad_product, keys)
    return (outputs, grad_queries, grad_keys, grad_values, taps_grad)


def on_device(queries, keys, values, w_out, taps, seg_ids, cotangent):
    rows, chans = queries.shape
    length = taps.shape[1]
    assert rows == length
    nseq = lax.axis_size("seq")
    place = lax.axis_index("seq")
    table, high, low = spectrum_table(length)
    table_now, high_now, low_now = table[:, length:], high[:, length:], low[:, length:]
    scale = 1.0 / length
    later = [(i, i + 1) for i in range(nseq - 1)]
    earlier = [(i + 1, i) for i in range(nseq - 1)]
    linked = links(seg_ids, place)

    product = mul(keys, values)
    before = lax.ppermute(product, "seq", later)
    before = jnp.where(linked, before, jnp.zeros_like(before))
    data = forward_dft(high, low, jnp.concatenate([before, product], 0), ((1,), (0,)))
    filt = forward_dft(high_now, low_now, taps, ((1,), (1,)))
    filtered = inverse_dft(table_now, times(filt, data), scale).astype(BF16)
    gated = mul(queries, filtered)

    grad_gated, outputs = gathered_products(gated, cotangent, w_out)
    grad_queries = mul(grad_gated, filtered)
    grad_filtered = mul(grad_gated, queries)
    grads = forward_dft(high_now, low_now, grad_filtered, ((1,), (0,)))
    back = inverse_dft(table, times_conj(grads, filt), scale)
    across = jnp.where(linked, back[:length], 0.0).astype(BF16)
    ahead = lax.ppermute(across, "seq", earlier)
    taps_part = inverse_dft(table_now, times_conj(grads, data), scale)
    taps_grad = scatter_sum(taps_part, nseq, place, ()).T
    grad_product = (back[length:] + ahead.astype(F32)).astype(BF16)
    grad_keys = mul(grad_product, values)
    grad_values = mul(grad_product, keys)
    return (outputs, grad_queries, grad_keys, grad_values, taps_grad)


def solution(mesh):
    block = P("seq", "tp")
    count = mesh.shape["seq"]
    ring = mesh.shape["tp"] == 1 and count & (count - 1) == 0 and count >= 8

    def run(queries, keys, values, w_out, taps, seg_ids, cotangent):
        rows, chans = queries.shape
        place = on_ring if ring and rows * count == chans else on_device
        return place(queries, keys, values, w_out, taps, seg_ids, cotangent)

    return jax.shard_map(
        run,
        mesh=mesh,
        in_specs=(block, block, block, block, P("tp", None), P(), block),
        out_specs=(block, block, block, block, P(("tp", "seq"), None)),
        check_vma=False,
    )
```

```python
import functools

import jax
import jax.numpy as jnp
import numpy as np
from jax import lax
from jax.experimental import pallas as pl
from jax.experimental.pallas import tpu as pltpu
from jax.sharding import PartitionSpec as P

F32 = jnp.float32
BF16 = jnp.bfloat16
GRANT = 16 << 20


def spectrum_table(length):
    angles = np.pi * (2 * np.arange(length)[:, None] + 1) * np.arange(-length, length)[None, :] / (2 * length)
    table = np.concatenate([np.cos(angles), -np.sin(angles)], 0).astype(np.float32)
    high = table.astype(BF16)
    low = (table - high.astype(np.float32)).astype(BF16)
    return table, high, low


def forward_dft(high, low, data, dims):
    first = lax.dot_general(high, data, (dims, ((), ())), preferred_element_type=F32)
    second = lax.dot_general(low, data, (dims, ((), ())), preferred_element_type=F32)
    return first + second


def times(a, b):
    half = a.shape[0] // 2
    ar, ai, br, bi = a[:half], a[half:], b[:half], b[half:]
    return jnp.concatenate([ar * br - ai * bi, ar * bi + ai * br], 0)


def times_conj(a, b):
    half = a.shape[0] // 2
    ar, ai, br, bi = a[:half], a[half:], b[:half], b[half:]
    return jnp.concatenate([ar * br + ai * bi, ai * br - ar * bi], 0)


def inverse_dft(table, spectrum, scale):
    done = lax.dot_general(
        table, spectrum, (((0,), (0,)), ((), ())), precision=lax.Precision.HIGH, preferred_element_type=F32
    )
    return done * scale


def mul(a, b):
    return (a.astype(F32) * b.astype(F32)).astype(BF16)


def pick(data, width, side):
    blocks = [data[:, i : i + width] for i in range(0, data.shape[1], width)]
    return jnp.concatenate([jnp.where(side == 0, a, b) for a, b in zip(blocks[::2], blocks[1::2])], 1)


def scatter_sum(part, nseq, place, order):
    share = part.shape[1] // nseq
    bits = nseq.bit_length() - 1
    if nseq != 1 << bits:
        return lax.psum_scatter(part, "seq", scatter_dimension=1, tiled=True)
    left = list(range(bits))
    for step in [b for b in order if b < bits] + [b for b in range(bits) if b not in order]:
        width = share << sum(b < step for b in left)
        left.remove(step)
        mine = (place >> step) & 1
        away = pick(part, width, 1 - mine)
        if step:
            away = away.astype(BF16)
        away = lax.ppermute(away, "seq", [(i, i ^ (1 << step)) for i in range(nseq)])
        part = pick(part, width, mine) + away.astype(F32)
    return part


def deal_kernel(sides, scalars, data, kept, away):
    width = kept.shape[-1]
    for i in range(data.shape[1] // (2 * width)):
        for ref, side in ((kept, scalars[0]), (away, 1 - scalars[0])):
            block = data[:, pl.ds(pl.multiple_of((2 * i + side) * width, width), width)]
            if sides:
                ref[i % sides, i // sides] = block
            else:
                ref[i] = block


def deal(side, data, width, sides=0):
    rows, chans = data.shape
    count = chans // (2 * width)
    lead = (sides, count // sides) if sides else (count,)
    out = jax.ShapeDtypeStruct(lead + (rows, width), data.dtype)
    vmem = pl.BlockSpec(memory_space=pltpu.VMEM)
    return pl.pallas_call(
        functools.partial(deal_kernel, sides),
        out_shape=(out, out),
        in_specs=[pl.BlockSpec(memory_space=pltpu.SMEM), vmem],
        out_specs=(vmem, vmem),
        compiler_params=pltpu.CompilerParams(vmem_limit_bytes=GRANT),
        cost_estimate=pl.CostEstimate(flops=0, bytes_accessed=8 * rows * chans, transcendentals=0),
    )(side.reshape(1), data)


def sum_over_ring(part, nseq, place):
    core, pair, row = place & 1, (place >> 1) & 1, place >> 2
    lags, chans = part.shape
    size, chans = nseq // 4, chans // nseq

    def halve(part, bit, mine, kind):
        away = lax.dynamic_index_in_dim(part, 1 - mine, 1, False).astype(kind)
        away = lax.ppermute(away, "seq", [(i, i ^ bit) for i in range(nseq)])
        return lax.dynamic_index_in_dim(part, mine, 1, False) + away.astype(F32)

    kept, away = deal(core.astype(jnp.int32), part, chans, 2)
    part = kept + lax.ppermute(away, "seq", [(i, i ^ 1) for i in range(nseq)])
    part = part.reshape(2, size, lags, chans)
    left = size
    while left > 1:
        bit = size // left
        mine = (row // bit) & 1
        part = part.reshape(2 * left // 2, 2, lags, chans)
        part = halve(part, 4 * bit, mine, BF16).reshape(2, left // 2, lags, chans)
        left //= 2
    return halve(part.reshape(1, 2, lags, chans), 2, pair, BF16).reshape(lags, chans)


def links(seg_ids, place):
    own = lax.dynamic_index_in_dim(seg_ids, place, 0, False)
    prior = lax.dynamic_index_in_dim(seg_ids, jnp.maximum(place - 1, 0), 0, False)
    return (place > 0) & (own == prior)


def gathered_products(gated, cotangent, w_out):
    weights = lax.all_gather(w_out, "seq", axis=0, tiled=True)
    grad_gated = lax.dot_general(cotangent, weights, (((1,), (1,)), ((), ())), preferred_element_type=F32)
    grad_gated = lax.psum_scatter(grad_gated, "tp", scatter_dimension=1, tiled=True).astype(BF16)
    outputs = jnp.dot(
        lax.all_gather(gated, "tp", axis=1, tiled=True), weights, preferred_element_type=F32
    ).astype(BF16)
    return grad_gated, outputs


def ring_place(step, size):
    half = (size + 1) // 2
    return jnp.where(step < half, 2 * step, 2 * (size - 1 - step) + 1)


def ring_step(row, size):
    return jnp.where(row & 1 == 0, row >> 1, size - 1 - (row >> 1))


def assemble_kernel(count, where_ref, *refs):
    pieces, out_ref = refs[:-1], refs[-1]
    width = out_ref.shape[0]
    for i in range(count):
        for half in range(2):
            at = pl.ds(pl.multiple_of(where_ref[2 * i + half] * width, width), width)
            out_ref[:, at] = pieces[i][:, half * width : (half + 1) * width]


def assemble(where, pieces, chans):
    rows = pieces[0].shape[0]
    vmem = pl.BlockSpec(memory_space=pltpu.VMEM)
    return pl.pallas_call(
        functools.partial(assemble_kernel, len(pieces)),
        out_shape=jax.ShapeDtypeStruct((rows, chans), pieces[0].dtype),
        in_specs=[pl.BlockSpec(memory_space=pltpu.SMEM)] + [vmem] * len(pieces),
        out_specs=vmem,
        compiler_params=pltpu.CompilerParams(vmem_limit_bytes=16 << 20),
        cost_estimate=pl.CostEstimate(flops=0, bytes_accessed=4 * rows * chans, transcendentals=0),
    )(where, *pieces)


def project_kernel(count, last, where_ref, gated_own, gated_away, *refs):
    weights, refs = refs[: 2 * count], refs[2 * count :]
    width = weights[0].shape[0]
    total = None
    for i in range(count):
        left = jnp.concatenate(
            [
                jnp.concatenate([ref[where_ref[2 * i]][:, :width], ref[where_ref[2 * i + 1]][:, width:]], 1)
                for ref in (gated_own, gated_away)
            ],
            0,
        )
        right = jnp.concatenate([weights[2 * i][...], weights[2 * i + 1][...]], 0)
        part = jnp.dot(left, right, preferred_element_type=F32)
        total = part if total is None else total + part
    if last:
        before_ref, own_ref, away_ref = refs
        total = total + before_ref[...]
        rows = own_ref.shape[0]
        own_ref[...] = total[:rows]
        away_ref[...] = total[rows:].astype(BF16)
    else:
        refs[0][...] = total


def project(where, gated_own, gated_away, weights, before=None):
    rows = gated_own.shape[1]
    depth, feats = weights[0].shape
    tile = min(512, feats)
    last = before is not None
    whole = pl.BlockSpec((2 * rows, tile), lambda j, where: (0, j))
    block = pl.BlockSpec((rows, tile), lambda j, where: (0, j))
    split = tuple(jax.ShapeDtypeStruct((rows, feats), kind) for kind in (F32, BF16))
    return pl.pallas_call(
        functools.partial(project_kernel, len(weights) // 2, last),
        out_shape=split if last else jax.ShapeDtypeStruct((2 * rows, feats), F32),
        grid_spec=pltpu.PrefetchScalarGridSpec(
            num_scalar_prefetch=1,
            grid=(feats // tile,),
            in_specs=[pl.BlockSpec(gated_own.shape, lambda j, where: (0, 0, 0))] * 2
            + [pl.BlockSpec((depth, tile), lambda j, where: (0, j))] * len(weights)
            + [whole] * last,
            out_specs=(block, block) if last else whole,
        ),
        compiler_params=pltpu.CompilerParams(vmem_limit_bytes=32 << 20),
        cost_estimate=pl.CostEstimate(
            flops=4 * rows * depth * len(weights) * feats,
            bytes_accessed=2 * depth * feats * len(weights) + 4 * gated_own.size + 8 * rows * feats,
            transcendentals=0,
        ),
    )(where, gated_own, gated_away, *weights, *([before] if last else []))


def on_ring(queries, keys, values, w_out, taps, seg_ids, cotangent):
    rows, chans = queries.shape
    length = rows
    feats = cotangent.shape[1]
    nseq = lax.axis_size("seq")
    place = lax.axis_index("seq")
    size = nseq // 4
    core, pair, row = [i.astype(jnp.int32) for i in (place & 1, (place >> 1) & 1, place >> 2)]
    at = ring_step(row, size)
    swap_core = [(i, i ^ 1) for i in range(nseq)]
    swap_pair = [(i, i ^ 2) for i in range(nseq)]
    walk = list(range(0, size, 2)) + list(range(1, size, 2))[::-1]
    onward = [(4 * walk[i] + k, 4 * walk[(i + 1) % size] + k) for i in range(size) for k in range(4)]
    behind = [(b, a) for a, b in onward]
    later = [(i, i + 1) for i in range(nseq - 1)]
    earlier = [(i + 1, i) for i in range(nseq - 1)]
    send = functools.partial(lax.ppermute, axis_name="seq")
    tie = lax.optimization_barrier
    linked = links(seg_ids, place)
    table, high, low = spectrum_table(length)
    table_now, high_now, low_now = table[:, length:], high[:, length:], low[:, length:]
    scale = 1.0 / length

    half = feats // 2
    low_half, high_half = w_out[:, :half], w_out[:, half:]
    kept = jnp.where(core == 0, low_half, high_half)
    swapped = send(jnp.where(core == 0, high_half, low_half), perm=swap_core)
    first = jnp.where(core == 0, kept, swapped)
    second = jnp.where(core == 0, swapped, kept)
    first, second, keys_then, taps, cotangent = tie((first, second, keys, taps, cotangent))
    cot_away = send(cotangent, perm=swap_pair)
    product = mul(keys_then, values)
    product, cot_away = tie((product, cot_away))
    before = send(product, perm=later)
    filt = forward_dft(high_now, low_now, tie(taps.T), ((1,), (0,)))

    dims = (((1,), (1,)), ((), ()))
    dot = functools.partial(lax.dot_general, dimension_numbers=dims, preferred_element_type=F32)
    mine, other, own, away, columns, places = [], [], [None] * size, [None] * size, [], []
    early = size - 2
    for step in range(size):
        first_row = ring_place(lax.rem(at - step + size, size), size)
        second_row = ring_place(lax.rem(at + step, size), size)
        columns += [first_row, second_row]
        for side in (pair, 1 - pair):
            places += [4 * first_row + 2 * side, 4 * second_row + 2 * side + 1]
    columns = jnp.stack(columns)

    def product_of(step):
        blocks = tie((mine[2 * step], mine[2 * step + 1], other[2 * step], other[2 * step + 1]))
        first_grad = (dot(cot_mine, blocks[0]) + dot(cot_other, blocks[2])).astype(BF16)
        second_grad = (dot(cot_mine, blocks[1]) + dot(cot_other, blocks[3])).astype(BF16)
        grad = jnp.concatenate([first_grad, second_grad], 1)
        own[step] = grad[:rows]
        away[step] = send(grad[rows:], perm=swap_pair)

    for step in range(size):
        if step:
            if step >= 3:
                for s in (0, 1) if step == 3 else (step - 2,):
                    first, second, own[s], away[s] = tie((first, second, own[s], away[s]))
            if step == size - 2:
                first, second, gated_away = tie((first, second, gated_away))
            if step == size - 1:
                sums = [project(columns[: 2 * early], gated_own, gated_away, w[: 2 * early]) for w in (mine, other)]
                first, second, sums = tie((first, second, sums))
            first, second = send(first, perm=onward), send(second, perm=behind)
        mine += [first, second]
        other += [send(first, perm=swap_core), send(second, perm=swap_core)]
        if step == 0:
            continue
        if step == 1:
            _, _, cot_away = tie((first, second, cot_away))
            cot_pair = jnp.concatenate([cotangent, cot_away], 0)
            cot_mine = jnp.where(core == 0, cot_pair[:, :half], cot_pair[:, half:])
            cot_other = jnp.where(core == 0, cot_pair[:, half:], cot_pair[:, :half])
            product_of(0)
            _, _, before = tie((first, second, before))
            before = jnp.where(linked, before, jnp.zeros_like(before))
            data = forward_dft(high, low, jnp.concatenate([before, product], 0), ((1,), (0,)))
            filtered = inverse_dft(table_now, times(filt, data), scale).astype(BF16)
            gated = mul(queries, filtered)
            gated_own, gated_away = deal(pair, gated, chans // (2 * size))
            gated_away = send(gated_away, perm=swap_pair)
        product_of(step)

    outs = []
    for w, total in zip((mine, other), sums):
        kept, sent = project(columns[2 * early :], gated_own, gated_away, w[2 * early :], total)
        outs += [kept, send(sent, perm=swap_pair)]
    pieces = [p for s in range(size) for p in (own[s], away[s])]
    grad_gated = assemble(jnp.stack(places), pieces, chans)
    grad_queries = mul(grad_gated, filtered)
    grad_filtered = mul(grad_gated, queries)
    grads = forward_dft(high_now, low_now, grad_filtered, ((1,), (0,)))
    back = inverse_dft(table, times_conj(grads, filt), scale)
    across = jnp.where(linked, back[:length], 0.0).astype(BF16)
    ahead = send(across, perm=earlier)
    taps_part = inverse_dft(table_now, times_conj(grads, data), scale)
    taps_grad = sum_over_ring(taps_part, nseq, place).T
    ahead, outs, taps_grad = tie((ahead, outs, taps_grad))
    out_mine = (outs[0] + outs[1].astype(F32)).astype(BF16)
    out_other = (outs[2] + outs[3].astype(F32)).astype(BF16)
    outputs = jnp.concatenate(
        [jnp.where(core == 0, out_mine, out_other), jnp.where(core == 0, out_other, out_mine)], 1
    )
    grad_product = (back[length:] + ahead.astype(F32)).astype(BF16)
    grad_keys = mul(grad_product, values)
    grad_values = mul(grad_product, keys)
    return (outputs, grad_queries, grad_keys, grad_values, taps_grad)


def on_device(queries, keys, values, w_out, taps, seg_ids, cotangent):
    rows, chans = queries.shape
    length = taps.shape[1]
    assert rows == length
    nseq = lax.axis_size("seq")
    place = lax.axis_index("seq")
    table, high, low = spectrum_table(length)
    table_now, high_now, low_now = table[:, length:], high[:, length:], low[:, length:]
    scale = 1.0 / length
    later = [(i, i + 1) for i in range(nseq - 1)]
    earlier = [(i + 1, i) for i in range(nseq - 1)]
    linked = links(seg_ids, place)

    product = mul(keys, values)
    before = lax.ppermute(product, "seq", later)
    before = jnp.where(linked, before, jnp.zeros_like(before))
    data = forward_dft(high, low, jnp.concatenate([before, product], 0), ((1,), (0,)))
    filt = forward_dft(high_now, low_now, taps, ((1,), (1,)))
    filtered = inverse_dft(table_now, times(filt, data), scale).astype(BF16)
    gated = mul(queries, filtered)

    grad_gated, outputs = gathered_products(gated, cotangent, w_out)
    grad_queries = mul(grad_gated, filtered)
    grad_filtered = mul(grad_gated, queries)
    grads = forward_dft(high_now, low_now, grad_filtered, ((1,), (0,)))
    back = inverse_dft(table, times_conj(grads, filt), scale)
    across = jnp.where(linked, back[:length], 0.0).astype(BF16)
    ahead = lax.ppermute(across, "seq", earlier)
    taps_part = inverse_dft(table_now, times_conj(grads, data), scale)
    taps_grad = scatter_sum(taps_part, nseq, place, ()).T
    grad_product = (back[length:] + ahead.astype(F32)).astype(BF16)
    grad_keys = mul(grad_product, values)
    grad_values = mul(grad_product, keys)
    return (outputs, grad_queries, grad_keys, grad_values, taps_grad)


def solution(mesh):
    block = P("seq", "tp")
    count = mesh.shape["seq"]
    ring = mesh.shape["tp"] == 1 and count & (count - 1) == 0 and count >= 16

    def run(queries, keys, values, w_out, taps, seg_ids, cotangent):
        rows, chans = queries.shape
        place = on_ring if ring and rows * count == chans else on_device
        return place(queries, keys, values, w_out, taps, seg_ids, cotangent)

    return jax.shard_map(
        run,
        mesh=mesh,
        in_specs=(block, block, block, block, P("tp", None), P(), block),
        out_specs=(block, block, block, block, P(("tp", "seq"), None)),
        check_vma=False,
    )
```

```python
import functools

import jax
import jax.numpy as jnp
import numpy as np
from jax import lax
from jax.experimental import pallas as pl
from jax.experimental.pallas import tpu as pltpu
from jax.sharding import PartitionSpec as P

F32 = jnp.float32
BF16 = jnp.bfloat16
GRANT = 16 << 20


def spectrum_table(length):
    angles = np.pi * (2 * np.arange(length)[:, None] + 1) * np.arange(-length, length)[None, :] / (2 * length)
    table = np.concatenate([np.cos(angles), -np.sin(angles)], 0).astype(np.float32)
    high = table.astype(BF16)
    low = (table - high.astype(np.float32)).astype(BF16)
    return table, high, low


def forward_dft(high, low, data, dims):
    first = lax.dot_general(high, data, (dims, ((), ())), preferred_element_type=F32)
    second = lax.dot_general(low, data, (dims, ((), ())), preferred_element_type=F32)
    return first + second


def times(a, b):
    half = a.shape[0] // 2
    ar, ai, br, bi = a[:half], a[half:], b[:half], b[half:]
    return jnp.concatenate([ar * br - ai * bi, ar * bi + ai * br], 0)


def times_conj(a, b):
    half = a.shape[0] // 2
    ar, ai, br, bi = a[:half], a[half:], b[:half], b[half:]
    return jnp.concatenate([ar * br + ai * bi, ai * br - ar * bi], 0)


def inverse_dft(table, spectrum, scale):
    done = lax.dot_general(
        table, spectrum, (((0,), (0,)), ((), ())), precision=lax.Precision.HIGH, preferred_element_type=F32
    )
    return done * scale


def mul(a, b):
    return (a.astype(F32) * b.astype(F32)).astype(BF16)


def pick(data, width, side):
    blocks = [data[:, i : i + width] for i in range(0, data.shape[1], width)]
    return jnp.concatenate([jnp.where(side == 0, a, b) for a, b in zip(blocks[::2], blocks[1::2])], 1)


def scatter_sum(part, nseq, place, order):
    share = part.shape[1] // nseq
    bits = nseq.bit_length() - 1
    if nseq != 1 << bits:
        return lax.psum_scatter(part, "seq", scatter_dimension=1, tiled=True)
    left = list(range(bits))
    for step in [b for b in order if b < bits] + [b for b in range(bits) if b not in order]:
        width = share << sum(b < step for b in left)
        left.remove(step)
        mine = (place >> step) & 1
        away = pick(part, width, 1 - mine)
        if step:
            away = away.astype(BF16)
        away = lax.ppermute(away, "seq", [(i, i ^ (1 << step)) for i in range(nseq)])
        part = pick(part, width, mine) + away.astype(F32)
    return part


def deal_kernel(sides, scalars, data, kept, away):
    width = kept.shape[-1]
    for i in range(data.shape[1] // (2 * width)):
        for ref, side in ((kept, scalars[0]), (away, 1 - scalars[0])):
            block = data[:, pl.ds(pl.multiple_of((2 * i + side) * width, width), width)]
            if sides:
                ref[i % sides, i // sides] = block
            else:
                ref[i] = block


def deal(side, data, width, sides=0):
    rows, chans = data.shape
    count = chans // (2 * width)
    lead = (sides, count // sides) if sides else (count,)
    out = jax.ShapeDtypeStruct(lead + (rows, width), data.dtype)
    vmem = pl.BlockSpec(memory_space=pltpu.VMEM)
    return pl.pallas_call(
        functools.partial(deal_kernel, sides),
        out_shape=(out, out),
        in_specs=[pl.BlockSpec(memory_space=pltpu.SMEM), vmem],
        out_specs=(vmem, vmem),
        compiler_params=pltpu.CompilerParams(vmem_limit_bytes=GRANT),
        cost_estimate=pl.CostEstimate(flops=0, bytes_accessed=8 * rows * chans, transcendentals=0),
    )(side.reshape(1), data)


def sum_over_ring(part, nseq, place):
    core, pair, row = place & 1, (place >> 1) & 1, place >> 2
    lags, chans = part.shape
    size, chans = nseq // 4, chans // nseq

    def halve(part, bit, mine, kind):
        away = lax.dynamic_index_in_dim(part, 1 - mine, 1, False).astype(kind)
        away = lax.ppermute(away, "seq", [(i, i ^ bit) for i in range(nseq)])
        return lax.dynamic_index_in_dim(part, mine, 1, False) + away.astype(F32)

    kept, away = deal(core.astype(jnp.int32), part, chans, 2)
    part = kept + lax.ppermute(away, "seq", [(i, i ^ 1) for i in range(nseq)])
    part = part.reshape(2, size, lags, chans)
    left = size
    while left > 1:
        bit = size // left
        mine = (row // bit) & 1
        part = part.reshape(2 * left // 2, 2, lags, chans)
        part = halve(part, 4 * bit, mine, BF16).reshape(2, left // 2, lags, chans)
        left //= 2
    return halve(part.reshape(1, 2, lags, chans), 2, pair, BF16).reshape(lags, chans)


def links(seg_ids, place):
    own = lax.dynamic_index_in_dim(seg_ids, place, 0, False)
    prior = lax.dynamic_index_in_dim(seg_ids, jnp.maximum(place - 1, 0), 0, False)
    return (place > 0) & (own == prior)


def gathered_products(gated, cotangent, w_out):
    weights = lax.all_gather(w_out, "seq", axis=0, tiled=True)
    grad_gated = lax.dot_general(cotangent, weights, (((1,), (1,)), ((), ())), preferred_element_type=F32)
    grad_gated = lax.psum_scatter(grad_gated, "tp", scatter_dimension=1, tiled=True).astype(BF16)
    outputs = jnp.dot(
        lax.all_gather(gated, "tp", axis=1, tiled=True), weights, preferred_element_type=F32
    ).astype(BF16)
    return grad_gated, outputs


def ring_place(step, size):
    half = (size + 1) // 2
    return jnp.where(step < half, 2 * step, 2 * (size - 1 - step) + 1)


def ring_step(row, size):
    return jnp.where(row & 1 == 0, row >> 1, size - 1 - (row >> 1))


def products_kernel(size, scalars, cot_own, cot_away, gated_own, gated_away, *refs):
    pieces, (grad_own, grad_away, out_own, out_away, grad) = refs[: 4 * size], refs[4 * size :]
    rows = cot_own.shape[0]

    @pl.when(pl.program_id(0) == 0)
    def _():
        grad[...] = jnp.zeros_like(grad)

    def add(order):
        cot = jnp.concatenate([cot_own[...], cot_away[...]], 0)
        total = None
        for s in range(size):
            m = (size - s) % size
            block = (pieces[4 * s], pieces[4 * m + 2], pieces[4 * s + 1], pieces[4 * m + 3])
            block = jnp.concatenate([block[k][...] for k in order], 0)
            grad[s] += lax.dot_general(cot, block, (((1,), (1,)), ((), ())), preferred_element_type=F32)
            left = jnp.concatenate([gated_own[scalars[1 + s]], gated_away[scalars[1 + s]]], 0)
            part = jnp.dot(left, block, preferred_element_type=F32)
            total = part if total is None else total + part
        out_own[...] = total[:rows]
        out_away[...] = total[rows:].astype(BF16)

    @pl.when(scalars[0] == 0)
    def _():
        add((0, 1, 2, 3))

    @pl.when(scalars[0] != 0)
    def _():
        add((2, 3, 0, 1))

    @pl.when(pl.program_id(0) == pl.num_programs(0) - 1)
    def _():
        for s in range(size):
            grad_own[scalars[1 + s]] = grad[s, :rows].astype(BF16)
            grad_away[scalars[1 + s]] = grad[s, rows:].astype(BF16)


def products(scalars, cot_own, cot_away, gated_own, gated_away, pieces):
    rows, feats = cot_own.shape
    size, _, width = gated_own.shape
    depth = pieces[0].shape[0]
    tile = min(512, feats)
    block = pl.BlockSpec((rows, tile), lambda j, s: (0, j))
    whole = pl.BlockSpec(gated_own.shape, lambda j, s: (0, 0, 0))
    return pl.pallas_call(
        functools.partial(products_kernel, size),
        out_shape=(
            jax.ShapeDtypeStruct(gated_own.shape, BF16),
            jax.ShapeDtypeStruct(gated_own.shape, BF16),
            jax.ShapeDtypeStruct((rows, feats), F32),
            jax.ShapeDtypeStruct((rows, feats), BF16),
        ),
        grid_spec=pltpu.PrefetchScalarGridSpec(
            num_scalar_prefetch=1,
            grid=(feats // tile,),
            in_specs=[block] * 2 + [whole] * 2 + [pl.BlockSpec((depth, tile), lambda j, s: (0, j))] * len(pieces),
            out_specs=(whole, whole, block, block),
            scratch_shapes=[pltpu.VMEM((size, 2 * rows, width), F32)],
        ),
        compiler_params=pltpu.CompilerParams(vmem_limit_bytes=28 << 20),
        cost_estimate=pl.CostEstimate(
            flops=8 * rows * depth * len(pieces) * feats,
            bytes_accessed=2 * depth * len(pieces) * feats + 10 * rows * feats,
            transcendentals=0,
        ),
    )(
        scalars,
        *[
            pltpu.with_memory_space_constraint(a, pltpu.HBM)
            for a in (cot_own, cot_away, gated_own, gated_away, *pieces)
        ],
    )


def merge_kernel(scalars, own, away, out):
    size, _, width = own.shape
    for r in range(size):
        for ref, side in ((own, scalars[0]), (away, 1 - scalars[0])):
            out[:, pl.ds(pl.multiple_of((2 * r + side) * width, width), width)] = ref[r]


def merge(side, own, away):
    size, rows, width = own.shape
    vmem = pl.BlockSpec(memory_space=pltpu.VMEM)
    return pl.pallas_call(
        merge_kernel,
        out_shape=jax.ShapeDtypeStruct((rows, 2 * size * width), own.dtype),
        in_specs=[pl.BlockSpec(memory_space=pltpu.SMEM), vmem, vmem],
        out_specs=vmem,
        compiler_params=pltpu.CompilerParams(vmem_limit_bytes=GRANT),
        cost_estimate=pl.CostEstimate(flops=0, bytes_accessed=8 * own.size, transcendentals=0),
    )(side.reshape(1), own, away)


def on_ring(queries, keys, values, w_out, taps, seg_ids, cotangent):
    rows, chans = queries.shape
    length = rows
    nseq = lax.axis_size("seq")
    place = lax.axis_index("seq")
    size = nseq // 4
    core, pair, row = [i.astype(jnp.int32) for i in (place & 1, (place >> 1) & 1, place >> 2)]
    at = ring_step(row, size)
    swap_core = [(i, i ^ 1) for i in range(nseq)]
    swap_pair = [(i, i ^ 2) for i in range(nseq)]
    walk = list(range(0, size, 2)) + list(range(1, size, 2))[::-1]
    onward = [(4 * walk[i] + k, 4 * walk[(i + 1) % size] + k) for i in range(size) for k in range(4)]
    behind = [(b, a) for a, b in onward]
    later = [(i, i + 1) for i in range(nseq - 1)]
    earlier = [(i + 1, i) for i in range(nseq - 1)]
    send = functools.partial(lax.ppermute, axis_name="seq")
    tie = lax.optimization_barrier
    linked = links(seg_ids, place)
    table, high, low = spectrum_table(length)
    table_now, high_now, low_now = table[:, length:], high[:, length:], low[:, length:]
    scale = 1.0 / length

    half = rows // 2
    first, second = w_out[:half], w_out[half:]
    swapped = send(w_out, perm=swap_core)
    cot_away = send(cotangent, perm=swap_pair)
    product, cot_away = tie((mul(keys, values), cot_away))
    before = send(product, perm=later)
    filt = forward_dft(high_now, low_now, tie(taps.T), ((1,), (0,)))

    pieces = [first, swapped[:half], second, swapped[half:]]
    for step in range(1, size):
        first, second = send(first, perm=onward), send(second, perm=behind)
        swap = (first, second)
        if step == 1:
            *swap, filt = tie((*swap, filt))
        if step == 3:
            before = jnp.where(linked, before, jnp.zeros_like(before))
            data = forward_dft(high, low, jnp.concatenate([before, product], 0), ((1,), (0,)))
            filtered = inverse_dft(table_now, times(filt, data), scale).astype(BF16)
            gated = mul(queries, filtered)
            gated_own, gated_away = deal(pair, gated, chans // (2 * size))
            *swap, gated_own, gated_away = tie((*swap, gated_own, gated_away))
            gated_away = send(gated_away, perm=swap_pair)
        pieces += [first, send(swap[0], perm=swap_core), second, send(swap[1], perm=swap_core)]
    places = [core] + [ring_place(lax.rem(at - s + size, size), size) for s in range(size)]
    grad_own, grad_away, out_own, out_away = products(
        jnp.stack(places), cotangent, cot_away, gated_own, gated_away, pieces
    )
    grad_gated = merge(pair, grad_own, send(grad_away, perm=swap_pair))
    out_away = send(out_away, perm=swap_pair)
    grad_queries = mul(grad_gated, filtered)
    grad_filtered = mul(grad_gated, queries)
    grads = forward_dft(high_now, low_now, grad_filtered, ((1,), (0,)))
    back = inverse_dft(table, times_conj(grads, filt), scale)
    across = jnp.where(linked, back[:length], 0.0).astype(BF16)
    ahead = send(across, perm=earlier)
    taps_part = inverse_dft(table_now, times_conj(grads, data), scale)
    taps_grad = sum_over_ring(taps_part, nseq, place).T
    outputs = (out_own + out_away.astype(F32)).astype(BF16)
    grad_product = (back[length:] + ahead.astype(F32)).astype(BF16)
    grad_keys = mul(grad_product, values)
    grad_values = mul(grad_product, keys)
    return (outputs, grad_queries, grad_keys, grad_values, taps_grad)


def on_device(queries, keys, values, w_out, taps, seg_ids, cotangent):
    rows, chans = queries.shape
    length = taps.shape[1]
    assert rows == length
    nseq = lax.axis_size("seq")
    place = lax.axis_index("seq")
    table, high, low = spectrum_table(length)
    table_now, high_now, low_now = table[:, length:], high[:, length:], low[:, length:]
    scale = 1.0 / length
    later = [(i, i + 1) for i in range(nseq - 1)]
    earlier = [(i + 1, i) for i in range(nseq - 1)]
    linked = links(seg_ids, place)

    product = mul(keys, values)
    before = lax.ppermute(product, "seq", later)
    before = jnp.where(linked, before, jnp.zeros_like(before))
    data = forward_dft(high, low, jnp.concatenate([before, product], 0), ((1,), (0,)))
    filt = forward_dft(high_now, low_now, taps, ((1,), (1,)))
    filtered = inverse_dft(table_now, times(filt, data), scale).astype(BF16)
    gated = mul(queries, filtered)

    grad_gated, outputs = gathered_products(gated, cotangent, w_out)
    grad_queries = mul(grad_gated, filtered)
    grad_filtered = mul(grad_gated, queries)
    grads = forward_dft(high_now, low_now, grad_filtered, ((1,), (0,)))
    back = inverse_dft(table, times_conj(grads, filt), scale)
    across = jnp.where(linked, back[:length], 0.0).astype(BF16)
    ahead = lax.ppermute(across, "seq", earlier)
    taps_part = inverse_dft(table_now, times_conj(grads, data), scale)
    taps_grad = scatter_sum(taps_part, nseq, place, ()).T
    grad_product = (back[length:] + ahead.astype(F32)).astype(BF16)
    grad_keys = mul(grad_product, values)
    grad_values = mul(grad_product, keys)
    return (outputs, grad_queries, grad_keys, grad_values, taps_grad)


def solution(mesh):
    block = P("seq", "tp")
    count = mesh.shape["seq"]
    ring = mesh.shape["tp"] == 1 and count & (count - 1) == 0 and count >= 16

    def run(queries, keys, values, w_out, taps, seg_ids, cotangent):
        rows, chans = queries.shape
        place = on_ring if ring and rows * count == chans else on_device
        return place(queries, keys, values, w_out, taps, seg_ids, cotangent)

    return jax.shard_map(
        run,
        mesh=mesh,
        in_specs=(block, block, block, block, P("tp", None), P(), block),
        out_specs=(block, block, block, block, P(("tp", "seq"), None)),
        check_vma=False,
    )
```

```python
import functools

import jax
import jax.numpy as jnp
import numpy as np
from jax import lax
from jax.experimental import pallas as pl
from jax.experimental.pallas import tpu as pltpu
from jax.sharding import PartitionSpec as P

F32 = jnp.float32
BF16 = jnp.bfloat16
GRANT = 16 << 20


def spectrum_table(length):
    angles = np.pi * (2 * np.arange(length)[:, None] + 1) * np.arange(-length, length)[None, :] / (2 * length)
    table = np.concatenate([np.cos(angles), -np.sin(angles)], 0).astype(np.float32)
    high = table.astype(BF16)
    low = (table - high.astype(np.float32)).astype(BF16)
    return table, high, low


def forward_dft(high, low, data, dims):
    first = lax.dot_general(high, data, (dims, ((), ())), preferred_element_type=F32)
    second = lax.dot_general(low, data, (dims, ((), ())), preferred_element_type=F32)
    return first + second


def times(a, b):
    half = a.shape[0] // 2
    ar, ai, br, bi = a[:half], a[half:], b[:half], b[half:]
    return jnp.concatenate([ar * br - ai * bi, ar * bi + ai * br], 0)


def times_conj(a, b):
    half = a.shape[0] // 2
    ar, ai, br, bi = a[:half], a[half:], b[:half], b[half:]
    return jnp.concatenate([ar * br + ai * bi, ai * br - ar * bi], 0)


def inverse_dft(table, spectrum, scale):
    done = lax.dot_general(
        table, spectrum, (((0,), (0,)), ((), ())), precision=lax.Precision.HIGH, preferred_element_type=F32
    )
    return done * scale


def mul(a, b):
    return (a.astype(F32) * b.astype(F32)).astype(BF16)


def pick(data, width, side):
    blocks = [data[:, i : i + width] for i in range(0, data.shape[1], width)]
    return jnp.concatenate([jnp.where(side == 0, a, b) for a, b in zip(blocks[::2], blocks[1::2])], 1)


def scatter_sum(part, nseq, place, order):
    share = part.shape[1] // nseq
    bits = nseq.bit_length() - 1
    if nseq != 1 << bits:
        return lax.psum_scatter(part, "seq", scatter_dimension=1, tiled=True)
    left = list(range(bits))
    for step in [b for b in order if b < bits] + [b for b in range(bits) if b not in order]:
        width = share << sum(b < step for b in left)
        left.remove(step)
        mine = (place >> step) & 1
        away = pick(part, width, 1 - mine)
        if step:
            away = away.astype(BF16)
        away = lax.ppermute(away, "seq", [(i, i ^ (1 << step)) for i in range(nseq)])
        part = pick(part, width, mine) + away.astype(F32)
    return part


def deal_kernel(sides, scalars, data, kept, away):
    width = kept.shape[-1]
    for i in range(data.shape[1] // (2 * width)):
        for ref, side in ((kept, scalars[0]), (away, 1 - scalars[0])):
            block = data[:, pl.ds(pl.multiple_of((2 * i + side) * width, width), width)]
            if sides:
                ref[i % sides, i // sides] = block
            else:
                ref[i] = block


def deal(side, data, width, sides=0):
    rows, chans = data.shape
    count = chans // (2 * width)
    lead = (sides, count // sides) if sides else (count,)
    out = jax.ShapeDtypeStruct(lead + (rows, width), data.dtype)
    vmem = pl.BlockSpec(memory_space=pltpu.VMEM)
    return pl.pallas_call(
        functools.partial(deal_kernel, sides),
        out_shape=(out, out),
        in_specs=[pl.BlockSpec(memory_space=pltpu.SMEM), vmem],
        out_specs=(vmem, vmem),
        compiler_params=pltpu.CompilerParams(vmem_limit_bytes=GRANT),
        cost_estimate=pl.CostEstimate(flops=0, bytes_accessed=8 * rows * chans, transcendentals=0),
    )(side.reshape(1), data)


def sum_over_ring(part, nseq, place, guest):
    core, pair, row = place & 1, (place >> 1) & 1, place >> 2
    lags, chans = part.shape
    size, chans = nseq // 4, chans // nseq

    def halve(part, bit, mine, kind):
        away = lax.dynamic_index_in_dim(part, 1 - mine, 1, False).astype(kind)
        away = lax.ppermute(away, "seq", [(i, i ^ bit) for i in range(nseq)])
        return lax.dynamic_index_in_dim(part, mine, 1, False) + away.astype(F32)

    kept, away = deal(core.astype(jnp.int32), part, chans, 2)
    part = kept + lax.ppermute(away, "seq", [(i, i ^ 1) for i in range(nseq)])
    part = part.reshape(2, size, lags, chans)
    left = size
    while left > 1:
        bit = size // left
        mine = (row // bit) & 1
        part = part.reshape(2 * left // 2, 2, lags, chans)
        part = halve(part, 4 * bit, mine, BF16).reshape(2, left // 2, lags, chans)
        if left == size:
            part, guest = lax.optimization_barrier((part, guest))
        left //= 2
    return halve(part.reshape(1, 2, lags, chans), 2, pair, BF16).reshape(lags, chans), guest


def links(seg_ids, place):
    own = lax.dynamic_index_in_dim(seg_ids, place, 0, False)
    prior = lax.dynamic_index_in_dim(seg_ids, jnp.maximum(place - 1, 0), 0, False)
    return (place > 0) & (own == prior)


def gathered_products(gated, cotangent, w_out):
    weights = lax.all_gather(w_out, "seq", axis=0, tiled=True)
    grad_gated = lax.dot_general(cotangent, weights, (((1,), (1,)), ((), ())), preferred_element_type=F32)
    grad_gated = lax.psum_scatter(grad_gated, "tp", scatter_dimension=1, tiled=True).astype(BF16)
    outputs = jnp.dot(
        lax.all_gather(gated, "tp", axis=1, tiled=True), weights, preferred_element_type=F32
    ).astype(BF16)
    return grad_gated, outputs


def ring_place(step, size):
    half = (size + 1) // 2
    return jnp.where(step < half, 2 * step, 2 * (size - 1 - step) + 1)


def ring_step(row, size):
    return jnp.where(row & 1 == 0, row >> 1, size - 1 - (row >> 1))


def products_kernel(count, last, scalars, cot_own, cot_away, gated_own, gated_away, *refs):
    pieces, refs = refs[: 4 * count], refs[4 * count :]
    before, refs = (refs[:1], refs[1:]) if last else ((), refs)
    grad_own, grad_away, *outs, grad = refs
    rows = cot_own.shape[0]

    @pl.when(pl.program_id(0) == 0)
    def _():
        grad[...] = jnp.zeros_like(grad)

    def add(order):
        cot = jnp.concatenate([cot_own[...], cot_away[...]], 0)
        total = before[0][...] if last else None
        for s in range(count):
            block = jnp.concatenate([pieces[4 * s + k][...] for k in order], 0)
            grad[s] += lax.dot_general(cot, block, (((1,), (1,)), ((), ())), preferred_element_type=F32)
            left = jnp.concatenate([gated_own[scalars[1 + s]], gated_away[scalars[1 + s]]], 0)
            part = jnp.dot(left, block, preferred_element_type=F32)
            total = part if total is None else total + part
        if last:
            outs[0][...] = total[:rows]
            outs[1][...] = total[rows:].astype(BF16)
        else:
            outs[0][...] = total

    @pl.when(scalars[0] == 0)
    def _():
        add((0, 1, 2, 3))

    @pl.when(scalars[0] != 0)
    def _():
        add((2, 3, 0, 1))

    @pl.when(pl.program_id(0) == pl.num_programs(0) - 1)
    def _():
        for s in range(count):
            grad_own[s] = grad[s, :rows].astype(BF16)
            grad_away[s] = grad[s, rows:].astype(BF16)


def products(scalars, cot_own, cot_away, gated_own, gated_away, groups, before=None):
    rows, feats = cot_own.shape
    width = gated_own.shape[2]
    count = len(groups)
    pieces = [p for group in groups for p in group]
    depth = pieces[0].shape[0]
    tile = min(512, feats)
    last = before is not None
    block = pl.BlockSpec((rows, tile), lambda j, s: (0, j))
    double = pl.BlockSpec((2 * rows, tile), lambda j, s: (0, j))
    whole = pl.BlockSpec(gated_own.shape, lambda j, s: (0, 0, 0))
    part = pl.BlockSpec((count, rows, width), lambda j, s: (0, 0, 0))
    grad = (jax.ShapeDtypeStruct((count, rows, width), BF16), pltpu.HBM((count, rows, width), BF16))
    halves = (pltpu.HBM((rows, feats), F32), pltpu.HBM((rows, feats), BF16))
    return pl.pallas_call(
        functools.partial(products_kernel, count, last),
        out_shape=grad + (halves if last else (pltpu.HBM((2 * rows, feats), F32),)),
        grid_spec=pltpu.PrefetchScalarGridSpec(
            num_scalar_prefetch=1,
            grid=(feats // tile,),
            in_specs=[block] * 2
            + [whole] * 2
            + [pl.BlockSpec((depth, tile), lambda j, s: (0, j))] * len(pieces)
            + [double] * last,
            out_specs=(part, part) + ((block, block) if last else (double,)),
            scratch_shapes=[pltpu.VMEM((count, 2 * rows, width), F32)],
        ),
        compiler_params=pltpu.CompilerParams(vmem_limit_bytes=28 << 20),
        cost_estimate=pl.CostEstimate(
            flops=8 * rows * depth * len(pieces) * feats,
            bytes_accessed=2 * depth * len(pieces) * feats + 12 * rows * feats,
            transcendentals=0,
        ),
    )(
        scalars,
        *[
            pltpu.with_memory_space_constraint(a, pltpu.HBM)
            for a in (cot_own, cot_away, gated_own, gated_away, *pieces, *([before] if last else []))
        ],
    )


def merge_kernel(scalars, *refs):
    out = refs[-1]
    at = 1
    for own, away in zip(refs[:-1:2], refs[1:-1:2]):
        count, _, width = own.shape
        for i in range(count):
            for ref, side in ((own, scalars[0]), (away, 1 - scalars[0])):
                out[:, pl.ds(pl.multiple_of((2 * scalars[at] + side) * width, width), width)] = ref[i]
            at += 1


def merge(scalars, pairs, chans):
    rows = pairs[0].shape[1]
    vmem = pl.BlockSpec(memory_space=pltpu.VMEM)
    return pl.pallas_call(
        merge_kernel,
        out_shape=jax.ShapeDtypeStruct((rows, chans), BF16),
        in_specs=[pl.BlockSpec(memory_space=pltpu.SMEM)] + [vmem] * len(pairs),
        out_specs=vmem,
        compiler_params=pltpu.CompilerParams(vmem_limit_bytes=GRANT),
        cost_estimate=pl.CostEstimate(flops=0, bytes_accessed=4 * rows * chans, transcendentals=0),
    )(scalars, *pairs)


def on_ring(queries, keys, values, w_out, taps, seg_ids, cotangent):
    rows, chans = queries.shape
    length = rows
    nseq = lax.axis_size("seq")
    place = lax.axis_index("seq")
    size = nseq // 4
    core, pair, row = [i.astype(jnp.int32) for i in (place & 1, (place >> 1) & 1, place >> 2)]
    at = ring_step(row, size)
    swap_core = [(i, i ^ 1) for i in range(nseq)]
    swap_pair = [(i, i ^ 2) for i in range(nseq)]
    walk = list(range(0, size, 2)) + list(range(1, size, 2))[::-1]
    onward = [(4 * walk[i] + k, 4 * walk[(i + 1) % size] + k) for i in range(size) for k in range(4)]
    behind = [(b, a) for a, b in onward]
    later = [(i, i + 1) for i in range(nseq - 1)]
    earlier = [(i + 1, i) for i in range(nseq - 1)]
    send = functools.partial(lax.ppermute, axis_name="seq")
    tie = lax.optimization_barrier
    linked = links(seg_ids, place)
    table, high, low = spectrum_table(length)
    table_now, high_now, low_now = table[:, length:], high[:, length:], low[:, length:]
    scale = 1.0 / length

    half = rows // 2
    first, second = w_out[:half], w_out[half:]
    swapped = send(w_out, perm=swap_core)
    cot_away = send(cotangent, perm=swap_pair)
    product, cot_away = tie((mul(keys, values), cot_away))
    before = send(product, perm=later)
    filt = forward_dft(high_now, low_now, tie(taps.T), ((1,), (0,)))

    firsts, seconds = [(first, swapped[:half])], [(second, swapped[half:])]
    block = [ring_place(lax.rem(at - s + size, size), size) for s in range(size)]
    ready = [max(s, size - s) if s else 0 for s in range(size)]
    early = [s for s in range(size) if ready[s] <= size - 3]
    late = [s for s in range(size) if ready[s] > size - 3]

    def products_of(sets, before):
        groups = []
        for s in sets:
            m = (size - s) % size
            groups.append((firsts[s][0], seconds[m][0], firsts[s][1], seconds[m][1]))
        scalars = jnp.stack([core] + [block[s] for s in sets])
        grad_own, grad_away, *sums = products(scalars, cotangent, cot_away, gated_own, gated_away, groups, before)
        return grad_own, send(grad_away, perm=swap_pair), sums

    for step in range(1, size):
        first, second = send(first, perm=onward), send(second, perm=behind)
        swap = (first, second)
        if step == 1:
            *swap, filt = tie((*swap, filt))
        if step == 3:
            before = jnp.where(linked, before, jnp.zeros_like(before))
            data = forward_dft(high, low, jnp.concatenate([before, product], 0), ((1,), (0,)))
            filtered = inverse_dft(table_now, times(filt, data), scale).astype(BF16)
            gated = mul(queries, filtered)
            gated_own, gated_away = deal(pair, gated, chans // (2 * size))
            *swap, gated_own, gated_away = tie((*swap, gated_own, gated_away))
            gated_away = send(gated_away, perm=swap_pair)
        if step == size - 1:
            grad_own, grad_away, sums = products_of(early, None)
            *swap, grad_own, sums[0] = tie((*swap, grad_own, sums[0]))
        firsts.append((first, send(swap[0], perm=swap_core)))
        seconds.append((second, send(swap[1], perm=swap_core)))
    grad_away, sums[0] = tie((grad_away, sums[0]))
    late_own, late_away, (out_own, out_away) = products_of(late, sums[0])
    grad_gated = merge(
        jnp.stack([pair] + [block[s] for s in early + late]), (grad_own, grad_away, late_own, late_away), chans
    )
    out_away = send(out_away, perm=swap_pair)
    grad_queries = mul(grad_gated, filtered)
    grad_filtered = mul(grad_gated, queries)
    grads = forward_dft(high_now, low_now, grad_filtered, ((1,), (0,)))
    back = inverse_dft(table, times_conj(grads, filt), scale)
    across = jnp.where(linked, back[:length], 0.0).astype(BF16)
    ahead = send(across, perm=earlier)
    taps_part = inverse_dft(table_now, times_conj(grads, data), scale)
    taps_grad, out_away = sum_over_ring(taps_part, nseq, place, out_away)
    taps_grad = taps_grad.T
    outputs = (out_own + out_away.astype(F32)).astype(BF16)
    grad_product = (back[length:] + ahead.astype(F32)).astype(BF16)
    grad_keys = mul(grad_product, values)
    grad_values = mul(grad_product, keys)
    return (outputs, grad_queries, grad_keys, grad_values, taps_grad)


def on_device(queries, keys, values, w_out, taps, seg_ids, cotangent):
    rows, chans = queries.shape
    length = taps.shape[1]
    assert rows == length
    nseq = lax.axis_size("seq")
    place = lax.axis_index("seq")
    table, high, low = spectrum_table(length)
    table_now, high_now, low_now = table[:, length:], high[:, length:], low[:, length:]
    scale = 1.0 / length
    later = [(i, i + 1) for i in range(nseq - 1)]
    earlier = [(i + 1, i) for i in range(nseq - 1)]
    linked = links(seg_ids, place)

    product = mul(keys, values)
    before = lax.ppermute(product, "seq", later)
    before = jnp.where(linked, before, jnp.zeros_like(before))
    data = forward_dft(high, low, jnp.concatenate([before, product], 0), ((1,), (0,)))
    filt = forward_dft(high_now, low_now, taps, ((1,), (1,)))
    filtered = inverse_dft(table_now, times(filt, data), scale).astype(BF16)
    gated = mul(queries, filtered)

    grad_gated, outputs = gathered_products(gated, cotangent, w_out)
    grad_queries = mul(grad_gated, filtered)
    grad_filtered = mul(grad_gated, queries)
    grads = forward_dft(high_now, low_now, grad_filtered, ((1,), (0,)))
    back = inverse_dft(table, times_conj(grads, filt), scale)
    across = jnp.where(linked, back[:length], 0.0).astype(BF16)
    ahead = lax.ppermute(across, "seq", earlier)
    taps_part = inverse_dft(table_now, times_conj(grads, data), scale)
    taps_grad = scatter_sum(taps_part, nseq, place, ()).T
    grad_product = (back[length:] + ahead.astype(F32)).astype(BF16)
    grad_keys = mul(grad_product, values)
    grad_values = mul(grad_product, keys)
    return (outputs, grad_queries, grad_keys, grad_values, taps_grad)


def solution(mesh):
    block = P("seq", "tp")
    count = mesh.shape["seq"]
    ring = mesh.shape["tp"] == 1 and count & (count - 1) == 0 and count >= 16

    def run(queries, keys, values, w_out, taps, seg_ids, cotangent):
        rows, chans = queries.shape
        place = on_ring if ring and rows * count == chans else on_device
        return place(queries, keys, values, w_out, taps, seg_ids, cotangent)

    return jax.shard_map(
        run,
        mesh=mesh,
        in_specs=(block, block, block, block, P("tp", None), P(), block),
        out_specs=(block, block, block, block, P(("tp", "seq"), None)),
        check_vma=False,
    )
```

```python
import functools

import jax
import jax.numpy as jnp
import numpy as np
from jax import lax
from jax.experimental import pallas as pl
from jax.experimental.pallas import tpu as pltpu
from jax.sharding import PartitionSpec as P

F32 = jnp.float32
BF16 = jnp.bfloat16
GRANT = 16 << 20
CHUNKS = 4


def spectrum_table(length):
    angles = np.pi * (2 * np.arange(length)[:, None] + 1) * np.arange(-length, length)[None, :] / (2 * length)
    table = np.concatenate([np.cos(angles), -np.sin(angles)], 0).astype(np.float32)
    high = table.astype(BF16)
    low = (table - high.astype(np.float32)).astype(BF16)
    return table, high, low


def forward_dft(high, low, data, dims):
    first = lax.dot_general(high, data, (dims, ((), ())), preferred_element_type=F32)
    second = lax.dot_general(low, data, (dims, ((), ())), preferred_element_type=F32)
    return first + second


def times(a, b):
    half = a.shape[0] // 2
    ar, ai, br, bi = a[:half], a[half:], b[:half], b[half:]
    return jnp.concatenate([ar * br - ai * bi, ar * bi + ai * br], 0)


def times_conj(a, b):
    half = a.shape[0] // 2
    ar, ai, br, bi = a[:half], a[half:], b[:half], b[half:]
    return jnp.concatenate([ar * br + ai * bi, ai * br - ar * bi], 0)


def inverse_dft(table, spectrum, scale):
    done = lax.dot_general(
        table, spectrum, (((0,), (0,)), ((), ())), precision=lax.Precision.HIGH, preferred_element_type=F32
    )
    return done * scale


def mul(a, b):
    return (a.astype(F32) * b.astype(F32)).astype(BF16)


def pick(data, width, side):
    blocks = [data[:, i : i + width] for i in range(0, data.shape[1], width)]
    return jnp.concatenate([jnp.where(side == 0, a, b) for a, b in zip(blocks[::2], blocks[1::2])], 1)


def scatter_sum(part, nseq, place, order):
    share = part.shape[1] // nseq
    bits = nseq.bit_length() - 1
    if nseq != 1 << bits:
        return lax.psum_scatter(part, "seq", scatter_dimension=1, tiled=True)
    left = list(range(bits))
    for step in [b for b in order if b < bits] + [b for b in range(bits) if b not in order]:
        width = share << sum(b < step for b in left)
        left.remove(step)
        mine = (place >> step) & 1
        away = pick(part, width, 1 - mine)
        if step:
            away = away.astype(BF16)
        away = lax.ppermute(away, "seq", [(i, i ^ (1 << step)) for i in range(nseq)])
        part = pick(part, width, mine) + away.astype(F32)
    return part


def deal_kernel(sides, scalars, data, kept, away):
    width = kept.shape[-1]
    for i in range(data.shape[1] // (2 * width)):
        for ref, side in ((kept, scalars[0]), (away, 1 - scalars[0])):
            block = data[:, pl.ds(pl.multiple_of((2 * i + side) * width, width), width)]
            if sides:
                ref[i % sides, i // sides] = block
            else:
                ref[i] = block


def deal(side, data, width, sides=0):
    rows, chans = data.shape
    count = chans // (2 * width)
    lead = (sides, count // sides) if sides else (count,)
    out = jax.ShapeDtypeStruct(lead + (rows, width), data.dtype)
    vmem = pl.BlockSpec(memory_space=pltpu.VMEM)
    return pl.pallas_call(
        functools.partial(deal_kernel, sides),
        out_shape=(out, out),
        in_specs=[pl.BlockSpec(memory_space=pltpu.SMEM), vmem],
        out_specs=(vmem, vmem),
        compiler_params=pltpu.CompilerParams(vmem_limit_bytes=GRANT),
        cost_estimate=pl.CostEstimate(flops=0, bytes_accessed=8 * rows * chans, transcendentals=0),
    )(side.reshape(1), data)


def sum_over_ring(part, nseq, place, guests):
    core, pair, row = place & 1, (place >> 1) & 1, place >> 2
    lags, chans = part.shape
    size, chans = nseq // 4, chans // nseq

    def halve(part, bit, mine, kind):
        away = lax.dynamic_index_in_dim(part, 1 - mine, 1, False).astype(kind)
        away = lax.ppermute(away, "seq", [(i, i ^ bit) for i in range(nseq)])
        return lax.dynamic_index_in_dim(part, mine, 1, False) + away.astype(F32)

    kept, away = deal(core.astype(jnp.int32), part, chans, 2)
    part = kept + lax.ppermute(away, "seq", [(i, i ^ 1) for i in range(nseq)])
    part = part.reshape(2, size, lags, chans)
    left, done = size, 0
    while left > 1:
        bit = size // left
        mine = (row // bit) & 1
        if done < len(guests) - 1:
            part, guests[done] = lax.optimization_barrier((part, guests[done]))
            done += 1
        part = part.reshape(2 * left // 2, 2, lags, chans)
        part = halve(part, 4 * bit, mine, BF16).reshape(2, left // 2, lags, chans)
        left //= 2
    return halve(part.reshape(1, 2, lags, chans), 2, pair, BF16).reshape(lags, chans), guests


def links(seg_ids, place):
    own = lax.dynamic_index_in_dim(seg_ids, place, 0, False)
    prior = lax.dynamic_index_in_dim(seg_ids, jnp.maximum(place - 1, 0), 0, False)
    return (place > 0) & (own == prior)


def gathered_products(gated, cotangent, w_out):
    weights = lax.all_gather(w_out, "seq", axis=0, tiled=True)
    grad_gated = lax.dot_general(cotangent, weights, (((1,), (1,)), ((), ())), preferred_element_type=F32)
    grad_gated = lax.psum_scatter(grad_gated, "tp", scatter_dimension=1, tiled=True).astype(BF16)
    outputs = jnp.dot(
        lax.all_gather(gated, "tp", axis=1, tiled=True), weights, preferred_element_type=F32
    ).astype(BF16)
    return grad_gated, outputs


def ring_place(step, size):
    half = (size + 1) // 2
    return jnp.where(step < half, 2 * step, 2 * (size - 1 - step) + 1)


def ring_step(row, size):
    return jnp.where(row & 1 == 0, row >> 1, size - 1 - (row >> 1))


def stacked(pieces, size, order):
    rows = []
    for s in range(size):
        m = (size - s) % size
        block = (pieces[4 * s], pieces[4 * m + 2], pieces[4 * s + 1], pieces[4 * m + 3])
        rows += [block[k][...] for k in order]
    return jnp.concatenate(rows, 0)


def grad_kernel(size, scalars, cot_own, cot_away, *refs):
    pieces, (grad_own, grad_away, grad) = refs[: 4 * size], refs[4 * size :]
    rows = cot_own.shape[0]
    width = grad_own.shape[2]

    @pl.when(pl.program_id(0) == 0)
    def _():
        grad[...] = jnp.zeros_like(grad)

    def add(order):
        cot = jnp.concatenate([cot_own[...], cot_away[...]], 0)
        dims = (((1,), (1,)), ((), ()))
        grad[...] += lax.dot_general(cot, stacked(pieces, size, order), dims, preferred_element_type=F32)

    @pl.when(scalars[0] == 0)
    def _():
        add((0, 1, 2, 3))

    @pl.when(scalars[0] != 0)
    def _():
        add((2, 3, 0, 1))

    @pl.when(pl.program_id(0) == pl.num_programs(0) - 1)
    def _():
        for s in range(size):
            block = grad[:, s * width : (s + 1) * width].astype(BF16)
            grad_own[scalars[1 + s]] = block[:rows]
            grad_away[scalars[1 + s]] = block[rows:]


def output_kernel(size, scalars, gated_own, gated_away, *refs):
    pieces, (out_own, *out_away, left) = refs[: 4 * size], refs[4 * size :]
    rows = out_own.shape[0]
    width = gated_own.shape[2]
    run = pl.num_programs(0) // len(out_away)

    @pl.when(pl.program_id(0) == 0)
    def _():
        for s in range(size):
            left[:rows, s * width : (s + 1) * width] = gated_own[scalars[1 + s]]
            left[rows:, s * width : (s + 1) * width] = gated_away[scalars[1 + s]]

    def add(order):
        total = jnp.dot(left[...], stacked(pieces, size, order), preferred_element_type=F32)
        out_own[...] = total[:rows]
        for k, ref in enumerate(out_away):

            @pl.when(pl.program_id(0) // run == k)
            def _(ref=ref):
                ref[...] = total[rows:].astype(BF16)

    @pl.when(scalars[0] == 0)
    def _():
        add((0, 1, 2, 3))

    @pl.when(scalars[0] != 0)
    def _():
        add((2, 3, 0, 1))


def far(arrays):
    return [pltpu.with_memory_space_constraint(a, pltpu.HBM) for a in arrays]


def grad_of_gated(scalars, cot_own, cot_away, pieces):
    rows, feats = cot_own.shape
    size, depth = len(pieces) // 4, pieces[0].shape[0]
    tile = min(512, feats)
    out = (size, rows, 4 * depth)
    whole = pl.BlockSpec(out, lambda j, s: (0, 0, 0))
    return pl.pallas_call(
        functools.partial(grad_kernel, size),
        out_shape=(jax.ShapeDtypeStruct(out, BF16), pltpu.HBM(out, BF16)),
        grid_spec=pltpu.PrefetchScalarGridSpec(
            num_scalar_prefetch=1,
            grid=(feats // tile,),
            in_specs=[pl.BlockSpec((rows, tile), lambda j, s: (0, j))] * 2
            + [pl.BlockSpec((depth, tile), lambda j, s: (0, j))] * len(pieces),
            out_specs=(whole, whole),
            scratch_shapes=[pltpu.VMEM((2 * rows, 4 * depth * size), F32)],
        ),
        compiler_params=pltpu.CompilerParams(vmem_limit_bytes=28 << 20),
        cost_estimate=pl.CostEstimate(
            flops=4 * rows * depth * len(pieces) * feats,
            bytes_accessed=2 * depth * len(pieces) * feats + 4 * rows * feats,
            transcendentals=0,
        ),
    )(scalars, *far([cot_own, cot_away, *pieces]))


def output_of(scalars, gated_own, gated_away, pieces):
    size, rows, width = gated_own.shape
    depth, feats = pieces[0].shape
    tile = min(512, feats // CHUNKS)
    run = feats // CHUNKS // tile
    block = pl.BlockSpec((rows, tile), lambda j, s: (0, j))

    def chunk(k):
        return pl.BlockSpec((rows, tile), lambda j, s: (0, jnp.clip(j - k * run, 0, run - 1)))

    return pl.pallas_call(
        functools.partial(output_kernel, size),
        out_shape=(pltpu.HBM((rows, feats), F32),) + (pltpu.HBM((rows, feats // CHUNKS), BF16),) * CHUNKS,
        grid_spec=pltpu.PrefetchScalarGridSpec(
            num_scalar_prefetch=1,
            grid=(feats // tile,),
            in_specs=[pl.BlockSpec(gated_own.shape, lambda j, s: (0, 0, 0))] * 2
            + [pl.BlockSpec((depth, tile), lambda j, s: (0, j))] * len(pieces),
            out_specs=(block,) + tuple(chunk(k) for k in range(CHUNKS)),
            scratch_shapes=[pltpu.VMEM((2 * rows, size * width), BF16)],
        ),
        compiler_params=pltpu.CompilerParams(vmem_limit_bytes=28 << 20),
        cost_estimate=pl.CostEstimate(
            flops=4 * rows * depth * len(pieces) * feats,
            bytes_accessed=2 * depth * len(pieces) * feats + 6 * rows * feats,
            transcendentals=0,
        ),
    )(scalars, *far([gated_own, gated_away, *pieces]))


def merge_kernel(scalars, own, away, out):
    size, _, width = own.shape
    for r in range(size):
        for ref, side in ((own, scalars[0]), (away, 1 - scalars[0])):
            out[:, pl.ds(pl.multiple_of((2 * r + side) * width, width), width)] = ref[r]


def merge(side, own, away):
    size, rows, width = own.shape
    vmem = pl.BlockSpec(memory_space=pltpu.VMEM)
    return pl.pallas_call(
        merge_kernel,
        out_shape=jax.ShapeDtypeStruct((rows, 2 * size * width), own.dtype),
        in_specs=[pl.BlockSpec(memory_space=pltpu.SMEM), vmem, vmem],
        out_specs=vmem,
        compiler_params=pltpu.CompilerParams(vmem_limit_bytes=GRANT),
        cost_estimate=pl.CostEstimate(flops=0, bytes_accessed=8 * own.size, transcendentals=0),
    )(side.reshape(1), own, away)


def on_ring(queries, keys, values, w_out, taps, seg_ids, cotangent):
    rows, chans = queries.shape
    length = rows
    nseq = lax.axis_size("seq")
    place = lax.axis_index("seq")
    size = nseq // 4
    core, pair, row = [i.astype(jnp.int32) for i in (place & 1, (place >> 1) & 1, place >> 2)]
    at = ring_step(row, size)
    swap_core = [(i, i ^ 1) for i in range(nseq)]
    swap_pair = [(i, i ^ 2) for i in range(nseq)]
    walk = list(range(0, size, 2)) + list(range(1, size, 2))[::-1]
    onward = [(4 * walk[i] + k, 4 * walk[(i + 1) % size] + k) for i in range(size) for k in range(4)]
    behind = [(b, a) for a, b in onward]
    later = [(i, i + 1) for i in range(nseq - 1)]
    earlier = [(i + 1, i) for i in range(nseq - 1)]
    send = functools.partial(lax.ppermute, axis_name="seq")
    tie = lax.optimization_barrier
    linked = links(seg_ids, place)
    table, high, low = spectrum_table(length)
    table_now, high_now, low_now = table[:, length:], high[:, length:], low[:, length:]
    scale = 1.0 / length

    half = rows // 2
    first, second, cotangent, w_out = tie((w_out[:half], w_out[half:], cotangent, w_out))
    swapped = send(w_out, perm=swap_core)
    cot_away = send(cotangent, perm=swap_pair)
    product, cot_away = tie((mul(keys, values), cot_away))
    before = send(product, perm=later)
    filt = forward_dft(high_now, low_now, tie(taps.T), ((1,), (0,)))

    pieces = [first, swapped[:half], second, swapped[half:]]
    for step in range(1, size):
        first, second = send(first, perm=onward), send(second, perm=behind)
        swap = (first, second)
        if step == 1:
            *swap, filt = tie((*swap, filt))
        if step == 3:
            before = jnp.where(linked, before, jnp.zeros_like(before))
            data = forward_dft(high, low, jnp.concatenate([before, product], 0), ((1,), (0,)))
            filtered = inverse_dft(table_now, times(filt, data), scale).astype(BF16)
            gated = mul(queries, filtered)
            gated_own, gated_away = deal(pair, gated, chans // (2 * size))
            *swap, gated_own, gated_away = tie((*swap, gated_own, gated_away))
            gated_away = send(gated_away, perm=swap_pair)
        if step == max(size - 2, 3):
            *swap, gated_away = tie((*swap, gated_away))
        pieces += [first, send(swap[0], perm=swap_core), second, send(swap[1], perm=swap_core)]
    places = [core] + [ring_place(lax.rem(at - s + size, size), size) for s in range(size)]
    scalars = jnp.stack(places)
    grad_own, grad_away = grad_of_gated(scalars, cotangent, cot_away, pieces)
    grad_away = send(grad_away, perm=swap_pair)
    out_own, *out_away = output_of(scalars, gated_own, gated_away, pieces)
    grad_away, out_own, out_away = tie((grad_away, out_own, out_away))
    grad_gated = merge(pair, grad_own, grad_away)
    out_away = [send(chunk, perm=swap_pair) for chunk in out_away]
    grad_queries = mul(grad_gated, filtered)
    grad_filtered = mul(grad_gated, queries)
    grads = forward_dft(high_now, low_now, grad_filtered, ((1,), (0,)))
    filt, out_away[0] = tie((filt, out_away[0]))
    back = inverse_dft(table, times_conj(grads, filt), scale)
    across = jnp.where(linked, back[:length], 0.0).astype(BF16)
    ahead = send(across, perm=earlier)
    taps_part = inverse_dft(table_now, times_conj(grads, data), scale)
    taps_grad, out_away[1:] = sum_over_ring(taps_part, nseq, place, out_away[1:])
    taps_grad = taps_grad.T
    outputs = (out_own + jnp.concatenate(out_away, 1).astype(F32)).astype(BF16)
    grad_product = (back[length:] + ahead.astype(F32)).astype(BF16)
    grad_keys = mul(grad_product, values)
    grad_values = mul(grad_product, keys)
    return (outputs, grad_queries, grad_keys, grad_values, taps_grad)


def on_device(queries, keys, values, w_out, taps, seg_ids, cotangent):
    rows, chans = queries.shape
    length = taps.shape[1]
    assert rows == length
    nseq = lax.axis_size("seq")
    place = lax.axis_index("seq")
    table, high, low = spectrum_table(length)
    table_now, high_now, low_now = table[:, length:], high[:, length:], low[:, length:]
    scale = 1.0 / length
    later = [(i, i + 1) for i in range(nseq - 1)]
    earlier = [(i + 1, i) for i in range(nseq - 1)]
    linked = links(seg_ids, place)

    product = mul(keys, values)
    before = lax.ppermute(product, "seq", later)
    before = jnp.where(linked, before, jnp.zeros_like(before))
    data = forward_dft(high, low, jnp.concatenate([before, product], 0), ((1,), (0,)))
    filt = forward_dft(high_now, low_now, taps, ((1,), (1,)))
    filtered = inverse_dft(table_now, times(filt, data), scale).astype(BF16)
    gated = mul(queries, filtered)

    grad_gated, outputs = gathered_products(gated, cotangent, w_out)
    grad_queries = mul(grad_gated, filtered)
    grad_filtered = mul(grad_gated, queries)
    grads = forward_dft(high_now, low_now, grad_filtered, ((1,), (0,)))
    back = inverse_dft(table, times_conj(grads, filt), scale)
    across = jnp.where(linked, back[:length], 0.0).astype(BF16)
    ahead = lax.ppermute(across, "seq", earlier)
    taps_part = inverse_dft(table_now, times_conj(grads, data), scale)
    taps_grad = scatter_sum(taps_part, nseq, place, ()).T
    grad_product = (back[length:] + ahead.astype(F32)).astype(BF16)
    grad_keys = mul(grad_product, values)
    grad_values = mul(grad_product, keys)
    return (outputs, grad_queries, grad_keys, grad_values, taps_grad)


def solution(mesh):
    block = P("seq", "tp")
    count = mesh.shape["seq"]
    ring = mesh.shape["tp"] == 1 and count & (count - 1) == 0 and count >= 16

    def run(queries, keys, values, w_out, taps, seg_ids, cotangent):
        rows, chans = queries.shape
        place = on_ring if ring and rows * count == chans else on_device
        return place(queries, keys, values, w_out, taps, seg_ids, cotangent)

    return jax.shard_map(
        run,
        mesh=mesh,
        in_specs=(block, block, block, block, P("tp", None), P(), block),
        out_specs=(block, block, block, block, P(("tp", "seq"), None)),
        check_vma=False,
    )
```

```python
import functools

import jax
import jax.numpy as jnp
import numpy as np
from jax import lax
from jax.experimental import pallas as pl
from jax.experimental.pallas import tpu as pltpu
from jax.sharding import PartitionSpec as P

F32 = jnp.float32
BF16 = jnp.bfloat16
GRANT = 16 << 20
CHUNKS = 4


def spectrum_table(length):
    angles = np.pi * (2 * np.arange(length)[:, None] + 1) * np.arange(-length, length)[None, :] / (2 * length)
    table = np.concatenate([np.cos(angles), -np.sin(angles)], 0).astype(np.float32)
    high = table.astype(BF16)
    low = (table - high.astype(np.float32)).astype(BF16)
    return table, high, low


def forward_dft(high, low, data, dims):
    first = lax.dot_general(high, data, (dims, ((), ())), preferred_element_type=F32)
    second = lax.dot_general(low, data, (dims, ((), ())), preferred_element_type=F32)
    return first + second


def times(a, b):
    half = a.shape[0] // 2
    ar, ai, br, bi = a[:half], a[half:], b[:half], b[half:]
    return jnp.concatenate([ar * br - ai * bi, ar * bi + ai * br], 0)


def times_conj(a, b):
    half = a.shape[0] // 2
    ar, ai, br, bi = a[:half], a[half:], b[:half], b[half:]
    return jnp.concatenate([ar * br + ai * bi, ai * br - ar * bi], 0)


def inverse_dft(table, spectrum, scale):
    done = lax.dot_general(
        table, spectrum, (((0,), (0,)), ((), ())), precision=lax.Precision.HIGH, preferred_element_type=F32
    )
    return done * scale


def mul(a, b):
    return (a.astype(F32) * b.astype(F32)).astype(BF16)


def pick(data, width, side):
    blocks = [data[:, i : i + width] for i in range(0, data.shape[1], width)]
    return jnp.concatenate([jnp.where(side == 0, a, b) for a, b in zip(blocks[::2], blocks[1::2])], 1)


def scatter_sum(part, nseq, place, order):
    share = part.shape[1] // nseq
    bits = nseq.bit_length() - 1
    if nseq != 1 << bits:
        return lax.psum_scatter(part, "seq", scatter_dimension=1, tiled=True)
    left = list(range(bits))
    for step in [b for b in order if b < bits] + [b for b in range(bits) if b not in order]:
        width = share << sum(b < step for b in left)
        left.remove(step)
        mine = (place >> step) & 1
        away = pick(part, width, 1 - mine)
        if step:
            away = away.astype(BF16)
        away = lax.ppermute(away, "seq", [(i, i ^ (1 << step)) for i in range(nseq)])
        part = pick(part, width, mine) + away.astype(F32)
    return part


def deal_kernel(sides, scalars, data, kept, away):
    width = kept.shape[-1]
    for i in range(data.shape[1] // (2 * width)):
        for ref, side in ((kept, scalars[0]), (away, 1 - scalars[0])):
            block = data[:, pl.ds(pl.multiple_of((2 * i + side) * width, width), width)]
            if sides:
                ref[i % sides, i // sides] = block
            else:
                ref[i] = block


def deal(side, data, width, sides=0):
    rows, chans = data.shape
    count = chans // (2 * width)
    lead = (sides, count // sides) if sides else (count,)
    out = jax.ShapeDtypeStruct(lead + (rows, width), data.dtype)
    vmem = pl.BlockSpec(memory_space=pltpu.VMEM)
    return pl.pallas_call(
        functools.partial(deal_kernel, sides),
        out_shape=(out, out),
        in_specs=[pl.BlockSpec(memory_space=pltpu.SMEM), vmem],
        out_specs=(vmem, vmem),
        compiler_params=pltpu.CompilerParams(vmem_limit_bytes=GRANT),
        cost_estimate=pl.CostEstimate(flops=0, bytes_accessed=8 * rows * chans, transcendentals=0),
    )(side.reshape(1), data)


def sum_over_ring(part, nseq, place, guests):
    core, pair, row = place & 1, (place >> 1) & 1, place >> 2
    lags, chans = part.shape
    size, chans = nseq // 4, chans // nseq

    def halve(part, bit, mine, kind):
        away = lax.dynamic_index_in_dim(part, 1 - mine, 1, False).astype(kind)
        away = lax.ppermute(away, "seq", [(i, i ^ bit) for i in range(nseq)])
        return lax.dynamic_index_in_dim(part, mine, 1, False) + away.astype(F32)

    kept, away = deal(core.astype(jnp.int32), part, chans, 2)
    part = kept + lax.ppermute(away, "seq", [(i, i ^ 1) for i in range(nseq)])
    part = part.reshape(2, size, lags, chans)
    left, done = size, 0
    while left > 1:
        bit = size // left
        mine = (row // bit) & 1
        if done < len(guests) - 1:
            part, guests[done] = lax.optimization_barrier((part, guests[done]))
            done += 1
        part = part.reshape(2 * left // 2, 2, lags, chans)
        part = halve(part, 4 * bit, mine, BF16).reshape(2, left // 2, lags, chans)
        left //= 2
    return halve(part.reshape(1, 2, lags, chans), 2, pair, BF16).reshape(lags, chans), guests


def links(seg_ids, place):
    own = lax.dynamic_index_in_dim(seg_ids, place, 0, False)
    prior = lax.dynamic_index_in_dim(seg_ids, jnp.maximum(place - 1, 0), 0, False)
    return (place > 0) & (own == prior)


def gathered_products(gated, cotangent, w_out):
    weights = lax.all_gather(w_out, "seq", axis=0, tiled=True)
    grad_gated = lax.dot_general(cotangent, weights, (((1,), (1,)), ((), ())), preferred_element_type=F32)
    grad_gated = lax.psum_scatter(grad_gated, "tp", scatter_dimension=1, tiled=True).astype(BF16)
    outputs = jnp.dot(
        lax.all_gather(gated, "tp", axis=1, tiled=True), weights, preferred_element_type=F32
    ).astype(BF16)
    return grad_gated, outputs


def ring_place(step, size):
    half = (size + 1) // 2
    return jnp.where(step < half, 2 * step, 2 * (size - 1 - step) + 1)


def ring_step(row, size):
    return jnp.where(row & 1 == 0, row >> 1, size - 1 - (row >> 1))


def stacked(pieces, size, order):
    rows = []
    for s in range(size):
        m = (size - s) % size
        block = (pieces[4 * s], pieces[4 * m + 2], pieces[4 * s + 1], pieces[4 * m + 3])
        rows += [block[k][...] for k in order]
    return jnp.concatenate(rows, 0)


def grad_kernel(size, scalars, cot_own, cot_away, *refs):
    pieces, (grad_own, grad_away, grad) = refs[: 4 * size], refs[4 * size :]
    rows = cot_own.shape[0]
    width = grad_own.shape[2]

    @pl.when(pl.program_id(0) == 0)
    def _():
        grad[...] = jnp.zeros_like(grad)

    def add(order):
        cot = jnp.concatenate([cot_own[...], cot_away[...]], 0)
        dims = (((1,), (1,)), ((), ()))
        grad[...] += lax.dot_general(cot, stacked(pieces, size, order), dims, preferred_element_type=F32)

    @pl.when(scalars[0] == 0)
    def _():
        add((0, 1, 2, 3))

    @pl.when(scalars[0] != 0)
    def _():
        add((2, 3, 0, 1))

    @pl.when(pl.program_id(0) == pl.num_programs(0) - 1)
    def _():
        for s in range(size):
            block = grad[:, s * width : (s + 1) * width].astype(BF16)
            grad_own[scalars[1 + s]] = block[:rows]
            grad_away[scalars[1 + s]] = block[rows:]


def output_kernel(size, scalars, gated_own, gated_away, *refs):
    pieces, (out_own, *out_away, left) = refs[: 4 * size], refs[4 * size :]
    rows = out_own.shape[0]
    width = gated_own.shape[2]
    run = pl.num_programs(0) // len(out_away)

    @pl.when(pl.program_id(0) == 0)
    def _():
        for s in range(size):
            left[:rows, s * width : (s + 1) * width] = gated_own[scalars[1 + s]]
            left[rows:, s * width : (s + 1) * width] = gated_away[scalars[1 + s]]

    def add(order):
        total = jnp.dot(left[...], stacked(pieces, size, order), preferred_element_type=F32)
        out_own[...] = total[:rows]
        for k, ref in enumerate(out_away):

            @pl.when(pl.program_id(0) // run == k)
            def _(ref=ref):
                ref[...] = total[rows:].astype(BF16)

    @pl.when(scalars[0] == 0)
    def _():
        add((0, 1, 2, 3))

    @pl.when(scalars[0] != 0)
    def _():
        add((2, 3, 0, 1))


def far(arrays):
    return [pltpu.with_memory_space_constraint(a, pltpu.HBM) for a in arrays]


def grad_of_gated(scalars, cot_own, cot_away, pieces):
    rows, feats = cot_own.shape
    size, depth = len(pieces) // 4, pieces[0].shape[0]
    tile = min(1024, feats)
    out = (size, rows, 4 * depth)
    whole = pl.BlockSpec(out, lambda j, s: (0, 0, 0))
    return pl.pallas_call(
        functools.partial(grad_kernel, size),
        out_shape=(jax.ShapeDtypeStruct(out, BF16), pltpu.HBM(out, BF16)),
        grid_spec=pltpu.PrefetchScalarGridSpec(
            num_scalar_prefetch=1,
            grid=(feats // tile,),
            in_specs=[pl.BlockSpec((rows, tile), lambda j, s: (0, j))] * 2
            + [pl.BlockSpec((depth, tile), lambda j, s: (0, j))] * len(pieces),
            out_specs=(whole, whole),
            scratch_shapes=[pltpu.VMEM((2 * rows, 4 * depth * size), F32)],
        ),
        compiler_params=pltpu.CompilerParams(vmem_limit_bytes=28 << 20),
        cost_estimate=pl.CostEstimate(
            flops=4 * rows * depth * len(pieces) * feats,
            bytes_accessed=2 * depth * len(pieces) * feats + 4 * rows * feats,
            transcendentals=0,
        ),
    )(scalars, *far([cot_own, cot_away, *pieces]))


def output_of(scalars, gated_own, gated_away, pieces):
    size, rows, width = gated_own.shape
    depth, feats = pieces[0].shape
    tile = min(1024, feats // CHUNKS)
    run = feats // CHUNKS // tile
    block = pl.BlockSpec((rows, tile), lambda j, s: (0, j))

    def chunk(k):
        return pl.BlockSpec((rows, tile), lambda j, s: (0, jnp.clip(j - k * run, 0, run - 1)))

    return pl.pallas_call(
        functools.partial(output_kernel, size),
        out_shape=(pltpu.HBM((rows, feats), F32),) + (pltpu.HBM((rows, feats // CHUNKS), BF16),) * CHUNKS,
        grid_spec=pltpu.PrefetchScalarGridSpec(
            num_scalar_prefetch=1,
            grid=(feats // tile,),
            in_specs=[pl.BlockSpec(gated_own.shape, lambda j, s: (0, 0, 0))] * 2
            + [pl.BlockSpec((depth, tile), lambda j, s: (0, j))] * len(pieces),
            out_specs=(block,) + tuple(chunk(k) for k in range(CHUNKS)),
            scratch_shapes=[pltpu.VMEM((2 * rows, size * width), BF16)],
        ),
        compiler_params=pltpu.CompilerParams(vmem_limit_bytes=28 << 20),
        cost_estimate=pl.CostEstimate(
            flops=4 * rows * depth * len(pieces) * feats,
            bytes_accessed=2 * depth * len(pieces) * feats + 6 * rows * feats,
            transcendentals=0,
        ),
    )(scalars, *far([gated_own, gated_away, *pieces]))


def merge_kernel(scalars, own, away, out):
    size, _, width = own.shape
    for r in range(size):
        for ref, side in ((own, scalars[0]), (away, 1 - scalars[0])):
            out[:, pl.ds(pl.multiple_of((2 * r + side) * width, width), width)] = ref[r]


def merge(side, own, away):
    size, rows, width = own.shape
    vmem = pl.BlockSpec(memory_space=pltpu.VMEM)
    return pl.pallas_call(
        merge_kernel,
        out_shape=jax.ShapeDtypeStruct((rows, 2 * size * width), own.dtype),
        in_specs=[pl.BlockSpec(memory_space=pltpu.SMEM), vmem, vmem],
        out_specs=vmem,
        compiler_params=pltpu.CompilerParams(vmem_limit_bytes=GRANT),
        cost_estimate=pl.CostEstimate(flops=0, bytes_accessed=8 * own.size, transcendentals=0),
    )(side.reshape(1), own, away)


def on_ring(queries, keys, values, w_out, taps, seg_ids, cotangent):
    rows, chans = queries.shape
    length = rows
    nseq = lax.axis_size("seq")
    place = lax.axis_index("seq")
    size = nseq // 4
    core, pair, row = [i.astype(jnp.int32) for i in (place & 1, (place >> 1) & 1, place >> 2)]
    at = ring_step(row, size)
    swap_core = [(i, i ^ 1) for i in range(nseq)]
    swap_pair = [(i, i ^ 2) for i in range(nseq)]
    walk = list(range(0, size, 2)) + list(range(1, size, 2))[::-1]
    onward = [(4 * walk[i] + k, 4 * walk[(i + 1) % size] + k) for i in range(size) for k in range(4)]
    behind = [(b, a) for a, b in onward]
    later = [(i, i + 1) for i in range(nseq - 1)]
    earlier = [(i + 1, i) for i in range(nseq - 1)]
    send = functools.partial(lax.ppermute, axis_name="seq")
    tie = lax.optimization_barrier
    linked = links(seg_ids, place)
    table, high, low = spectrum_table(length)
    table_now, high_now, low_now = table[:, length:], high[:, length:], low[:, length:]
    scale = 1.0 / length

    half = rows // 2
    first, second, cotangent, w_out = tie((w_out[:half], w_out[half:], cotangent, w_out))
    swapped = send(w_out, perm=swap_core)
    cot_away = send(cotangent, perm=swap_pair)
    product, cot_away = tie((mul(keys, values), cot_away))
    before = send(product, perm=later)
    filt = forward_dft(high_now, low_now, tie(taps.T), ((1,), (0,)))

    pieces = [first, swapped[:half], second, swapped[half:]]
    for step in range(1, size):
        first, second = send(first, perm=onward), send(second, perm=behind)
        swap = (first, second)
        if step == 1:
            *swap, filt = tie((*swap, filt))
        if step == 3:
            before = jnp.where(linked, before, jnp.zeros_like(before))
            data = forward_dft(high, low, jnp.concatenate([before, product], 0), ((1,), (0,)))
            filtered = inverse_dft(table_now, times(filt, data), scale).astype(BF16)
            gated = mul(queries, filtered)
            gated_own, gated_away = deal(pair, gated, chans // (2 * size))
            *swap, gated_own, gated_away = tie((*swap, gated_own, gated_away))
            gated_away = send(gated_away, perm=swap_pair)
        if step == max(size - 2, 3):
            *swap, gated_away = tie((*swap, gated_away))
        pieces += [first, send(swap[0], perm=swap_core), second, send(swap[1], perm=swap_core)]
    places = [core] + [ring_place(lax.rem(at - s + size, size), size) for s in range(size)]
    scalars = jnp.stack(places)
    grad_own, grad_away = grad_of_gated(scalars, cotangent, cot_away, pieces)
    grad_away = send(grad_away, perm=swap_pair)
    out_own, *out_away = output_of(scalars, gated_own, gated_away, pieces)
    grad_away, out_own, out_away = tie((grad_away, out_own, out_away))
    grad_gated = merge(pair, grad_own, grad_away)
    out_away = [send(chunk, perm=swap_pair) for chunk in out_away]
    grad_queries = mul(grad_gated, filtered)
    grad_filtered = mul(grad_gated, queries)
    grads = forward_dft(high_now, low_now, grad_filtered, ((1,), (0,)))
    filt, out_away[0] = tie((filt, out_away[0]))
    back = inverse_dft(table, times_conj(grads, filt), scale)
    across = jnp.where(linked, back[:length], 0.0).astype(BF16)
    taps_part = inverse_dft(table_now, times_conj(grads, data), scale)
    guests = [out_away[1], (out_away[2], across), out_away[3]]
    taps_grad, (out_away[1], (out_away[2], across), out_away[3]) = sum_over_ring(taps_part, nseq, place, guests)
    ahead = send(across, perm=earlier)
    taps_grad = taps_grad.T
    outputs = (out_own + jnp.concatenate(out_away, 1).astype(F32)).astype(BF16)
    grad_product = (back[length:] + ahead.astype(F32)).astype(BF16)
    grad_keys = mul(grad_product, values)
    grad_values = mul(grad_product, keys)
    return (outputs, grad_queries, grad_keys, grad_values, taps_grad)


def on_device(queries, keys, values, w_out, taps, seg_ids, cotangent):
    rows, chans = queries.shape
    length = taps.shape[1]
    assert rows == length
    nseq = lax.axis_size("seq")
    place = lax.axis_index("seq")
    table, high, low = spectrum_table(length)
    table_now, high_now, low_now = table[:, length:], high[:, length:], low[:, length:]
    scale = 1.0 / length
    later = [(i, i + 1) for i in range(nseq - 1)]
    earlier = [(i + 1, i) for i in range(nseq - 1)]
    linked = links(seg_ids, place)

    product = mul(keys, values)
    before = lax.ppermute(product, "seq", later)
    before = jnp.where(linked, before, jnp.zeros_like(before))
    data = forward_dft(high, low, jnp.concatenate([before, product], 0), ((1,), (0,)))
    filt = forward_dft(high_now, low_now, taps, ((1,), (1,)))
    filtered = inverse_dft(table_now, times(filt, data), scale).astype(BF16)
    gated = mul(queries, filtered)

    grad_gated, outputs = gathered_products(gated, cotangent, w_out)
    grad_queries = mul(grad_gated, filtered)
    grad_filtered = mul(grad_gated, queries)
    grads = forward_dft(high_now, low_now, grad_filtered, ((1,), (0,)))
    back = inverse_dft(table, times_conj(grads, filt), scale)
    across = jnp.where(linked, back[:length], 0.0).astype(BF16)
    ahead = lax.ppermute(across, "seq", earlier)
    taps_part = inverse_dft(table_now, times_conj(grads, data), scale)
    taps_grad = scatter_sum(taps_part, nseq, place, ()).T
    grad_product = (back[length:] + ahead.astype(F32)).astype(BF16)
    grad_keys = mul(grad_product, values)
    grad_values = mul(grad_product, keys)
    return (outputs, grad_queries, grad_keys, grad_values, taps_grad)


def solution(mesh):
    block = P("seq", "tp")
    count = mesh.shape["seq"]
    ring = mesh.shape["tp"] == 1 and count & (count - 1) == 0 and count >= 16

    def run(queries, keys, values, w_out, taps, seg_ids, cotangent):
        rows, chans = queries.shape
        place = on_ring if ring and rows * count == chans else on_device
        return place(queries, keys, values, w_out, taps, seg_ids, cotangent)

    return jax.shard_map(
        run,
        mesh=mesh,
        in_specs=(block, block, block, block, P("tp", None), P(), block),
        out_specs=(block, block, block, block, P(("tp", "seq"), None)),
        check_vma=False,
    )
```

```python
import functools

import jax
import jax.numpy as jnp
import numpy as np
from jax import lax
from jax.experimental import pallas as pl
from jax.experimental.pallas import tpu as pltpu
from jax.sharding import PartitionSpec as P

F32 = jnp.float32
BF16 = jnp.bfloat16
GRANT = 16 << 20
CHUNKS = 4


def spectrum_table(length):
    angles = np.pi * (2 * np.arange(length)[:, None] + 1) * np.arange(-length, length)[None, :] / (2 * length)
    table = np.concatenate([np.cos(angles), -np.sin(angles)], 0).astype(np.float32)
    high = table.astype(BF16)
    low = (table - high.astype(np.float32)).astype(BF16)
    return table, high, low


def forward_dft(high, low, data, dims):
    first = lax.dot_general(high, data, (dims, ((), ())), preferred_element_type=F32)
    second = lax.dot_general(low, data, (dims, ((), ())), preferred_element_type=F32)
    return first + second


def times(a, b):
    half = a.shape[0] // 2
    ar, ai, br, bi = a[:half], a[half:], b[:half], b[half:]
    return jnp.concatenate([ar * br - ai * bi, ar * bi + ai * br], 0)


def times_conj(a, b):
    half = a.shape[0] // 2
    ar, ai, br, bi = a[:half], a[half:], b[:half], b[half:]
    return jnp.concatenate([ar * br + ai * bi, ai * br - ar * bi], 0)


def inverse_dft(table, spectrum, scale):
    done = lax.dot_general(
        table, spectrum, (((0,), (0,)), ((), ())), precision=lax.Precision.HIGH, preferred_element_type=F32
    )
    return done * scale


def mul(a, b):
    return (a.astype(F32) * b.astype(F32)).astype(BF16)


def pick(data, width, side):
    blocks = [data[:, i : i + width] for i in range(0, data.shape[1], width)]
    return jnp.concatenate([jnp.where(side == 0, a, b) for a, b in zip(blocks[::2], blocks[1::2])], 1)


def scatter_sum(part, nseq, place, order):
    share = part.shape[1] // nseq
    bits = nseq.bit_length() - 1
    if nseq != 1 << bits:
        return lax.psum_scatter(part, "seq", scatter_dimension=1, tiled=True)
    left = list(range(bits))
    for step in [b for b in order if b < bits] + [b for b in range(bits) if b not in order]:
        width = share << sum(b < step for b in left)
        left.remove(step)
        mine = (place >> step) & 1
        away = pick(part, width, 1 - mine)
        if step:
            away = away.astype(BF16)
        away = lax.ppermute(away, "seq", [(i, i ^ (1 << step)) for i in range(nseq)])
        part = pick(part, width, mine) + away.astype(F32)
    return part


def deal_kernel(sides, scalars, data, kept, away):
    width = kept.shape[-1]
    for i in range(data.shape[1] // (2 * width)):
        for ref, side in ((kept, scalars[0]), (away, 1 - scalars[0])):
            block = data[:, pl.ds(pl.multiple_of((2 * i + side) * width, width), width)]
            if sides:
                ref[i % sides, i // sides] = block
            else:
                ref[i] = block


def deal(side, data, width, sides=0):
    rows, chans = data.shape
    count = chans // (2 * width)
    lead = (sides, count // sides) if sides else (count,)
    out = jax.ShapeDtypeStruct(lead + (rows, width), data.dtype)
    vmem = pl.BlockSpec(memory_space=pltpu.VMEM)
    return pl.pallas_call(
        functools.partial(deal_kernel, sides),
        out_shape=(out, out),
        in_specs=[pl.BlockSpec(memory_space=pltpu.SMEM), vmem],
        out_specs=(vmem, vmem),
        compiler_params=pltpu.CompilerParams(vmem_limit_bytes=GRANT),
        cost_estimate=pl.CostEstimate(flops=0, bytes_accessed=8 * rows * chans, transcendentals=0),
    )(side.reshape(1), data)


def sum_over_ring(part, nseq, place, guests):
    core, pair, row = place & 1, (place >> 1) & 1, place >> 2
    lags, chans = part.shape
    size, chans = nseq // 4, chans // nseq

    def halve(part, bit, mine, kind):
        away = lax.dynamic_index_in_dim(part, 1 - mine, 1, False).astype(kind)
        away = lax.ppermute(away, "seq", [(i, i ^ bit) for i in range(nseq)])
        return lax.dynamic_index_in_dim(part, mine, 1, False) + away.astype(F32)

    kept, away = deal(core.astype(jnp.int32), part, chans, 2)
    part = kept + lax.ppermute(away, "seq", [(i, i ^ 1) for i in range(nseq)])
    part = part.reshape(2, size, lags, chans)
    left, done = size, 0
    while left > 1:
        bit = size // left
        mine = (row // bit) & 1
        if done < len(guests) - 1:
            part, guests[done] = lax.optimization_barrier((part, guests[done]))
            done += 1
        part = part.reshape(2 * left // 2, 2, lags, chans)
        part = halve(part, 4 * bit, mine, BF16).reshape(2, left // 2, lags, chans)
        left //= 2
    return halve(part.reshape(1, 2, lags, chans), 2, pair, BF16).reshape(lags, chans), guests


def links(seg_ids, place):
    own = lax.dynamic_index_in_dim(seg_ids, place, 0, False)
    prior = lax.dynamic_index_in_dim(seg_ids, jnp.maximum(place - 1, 0), 0, False)
    return (place > 0) & (own == prior)


def gathered_products(gated, cotangent, w_out):
    weights = lax.all_gather(w_out, "seq", axis=0, tiled=True)
    grad_gated = lax.dot_general(cotangent, weights, (((1,), (1,)), ((), ())), preferred_element_type=F32)
    grad_gated = lax.psum_scatter(grad_gated, "tp", scatter_dimension=1, tiled=True).astype(BF16)
    outputs = jnp.dot(
        lax.all_gather(gated, "tp", axis=1, tiled=True), weights, preferred_element_type=F32
    ).astype(BF16)
    return grad_gated, outputs


def ring_place(step, size):
    half = (size + 1) // 2
    return jnp.where(step < half, 2 * step, 2 * (size - 1 - step) + 1)


def ring_step(row, size):
    return jnp.where(row & 1 == 0, row >> 1, size - 1 - (row >> 1))


def stacked(pieces, size, order):
    rows = []
    for s in range(size):
        m = (size - s) % size
        block = (pieces[4 * s], pieces[4 * m + 2], pieces[4 * s + 1], pieces[4 * m + 3])
        rows += [block[k][...] for k in order]
    return jnp.concatenate(rows, 0)


def grad_kernel(size, scalars, cot_own, cot_away, *refs):
    pieces, (grad_own, grad_away, grad) = refs[: 4 * size], refs[4 * size :]
    rows = cot_own.shape[0]
    width = grad_own.shape[2]

    @pl.when(pl.program_id(0) == 0)
    def _():
        grad[...] = jnp.zeros_like(grad)

    def add(order):
        cot = jnp.concatenate([cot_own[...], cot_away[...]], 0)
        dims = (((1,), (1,)), ((), ()))
        grad[...] += lax.dot_general(cot, stacked(pieces, size, order), dims, preferred_element_type=F32)

    @pl.when(scalars[0] == 0)
    def _():
        add((0, 1, 2, 3))

    @pl.when(scalars[0] != 0)
    def _():
        add((2, 3, 0, 1))

    @pl.when(pl.program_id(0) == pl.num_programs(0) - 1)
    def _():
        for s in range(size):
            block = grad[:, s * width : (s + 1) * width].astype(BF16)
            grad_own[scalars[1 + s]] = block[:rows]
            grad_away[scalars[1 + s]] = block[rows:]


def output_kernel(size, scalars, gated_own, gated_away, *refs):
    pieces, (out_own, *out_away, left) = refs[: 4 * size], refs[4 * size :]
    rows = out_own.shape[0]
    width = gated_own.shape[2]
    run = pl.num_programs(0) // len(out_away)

    @pl.when(pl.program_id(0) == 0)
    def _():
        for s in range(size):
            left[:rows, s * width : (s + 1) * width] = gated_own[scalars[1 + s]]
            left[rows:, s * width : (s + 1) * width] = gated_away[scalars[1 + s]]

    def add(order):
        total = jnp.dot(left[...], stacked(pieces, size, order), preferred_element_type=F32)
        out_own[...] = total[:rows]
        for k, ref in enumerate(out_away):

            @pl.when(pl.program_id(0) // run == k)
            def _(ref=ref):
                ref[...] = total[rows:].astype(BF16)

    @pl.when(scalars[0] == 0)
    def _():
        add((0, 1, 2, 3))

    @pl.when(scalars[0] != 0)
    def _():
        add((2, 3, 0, 1))


def far(arrays):
    return [pltpu.with_memory_space_constraint(a, pltpu.HBM) for a in arrays]


def grad_of_gated(scalars, cot_own, cot_away, pieces):
    rows, feats = cot_own.shape
    size, depth = len(pieces) // 4, pieces[0].shape[0]
    tile = min(1024, feats)
    out = (size, rows, 4 * depth)
    whole = pl.BlockSpec(out, lambda j, s: (0, 0, 0))
    return pl.pallas_call(
        functools.partial(grad_kernel, size),
        out_shape=(jax.ShapeDtypeStruct(out, BF16), pltpu.HBM(out, BF16)),
        grid_spec=pltpu.PrefetchScalarGridSpec(
            num_scalar_prefetch=1,
            grid=(feats // tile,),
            in_specs=[pl.BlockSpec((rows, tile), lambda j, s: (0, j))] * 2
            + [pl.BlockSpec((depth, tile), lambda j, s: (0, j))] * len(pieces),
            out_specs=(whole, whole),
            scratch_shapes=[pltpu.VMEM((2 * rows, 4 * depth * size), F32)],
        ),
        compiler_params=pltpu.CompilerParams(vmem_limit_bytes=28 << 20),
        cost_estimate=pl.CostEstimate(
            flops=4 * rows * depth * len(pieces) * feats,
            bytes_accessed=2 * depth * len(pieces) * feats + 4 * rows * feats,
            transcendentals=0,
        ),
    )(scalars, *far([cot_own, cot_away, *pieces]))


def output_of(scalars, gated_own, gated_away, pieces):
    size, rows, width = gated_own.shape
    depth, feats = pieces[0].shape
    tile = min(1024, feats // CHUNKS)
    run = feats // CHUNKS // tile
    block = pl.BlockSpec((rows, tile), lambda j, s: (0, j))

    def chunk(k):
        return pl.BlockSpec((rows, tile), lambda j, s: (0, jnp.clip(j - k * run, 0, run - 1)))

    return pl.pallas_call(
        functools.partial(output_kernel, size),
        out_shape=(pltpu.HBM((rows, feats), F32),) + (pltpu.HBM((rows, feats // CHUNKS), BF16),) * CHUNKS,
        grid_spec=pltpu.PrefetchScalarGridSpec(
            num_scalar_prefetch=1,
            grid=(feats // tile,),
            in_specs=[pl.BlockSpec(gated_own.shape, lambda j, s: (0, 0, 0))] * 2
            + [pl.BlockSpec((depth, tile), lambda j, s: (0, j))] * len(pieces),
            out_specs=(block,) + tuple(chunk(k) for k in range(CHUNKS)),
            scratch_shapes=[pltpu.VMEM((2 * rows, size * width), BF16)],
        ),
        compiler_params=pltpu.CompilerParams(vmem_limit_bytes=28 << 20),
        cost_estimate=pl.CostEstimate(
            flops=4 * rows * depth * len(pieces) * feats,
            bytes_accessed=2 * depth * len(pieces) * feats + 6 * rows * feats,
            transcendentals=0,
        ),
    )(scalars, *far([gated_own, gated_away, *pieces]))


def merge_kernel(scalars, own, away, out):
    size, _, width = own.shape
    for r in range(size):
        for ref, side in ((own, scalars[0]), (away, 1 - scalars[0])):
            out[:, pl.ds(pl.multiple_of((2 * r + side) * width, width), width)] = ref[r]


def merge(side, own, away):
    size, rows, width = own.shape
    vmem = pl.BlockSpec(memory_space=pltpu.VMEM)
    return pl.pallas_call(
        merge_kernel,
        out_shape=jax.ShapeDtypeStruct((rows, 2 * size * width), own.dtype),
        in_specs=[pl.BlockSpec(memory_space=pltpu.SMEM), vmem, vmem],
        out_specs=vmem,
        compiler_params=pltpu.CompilerParams(vmem_limit_bytes=GRANT),
        cost_estimate=pl.CostEstimate(flops=0, bytes_accessed=8 * own.size, transcendentals=0),
    )(side.reshape(1), own, away)


def on_ring(queries, keys, values, w_out, taps, seg_ids, cotangent):
    rows, chans = queries.shape
    length = rows
    nseq = lax.axis_size("seq")
    place = lax.axis_index("seq")
    size = nseq // 4
    core, pair, row = [i.astype(jnp.int32) for i in (place & 1, (place >> 1) & 1, place >> 2)]
    at = ring_step(row, size)
    swap_core = [(i, i ^ 1) for i in range(nseq)]
    swap_pair = [(i, i ^ 2) for i in range(nseq)]
    walk = list(range(0, size, 2)) + list(range(1, size, 2))[::-1]
    onward = [(4 * walk[i] + k, 4 * walk[(i + 1) % size] + k) for i in range(size) for k in range(4)]
    behind = [(b, a) for a, b in onward]
    later = [(i, i + 1) for i in range(nseq - 1)]
    earlier = [(i + 1, i) for i in range(nseq - 1)]
    send = functools.partial(lax.ppermute, axis_name="seq")
    tie = lax.optimization_barrier
    linked = links(seg_ids, place)
    table, high, low = spectrum_table(length)
    table_now, high_now, low_now = table[:, length:], high[:, length:], low[:, length:]
    scale = 1.0 / length

    half = rows // 2
    first, second, cotangent, w_out = tie((w_out[:half], w_out[half:], cotangent, w_out))
    swapped = send(w_out, perm=swap_core)
    cot_away = send(cotangent, perm=swap_pair)
    product, cot_away = tie((mul(keys, values), cot_away))
    before = send(product, perm=later)
    filt = forward_dft(high_now, low_now, tie(taps.T), ((1,), (0,)))

    pieces = [first, swapped[:half], second, swapped[half:]]
    for step in range(1, size):
        first, second = send(first, perm=onward), send(second, perm=behind)
        swap = (first, second)
        if step == 1:
            *swap, filt = tie((*swap, filt))
        if step == 3:
            before = jnp.where(linked, before, jnp.zeros_like(before))
            data = forward_dft(high, low, jnp.concatenate([before, product], 0), ((1,), (0,)))
            filtered = inverse_dft(table_now, times(filt, data), scale).astype(BF16)
            gated = mul(queries, filtered)
            gated_own, gated_away = deal(pair, gated, chans // (2 * size))
            *swap, gated_own, gated_away = tie((*swap, gated_own, gated_away))
            gated_away = send(gated_away, perm=swap_pair)
        if step == max(size - 2, 3):
            *swap, gated_away = tie((*swap, gated_away))
        pieces += [first, send(swap[0], perm=swap_core), second, send(swap[1], perm=swap_core)]
    places = [core] + [ring_place(lax.rem(at - s + size, size), size) for s in range(size)]
    scalars = jnp.stack(places)
    grad_own, grad_away = grad_of_gated(scalars, cotangent, cot_away, pieces)
    grad_away = send(grad_away, perm=swap_pair)
    out_own, *out_away = output_of(scalars, gated_own, gated_away, pieces)
    grad_away, out_own, out_away = tie((grad_away, out_own, out_away))
    grad_gated = merge(pair, grad_own, grad_away)
    out_away = [send(chunk, perm=swap_pair) for chunk in out_away]
    grad_queries = mul(grad_gated, filtered)
    grad_filtered = mul(grad_gated, queries)
    grads = forward_dft(high_now, low_now, grad_filtered, ((1,), (0,)))
    back = inverse_dft(table, times_conj(grads, filt), scale)
    across = jnp.where(linked, back[:length], 0.0).astype(BF16)
    ahead = send(across, perm=earlier)
    grads, across, out_away[0] = tie((grads, across, out_away[0]))
    taps_part = inverse_dft(table_now, times_conj(grads, data), scale)
    guests = [out_away[1], ahead, out_away[2], out_away[3]]
    taps_grad, (out_away[1], ahead, out_away[2], out_away[3]) = sum_over_ring(taps_part, nseq, place, guests)
    taps_grad = taps_grad.T
    outputs = (out_own + jnp.concatenate(out_away, 1).astype(F32)).astype(BF16)
    grad_product = (back[length:] + ahead.astype(F32)).astype(BF16)
    grad_keys = mul(grad_product, values)
    grad_values = mul(grad_product, keys)
    return (outputs, grad_queries, grad_keys, grad_values, taps_grad)


def on_device(queries, keys, values, w_out, taps, seg_ids, cotangent):
    rows, chans = queries.shape
    length = taps.shape[1]
    assert rows == length
    nseq = lax.axis_size("seq")
    place = lax.axis_index("seq")
    table, high, low = spectrum_table(length)
    table_now, high_now, low_now = table[:, length:], high[:, length:], low[:, length:]
    scale = 1.0 / length
    later = [(i, i + 1) for i in range(nseq - 1)]
    earlier = [(i + 1, i) for i in range(nseq - 1)]
    linked = links(seg_ids, place)

    product = mul(keys, values)
    before = lax.ppermute(product, "seq", later)
    before = jnp.where(linked, before, jnp.zeros_like(before))
    data = forward_dft(high, low, jnp.concatenate([before, product], 0), ((1,), (0,)))
    filt = forward_dft(high_now, low_now, taps, ((1,), (1,)))
    filtered = inverse_dft(table_now, times(filt, data), scale).astype(BF16)
    gated = mul(queries, filtered)

    grad_gated, outputs = gathered_products(gated, cotangent, w_out)
    grad_queries = mul(grad_gated, filtered)
    grad_filtered = mul(grad_gated, queries)
    grads = forward_dft(high_now, low_now, grad_filtered, ((1,), (0,)))
    back = inverse_dft(table, times_conj(grads, filt), scale)
    across = jnp.where(linked, back[:length], 0.0).astype(BF16)
    ahead = lax.ppermute(across, "seq", earlier)
    taps_part = inverse_dft(table_now, times_conj(grads, data), scale)
    taps_grad = scatter_sum(taps_part, nseq, place, ()).T
    grad_product = (back[length:] + ahead.astype(F32)).astype(BF16)
    grad_keys = mul(grad_product, values)
    grad_values = mul(grad_product, keys)
    return (outputs, grad_queries, grad_keys, grad_values, taps_grad)


def solution(mesh):
    block = P("seq", "tp")
    count = mesh.shape["seq"]
    ring = mesh.shape["tp"] == 1 and count & (count - 1) == 0 and count >= 16

    def run(queries, keys, values, w_out, taps, seg_ids, cotangent):
        rows, chans = queries.shape
        place = on_ring if ring and rows * count == chans else on_device
        return place(queries, keys, values, w_out, taps, seg_ids, cotangent)

    return jax.shard_map(
        run,
        mesh=mesh,
        in_specs=(block, block, block, block, P("tp", None), P(), block),
        out_specs=(block, block, block, block, P(("tp", "seq"), None)),
        check_vma=False,
    )
```

```python
import functools

import jax
import jax.numpy as jnp
import numpy as np
from jax import lax
from jax.experimental import pallas as pl
from jax.experimental.pallas import tpu as pltpu
from jax.sharding import PartitionSpec as P

F32 = jnp.float32
BF16 = jnp.bfloat16
GRANT = 16 << 20
CHUNKS = 4


def spectrum_table(length):
    angles = np.pi * (2 * np.arange(length)[:, None] + 1) * np.arange(-length, length)[None, :] / (2 * length)
    table = np.concatenate([np.cos(angles), -np.sin(angles)], 0).astype(np.float32)
    high = table.astype(BF16)
    low = (table - high.astype(np.float32)).astype(BF16)
    return table, high, low


def forward_dft(high, low, data, dims):
    first = lax.dot_general(high, data, (dims, ((), ())), preferred_element_type=F32)
    second = lax.dot_general(low, data, (dims, ((), ())), preferred_element_type=F32)
    return first + second


def times(a, b):
    half = a.shape[0] // 2
    ar, ai, br, bi = a[:half], a[half:], b[:half], b[half:]
    return jnp.concatenate([ar * br - ai * bi, ar * bi + ai * br], 0)


def times_conj(a, b):
    half = a.shape[0] // 2
    ar, ai, br, bi = a[:half], a[half:], b[:half], b[half:]
    return jnp.concatenate([ar * br + ai * bi, ai * br - ar * bi], 0)


def inverse_dft(table, spectrum, scale):
    done = lax.dot_general(
        table, spectrum, (((0,), (0,)), ((), ())), precision=lax.Precision.HIGH, preferred_element_type=F32
    )
    return done * scale


def mul(a, b):
    return (a.astype(F32) * b.astype(F32)).astype(BF16)


def pick(data, width, side):
    blocks = [data[:, i : i + width] for i in range(0, data.shape[1], width)]
    return jnp.concatenate([jnp.where(side == 0, a, b) for a, b in zip(blocks[::2], blocks[1::2])], 1)


def scatter_sum(part, nseq, place, order):
    share = part.shape[1] // nseq
    bits = nseq.bit_length() - 1
    if nseq != 1 << bits:
        return lax.psum_scatter(part, "seq", scatter_dimension=1, tiled=True)
    left = list(range(bits))
    for step in [b for b in order if b < bits] + [b for b in range(bits) if b not in order]:
        width = share << sum(b < step for b in left)
        left.remove(step)
        mine = (place >> step) & 1
        away = pick(part, width, 1 - mine)
        if step:
            away = away.astype(BF16)
        away = lax.ppermute(away, "seq", [(i, i ^ (1 << step)) for i in range(nseq)])
        part = pick(part, width, mine) + away.astype(F32)
    return part


def deal_kernel(sides, scalars, data, kept, away):
    width = kept.shape[-1]
    for i in range(data.shape[1] // (2 * width)):
        for ref, side in ((kept, scalars[0]), (away, 1 - scalars[0])):
            block = data[:, pl.ds(pl.multiple_of((2 * i + side) * width, width), width)]
            if sides:
                ref[i % sides, i // sides] = block
            else:
                ref[i] = block


def deal(side, data, width, sides=0):
    rows, chans = data.shape
    count = chans // (2 * width)
    lead = (sides, count // sides) if sides else (count,)
    out = jax.ShapeDtypeStruct(lead + (rows, width), data.dtype)
    vmem = pl.BlockSpec(memory_space=pltpu.VMEM)
    return pl.pallas_call(
        functools.partial(deal_kernel, sides),
        out_shape=(out, out),
        in_specs=[pl.BlockSpec(memory_space=pltpu.SMEM), vmem],
        out_specs=(vmem, vmem),
        compiler_params=pltpu.CompilerParams(vmem_limit_bytes=GRANT),
        cost_estimate=pl.CostEstimate(flops=0, bytes_accessed=8 * rows * chans, transcendentals=0),
    )(side.reshape(1), data)


def sum_over_ring(part, nseq, place, guests):
    core, pair, row = place & 1, (place >> 1) & 1, place >> 2
    lags, chans = part.shape
    size, chans = nseq // 4, chans // nseq

    def halve(part, bit, mine, kind):
        away = lax.dynamic_index_in_dim(part, 1 - mine, 1, False).astype(kind)
        away = lax.ppermute(away, "seq", [(i, i ^ bit) for i in range(nseq)])
        return lax.dynamic_index_in_dim(part, mine, 1, False) + away.astype(F32)

    kept, away = deal(core.astype(jnp.int32), part, chans, 2)
    part = kept + lax.ppermute(away, "seq", [(i, i ^ 1) for i in range(nseq)])
    part = part.reshape(2, size, lags, chans)
    left, done = size, 0
    while left > 1:
        bit = size // left
        mine = (row // bit) & 1
        if done < len(guests) - 1:
            part, guests[done] = lax.optimization_barrier((part, guests[done]))
            done += 1
        part = part.reshape(2 * left // 2, 2, lags, chans)
        part = halve(part, 4 * bit, mine, BF16).reshape(2, left // 2, lags, chans)
        left //= 2
    return halve(part.reshape(1, 2, lags, chans), 2, pair, BF16).reshape(lags, chans), guests


def links(seg_ids, place):
    own = lax.dynamic_index_in_dim(seg_ids, place, 0, False)
    prior = lax.dynamic_index_in_dim(seg_ids, jnp.maximum(place - 1, 0), 0, False)
    return (place > 0) & (own == prior)


def gathered_products(gated, cotangent, w_out):
    weights = lax.all_gather(w_out, "seq", axis=0, tiled=True)
    grad_gated = lax.dot_general(cotangent, weights, (((1,), (1,)), ((), ())), preferred_element_type=F32)
    grad_gated = lax.psum_scatter(grad_gated, "tp", scatter_dimension=1, tiled=True).astype(BF16)
    outputs = jnp.dot(
        lax.all_gather(gated, "tp", axis=1, tiled=True), weights, preferred_element_type=F32
    ).astype(BF16)
    return grad_gated, outputs


def ring_place(step, size):
    half = (size + 1) // 2
    return jnp.where(step < half, 2 * step, 2 * (size - 1 - step) + 1)


def ring_step(row, size):
    return jnp.where(row & 1 == 0, row >> 1, size - 1 - (row >> 1))


def stacked(pieces, size, order):
    rows = []
    for s in range(size):
        m = (size - s) % size
        block = (pieces[4 * s], pieces[4 * m + 2], pieces[4 * s + 1], pieces[4 * m + 3])
        rows += [block[k][...] for k in order]
    return jnp.concatenate(rows, 0)


def grad_kernel(size, scalars, cot_own, cot_away, *refs):
    pieces, (grad_own, grad_away, grad) = refs[: 4 * size], refs[4 * size :]
    rows = cot_own.shape[0]
    width = grad_own.shape[2]

    @pl.when(pl.program_id(0) == 0)
    def _():
        grad[...] = jnp.zeros_like(grad)

    def add(order):
        cot = jnp.concatenate([cot_own[...], cot_away[...]], 0)
        dims = (((1,), (1,)), ((), ()))
        grad[...] += lax.dot_general(cot, stacked(pieces, size, order), dims, preferred_element_type=F32)

    @pl.when(scalars[0] == 0)
    def _():
        add((0, 1, 2, 3))

    @pl.when(scalars[0] != 0)
    def _():
        add((2, 3, 0, 1))

    @pl.when(pl.program_id(0) == pl.num_programs(0) - 1)
    def _():
        for s in range(size):
            block = grad[:, s * width : (s + 1) * width].astype(BF16)
            grad_own[scalars[1 + s]] = block[:rows]
            grad_away[scalars[1 + s]] = block[rows:]


def output_kernel(size, scalars, gated_own, gated_away, *refs):
    pieces, (out_own, *out_away, left) = refs[: 4 * size], refs[4 * size :]
    rows = out_own.shape[0]
    width = gated_own.shape[2]
    run = pl.num_programs(0) // len(out_away)

    @pl.when(pl.program_id(0) == 0)
    def _():
        for s in range(size):
            left[:rows, s * width : (s + 1) * width] = gated_own[scalars[1 + s]]
            left[rows:, s * width : (s + 1) * width] = gated_away[scalars[1 + s]]

    def add(order):
        total = jnp.dot(left[...], stacked(pieces, size, order), preferred_element_type=F32)
        out_own[...] = total[:rows]
        for k, ref in enumerate(out_away):

            @pl.when(pl.program_id(0) // run == k)
            def _(ref=ref):
                ref[...] = total[rows:].astype(BF16)

    @pl.when(scalars[0] == 0)
    def _():
        add((0, 1, 2, 3))

    @pl.when(scalars[0] != 0)
    def _():
        add((2, 3, 0, 1))


def far(arrays):
    return [pltpu.with_memory_space_constraint(a, pltpu.HBM) for a in arrays]


def grad_of_gated(scalars, cot_own, cot_away, pieces):
    rows, feats = cot_own.shape
    size, depth = len(pieces) // 4, pieces[0].shape[0]
    tile = min(1024, feats)
    out = (size, rows, 4 * depth)
    whole = pl.BlockSpec(out, lambda j, s: (0, 0, 0))
    return pl.pallas_call(
        functools.partial(grad_kernel, size),
        out_shape=(jax.ShapeDtypeStruct(out, BF16), pltpu.HBM(out, BF16)),
        grid_spec=pltpu.PrefetchScalarGridSpec(
            num_scalar_prefetch=1,
            grid=(feats // tile,),
            in_specs=[pl.BlockSpec((rows, tile), lambda j, s: (0, j))] * 2
            + [pl.BlockSpec((depth, tile), lambda j, s: (0, j))] * len(pieces),
            out_specs=(whole, whole),
            scratch_shapes=[pltpu.VMEM((2 * rows, 4 * depth * size), F32)],
        ),
        compiler_params=pltpu.CompilerParams(vmem_limit_bytes=28 << 20),
        cost_estimate=pl.CostEstimate(
            flops=4 * rows * depth * len(pieces) * feats,
            bytes_accessed=2 * depth * len(pieces) * feats + 4 * rows * feats,
            transcendentals=0,
        ),
    )(scalars, *far([cot_own, cot_away, *pieces]))


def output_of(scalars, gated_own, gated_away, pieces):
    size, rows, width = gated_own.shape
    depth, feats = pieces[0].shape
    tile = min(1024, feats // CHUNKS)
    run = feats // CHUNKS // tile
    block = pl.BlockSpec((rows, tile), lambda j, s: (0, j))

    def chunk(k):
        return pl.BlockSpec((rows, tile), lambda j, s: (0, jnp.clip(j - k * run, 0, run - 1)))

    return pl.pallas_call(
        functools.partial(output_kernel, size),
        out_shape=(pltpu.HBM((rows, feats), F32),) + (pltpu.HBM((rows, feats // CHUNKS), BF16),) * CHUNKS,
        grid_spec=pltpu.PrefetchScalarGridSpec(
            num_scalar_prefetch=1,
            grid=(feats // tile,),
            in_specs=[pl.BlockSpec(gated_own.shape, lambda j, s: (0, 0, 0))] * 2
            + [pl.BlockSpec((depth, tile), lambda j, s: (0, j))] * len(pieces),
            out_specs=(block,) + tuple(chunk(k) for k in range(CHUNKS)),
            scratch_shapes=[pltpu.VMEM((2 * rows, size * width), BF16)],
        ),
        compiler_params=pltpu.CompilerParams(vmem_limit_bytes=28 << 20),
        cost_estimate=pl.CostEstimate(
            flops=4 * rows * depth * len(pieces) * feats,
            bytes_accessed=2 * depth * len(pieces) * feats + 6 * rows * feats,
            transcendentals=0,
        ),
    )(scalars, *far([gated_own, gated_away, *pieces]))


def merge_kernel(scalars, own, away, out):
    size, _, width = own.shape
    for r in range(size):
        for ref, side in ((own, scalars[0]), (away, 1 - scalars[0])):
            out[:, pl.ds(pl.multiple_of((2 * r + side) * width, width), width)] = ref[r]


def merge(side, own, away):
    size, rows, width = own.shape
    vmem = pl.BlockSpec(memory_space=pltpu.VMEM)
    return pl.pallas_call(
        merge_kernel,
        out_shape=jax.ShapeDtypeStruct((rows, 2 * size * width), own.dtype),
        in_specs=[pl.BlockSpec(memory_space=pltpu.SMEM), vmem, vmem],
        out_specs=vmem,
        compiler_params=pltpu.CompilerParams(vmem_limit_bytes=GRANT),
        cost_estimate=pl.CostEstimate(flops=0, bytes_accessed=8 * own.size, transcendentals=0),
    )(side.reshape(1), own, away)


def on_ring(queries, keys, values, w_out, taps, seg_ids, cotangent):
    rows, chans = queries.shape
    length = rows
    nseq = lax.axis_size("seq")
    place = lax.axis_index("seq")
    size = nseq // 4
    core, pair, row = [i.astype(jnp.int32) for i in (place & 1, (place >> 1) & 1, place >> 2)]
    at = ring_step(row, size)
    swap_core = [(i, i ^ 1) for i in range(nseq)]
    swap_pair = [(i, i ^ 2) for i in range(nseq)]
    walk = list(range(0, size, 2)) + list(range(1, size, 2))[::-1]
    onward = [(4 * walk[i] + k, 4 * walk[(i + 1) % size] + k) for i in range(size) for k in range(4)]
    behind = [(b, a) for a, b in onward]
    later = [(i, i + 1) for i in range(nseq - 1)]
    earlier = [(i + 1, i) for i in range(nseq - 1)]
    send = functools.partial(lax.ppermute, axis_name="seq")
    tie = lax.optimization_barrier
    linked = links(seg_ids, place)
    table, high, low = spectrum_table(length)
    table_now, high_now, low_now = table[:, length:], high[:, length:], low[:, length:]
    scale = 1.0 / length

    half = rows // 2
    first, second, cotangent, w_out = tie((w_out[:half], w_out[half:], cotangent, w_out))
    swapped = send(w_out, perm=swap_core)
    cot_away = send(cotangent, perm=swap_pair)
    product, cot_away = tie((mul(keys, values), cot_away))
    before = send(product, perm=later)
    filt = forward_dft(high_now, low_now, tie(taps.T), ((1,), (0,)))

    pieces = [first, swapped[:half], second, swapped[half:]]
    for step in range(1, size):
        first, second = send(first, perm=onward), send(second, perm=behind)
        swap = (first, second)
        if step == 1:
            *swap, filt = tie((*swap, filt))
        if step == 3:
            before = jnp.where(linked, before, jnp.zeros_like(before))
            data = forward_dft(high, low, jnp.concatenate([before, product], 0), ((1,), (0,)))
            filtered = inverse_dft(table_now, times(filt, data), scale).astype(BF16)
            gated = mul(queries, filtered)
            gated_own, gated_away = deal(pair, gated, chans // (2 * size))
            *swap, gated_own, gated_away = tie((*swap, gated_own, gated_away))
            gated_away = send(gated_away, perm=swap_pair)
        if step == max(size - 2, 3):
            *swap, gated_away = tie((*swap, gated_away))
        pieces += [first, send(swap[0], perm=swap_core), second, send(swap[1], perm=swap_core)]
    places = [core] + [ring_place(lax.rem(at - s + size, size), size) for s in range(size)]
    scalars = jnp.stack(places)
    grad_own, grad_away = grad_of_gated(scalars, cotangent, cot_away, pieces)
    grad_away = send(grad_away, perm=swap_pair)
    out_own, *out_away = output_of(scalars, gated_own, gated_away, pieces)
    grad_away, out_own, out_away = tie((grad_away, out_own, out_away))
    grad_gated = merge(pair, grad_own, grad_away)
    out_away = [send(chunk, perm=swap_pair) for chunk in out_away]
    grad_queries = mul(grad_gated, filtered)
    grad_filtered = mul(grad_gated, queries)
    grads = forward_dft(high_now, low_now, grad_filtered, ((1,), (0,)))
    back = inverse_dft(table, times_conj(grads, filt), scale)
    across = jnp.where(linked, back[:length], 0.0).astype(BF16)
    ahead = send(across, perm=earlier)
    grads, across, out_away[0] = tie((grads, across, out_away[0]))
    taps_part = inverse_dft(table_now, times_conj(grads, data), scale)
    guests = [(), (), (ahead, out_away[1]), ()]
    taps_grad, (_, _, (ahead, out_away[1]), _) = sum_over_ring(taps_part, nseq, place, guests)
    taps_grad = taps_grad.T
    outputs = (out_own + jnp.concatenate(out_away, 1).astype(F32)).astype(BF16)
    grad_product = (back[length:] + ahead.astype(F32)).astype(BF16)
    grad_keys = mul(grad_product, values)
    grad_values = mul(grad_product, keys)
    return (outputs, grad_queries, grad_keys, grad_values, taps_grad)


def on_device(queries, keys, values, w_out, taps, seg_ids, cotangent):
    rows, chans = queries.shape
    length = taps.shape[1]
    assert rows == length
    nseq = lax.axis_size("seq")
    place = lax.axis_index("seq")
    table, high, low = spectrum_table(length)
    table_now, high_now, low_now = table[:, length:], high[:, length:], low[:, length:]
    scale = 1.0 / length
    later = [(i, i + 1) for i in range(nseq - 1)]
    earlier = [(i + 1, i) for i in range(nseq - 1)]
    linked = links(seg_ids, place)

    product = mul(keys, values)
    before = lax.ppermute(product, "seq", later)
    before = jnp.where(linked, before, jnp.zeros_like(before))
    data = forward_dft(high, low, jnp.concatenate([before, product], 0), ((1,), (0,)))
    filt = forward_dft(high_now, low_now, taps, ((1,), (1,)))
    filtered = inverse_dft(table_now, times(filt, data), scale).astype(BF16)
    gated = mul(queries, filtered)

    grad_gated, outputs = gathered_products(gated, cotangent, w_out)
    grad_queries = mul(grad_gated, filtered)
    grad_filtered = mul(grad_gated, queries)
    grads = forward_dft(high_now, low_now, grad_filtered, ((1,), (0,)))
    back = inverse_dft(table, times_conj(grads, filt), scale)
    across = jnp.where(linked, back[:length], 0.0).astype(BF16)
    ahead = lax.ppermute(across, "seq", earlier)
    taps_part = inverse_dft(table_now, times_conj(grads, data), scale)
    taps_grad = scatter_sum(taps_part, nseq, place, ()).T
    grad_product = (back[length:] + ahead.astype(F32)).astype(BF16)
    grad_keys = mul(grad_product, values)
    grad_values = mul(grad_product, keys)
    return (outputs, grad_queries, grad_keys, grad_values, taps_grad)


def solution(mesh):
    block = P("seq", "tp")
    count = mesh.shape["seq"]
    ring = mesh.shape["tp"] == 1 and count & (count - 1) == 0 and count >= 16

    def run(queries, keys, values, w_out, taps, seg_ids, cotangent):
        rows, chans = queries.shape
        place = on_ring if ring and rows * count == chans else on_device
        return place(queries, keys, values, w_out, taps, seg_ids, cotangent)

    return jax.shard_map(
        run,
        mesh=mesh,
        in_specs=(block, block, block, block, P("tp", None), P(), block),
        out_specs=(block, block, block, block, P(("tp", "seq"), None)),
        check_vma=False,
    )
```

```python
import functools

import jax
import jax.numpy as jnp
import numpy as np
from jax import lax
from jax.experimental import pallas as pl
from jax.experimental.pallas import tpu as pltpu
from jax.sharding import PartitionSpec as P

F32 = jnp.float32
BF16 = jnp.bfloat16
GRANT = 16 << 20


def spectrum_table(length):
    angles = np.pi * (2 * np.arange(length)[:, None] + 1) * np.arange(-length, length)[None, :] / (2 * length)
    table = np.concatenate([np.cos(angles), -np.sin(angles)], 0).astype(np.float32)
    high = table.astype(BF16)
    low = (table - high.astype(np.float32)).astype(BF16)
    return table, high, low


def forward_dft(high, low, data, dims):
    first = lax.dot_general(high, data, (dims, ((), ())), preferred_element_type=F32)
    second = lax.dot_general(low, data, (dims, ((), ())), preferred_element_type=F32)
    return first + second


def times(a, b):
    half = a.shape[0] // 2
    ar, ai, br, bi = a[:half], a[half:], b[:half], b[half:]
    return jnp.concatenate([ar * br - ai * bi, ar * bi + ai * br], 0)


def times_conj(a, b):
    half = a.shape[0] // 2
    ar, ai, br, bi = a[:half], a[half:], b[:half], b[half:]
    return jnp.concatenate([ar * br + ai * bi, ai * br - ar * bi], 0)


def inverse_dft(table, spectrum, scale):
    done = lax.dot_general(
        table, spectrum, (((0,), (0,)), ((), ())), precision=lax.Precision.HIGH, preferred_element_type=F32
    )
    return done * scale


def mul(a, b):
    return (a.astype(F32) * b.astype(F32)).astype(BF16)


def pick(data, width, side):
    blocks = [data[:, i : i + width] for i in range(0, data.shape[1], width)]
    return jnp.concatenate([jnp.where(side == 0, a, b) for a, b in zip(blocks[::2], blocks[1::2])], 1)


def scatter_sum(part, nseq, place, order):
    share = part.shape[1] // nseq
    bits = nseq.bit_length() - 1
    if nseq != 1 << bits:
        return lax.psum_scatter(part, "seq", scatter_dimension=1, tiled=True)
    left = list(range(bits))
    for step in [b for b in order if b < bits] + [b for b in range(bits) if b not in order]:
        width = share << sum(b < step for b in left)
        left.remove(step)
        mine = (place >> step) & 1
        away = pick(part, width, 1 - mine)
        if step:
            away = away.astype(BF16)
        away = lax.ppermute(away, "seq", [(i, i ^ (1 << step)) for i in range(nseq)])
        part = pick(part, width, mine) + away.astype(F32)
    return part


def deal_kernel(sides, scalars, data, kept, away):
    width = kept.shape[-1]
    for i in range(data.shape[1] // (2 * width)):
        for ref, side in ((kept, scalars[0]), (away, 1 - scalars[0])):
            block = data[:, pl.ds(pl.multiple_of((2 * i + side) * width, width), width)]
            if sides:
                ref[i % sides, i // sides] = block
            else:
                ref[i] = block


def deal(side, data, width, sides=0):
    rows, chans = data.shape
    count = chans // (2 * width)
    lead = (sides, count // sides) if sides else (count,)
    out = jax.ShapeDtypeStruct(lead + (rows, width), data.dtype)
    vmem = pl.BlockSpec(memory_space=pltpu.VMEM)
    return pl.pallas_call(
        functools.partial(deal_kernel, sides),
        out_shape=(out, out),
        in_specs=[pl.BlockSpec(memory_space=pltpu.SMEM), vmem],
        out_specs=(vmem, vmem),
        compiler_params=pltpu.CompilerParams(vmem_limit_bytes=GRANT),
        cost_estimate=pl.CostEstimate(flops=0, bytes_accessed=8 * rows * chans, transcendentals=0),
    )(side.reshape(1), data)


def sum_over_ring(part, nseq, place):
    core, pair, row = place & 1, (place >> 1) & 1, place >> 2
    lags, chans = part.shape
    size, chans = nseq // 4, chans // nseq

    def halve(part, bit, mine, kind):
        away = lax.dynamic_index_in_dim(part, 1 - mine, 1, False).astype(kind)
        away = lax.ppermute(away, "seq", [(i, i ^ bit) for i in range(nseq)])
        return lax.dynamic_index_in_dim(part, mine, 1, False) + away.astype(F32)

    kept, away = deal(core.astype(jnp.int32), part, chans, 2)
    part = kept + lax.ppermute(away, "seq", [(i, i ^ 1) for i in range(nseq)])
    part = part.reshape(2, size, lags, chans)
    left = size
    while left > 1:
        bit = size // left
        mine = (row // bit) & 1
        part = part.reshape(2 * left // 2, 2, lags, chans)
        part = halve(part, 4 * bit, mine, BF16).reshape(2, left // 2, lags, chans)
        left //= 2
    return halve(part.reshape(1, 2, lags, chans), 2, pair, BF16).reshape(lags, chans)


def links(seg_ids, place):
    own = lax.dynamic_index_in_dim(seg_ids, place, 0, False)
    prior = lax.dynamic_index_in_dim(seg_ids, jnp.maximum(place - 1, 0), 0, False)
    return (place > 0) & (own == prior)


def gathered_products(gated, cotangent, w_out):
    weights = lax.all_gather(w_out, "seq", axis=0, tiled=True)
    grad_gated = lax.dot_general(cotangent, weights, (((1,), (1,)), ((), ())), preferred_element_type=F32)
    grad_gated = lax.psum_scatter(grad_gated, "tp", scatter_dimension=1, tiled=True).astype(BF16)
    outputs = jnp.dot(
        lax.all_gather(gated, "tp", axis=1, tiled=True), weights, preferred_element_type=F32
    ).astype(BF16)
    return grad_gated, outputs


def ring_place(step, size):
    half = (size + 1) // 2
    return jnp.where(step < half, 2 * step, 2 * (size - 1 - step) + 1)


def ring_step(row, size):
    return jnp.where(row & 1 == 0, row >> 1, size - 1 - (row >> 1))


def products_kernel(size, scalars, cot_own, cot_away, gated_own, gated_away, *refs):
    pieces, (grad_own, grad_away, out_own, out_away, grad) = refs[: 4 * size], refs[4 * size :]
    rows = cot_own.shape[0]

    @pl.when(pl.program_id(0) == 0)
    def _():
        grad[...] = jnp.zeros_like(grad)

    def add(order):
        cot = jnp.concatenate([cot_own[...], cot_away[...]], 0)
        total = None
        for s in range(size):
            m = (size - s) % size
            block = (pieces[4 * s], pieces[4 * m + 2], pieces[4 * s + 1], pieces[4 * m + 3])
            block = jnp.concatenate([block[k][...] for k in order], 0)
            grad[s] += lax.dot_general(cot, block, (((1,), (1,)), ((), ())), preferred_element_type=F32)
            left = jnp.concatenate([gated_own[scalars[1 + s]], gated_away[scalars[1 + s]]], 0)
            part = jnp.dot(left, block, preferred_element_type=F32)
            total = part if total is None else total + part
        out_own[...] = total[:rows]
        out_away[...] = total[rows:].astype(BF16)

    @pl.when(scalars[0] == 0)
    def _():
        add((0, 1, 2, 3))

    @pl.when(scalars[0] != 0)
    def _():
        add((2, 3, 0, 1))

    @pl.when(pl.program_id(0) == pl.num_programs(0) - 1)
    def _():
        for s in range(size):
            grad_own[scalars[1 + s]] = grad[s, :rows].astype(BF16)
            grad_away[scalars[1 + s]] = grad[s, rows:].astype(BF16)


def products(scalars, cot_own, cot_away, gated_own, gated_away, pieces):
    rows, feats = cot_own.shape
    size, _, width = gated_own.shape
    depth = pieces[0].shape[0]
    tile = min(1024, feats)
    block = pl.BlockSpec((rows, tile), lambda j, s: (0, j))
    whole = pl.BlockSpec(gated_own.shape, lambda j, s: (0, 0, 0))
    return pl.pallas_call(
        functools.partial(products_kernel, size),
        out_shape=(
            jax.ShapeDtypeStruct(gated_own.shape, BF16),
            jax.ShapeDtypeStruct(gated_own.shape, BF16),
            jax.ShapeDtypeStruct((rows, feats), F32),
            jax.ShapeDtypeStruct((rows, feats), BF16),
        ),
        grid_spec=pltpu.PrefetchScalarGridSpec(
            num_scalar_prefetch=1,
            grid=(feats // tile,),
            in_specs=[block] * 2 + [whole] * 2 + [pl.BlockSpec((depth, tile), lambda j, s: (0, j))] * len(pieces),
            out_specs=(whole, whole, block, block),
            scratch_shapes=[pltpu.VMEM((size, 2 * rows, width), F32)],
        ),
        compiler_params=pltpu.CompilerParams(vmem_limit_bytes=28 << 20),
        cost_estimate=pl.CostEstimate(
            flops=8 * rows * depth * len(pieces) * feats,
            bytes_accessed=2 * depth * len(pieces) * feats + 10 * rows * feats,
            transcendentals=0,
        ),
    )(
        scalars,
        *[
            pltpu.with_memory_space_constraint(a, pltpu.HBM)
            for a in (cot_own, cot_away, gated_own, gated_away, *pieces)
        ],
    )


def merge_kernel(scalars, own, away, out):
    size, _, width = own.shape
    for r in range(size):
        for ref, side in ((own, scalars[0]), (away, 1 - scalars[0])):
            out[:, pl.ds(pl.multiple_of((2 * r + side) * width, width), width)] = ref[r]


def merge(side, own, away):
    size, rows, width = own.shape
    vmem = pl.BlockSpec(memory_space=pltpu.VMEM)
    return pl.pallas_call(
        merge_kernel,
        out_shape=jax.ShapeDtypeStruct((rows, 2 * size * width), own.dtype),
        in_specs=[pl.BlockSpec(memory_space=pltpu.SMEM), vmem, vmem],
        out_specs=vmem,
        compiler_params=pltpu.CompilerParams(vmem_limit_bytes=GRANT),
        cost_estimate=pl.CostEstimate(flops=0, bytes_accessed=8 * own.size, transcendentals=0),
    )(side.reshape(1), own, away)


def on_ring(queries, keys, values, w_out, taps, seg_ids, cotangent):
    rows, chans = queries.shape
    length = rows
    nseq = lax.axis_size("seq")
    place = lax.axis_index("seq")
    size = nseq // 4
    core, pair, row = [i.astype(jnp.int32) for i in (place & 1, (place >> 1) & 1, place >> 2)]
    at = ring_step(row, size)
    swap_core = [(i, i ^ 1) for i in range(nseq)]
    swap_pair = [(i, i ^ 2) for i in range(nseq)]
    walk = list(range(0, size, 2)) + list(range(1, size, 2))[::-1]
    onward = [(4 * walk[i] + k, 4 * walk[(i + 1) % size] + k) for i in range(size) for k in range(4)]
    behind = [(b, a) for a, b in onward]
    later = [(i, i + 1) for i in range(nseq - 1)]
    earlier = [(i + 1, i) for i in range(nseq - 1)]
    send = functools.partial(lax.ppermute, axis_name="seq")
    tie = lax.optimization_barrier
    linked = links(seg_ids, place)
    table, high, low = spectrum_table(length)
    table_now, high_now, low_now = table[:, length:], high[:, length:], low[:, length:]
    scale = 1.0 / length

    half = rows // 2
    first, second = w_out[:half], w_out[half:]
    swapped = send(w_out, perm=swap_core)
    cot_away = send(cotangent, perm=swap_pair)
    product, cot_away = tie((mul(keys, values), cot_away))
    before = send(product, perm=later)
    filt = forward_dft(high_now, low_now, tie(taps.T), ((1,), (0,)))

    pieces = [first, swapped[:half], second, swapped[half:]]
    for step in range(1, size):
        first, second = send(first, perm=onward), send(second, perm=behind)
        swap = (first, second)
        if step == 1:
            *swap, filt = tie((*swap, filt))
        if step == 3:
            before = jnp.where(linked, before, jnp.zeros_like(before))
            data = forward_dft(high, low, jnp.concatenate([before, product], 0), ((1,), (0,)))
            filtered = inverse_dft(table_now, times(filt, data), scale).astype(BF16)
            gated = mul(queries, filtered)
            gated_own, gated_away = deal(pair, gated, chans // (2 * size))
            *swap, gated_own, gated_away = tie((*swap, gated_own, gated_away))
            gated_away = send(gated_away, perm=swap_pair)
        pieces += [first, send(swap[0], perm=swap_core), second, send(swap[1], perm=swap_core)]
    places = [core] + [ring_place(lax.rem(at - s + size, size), size) for s in range(size)]
    grad_own, grad_away, out_own, out_away = products(
        jnp.stack(places), cotangent, cot_away, gated_own, gated_away, pieces
    )
    grad_gated = merge(pair, grad_own, send(grad_away, perm=swap_pair))
    out_away = send(out_away, perm=swap_pair)
    grad_queries = mul(grad_gated, filtered)
    grad_filtered = mul(grad_gated, queries)
    grads = forward_dft(high_now, low_now, grad_filtered, ((1,), (0,)))
    back = inverse_dft(table, times_conj(grads, filt), scale)
    across = jnp.where(linked, back[:length], 0.0).astype(BF16)
    ahead = send(across, perm=earlier)
    grads, across = tie((grads, across))
    taps_part = inverse_dft(table_now, times_conj(grads, data), scale)
    taps_grad = sum_over_ring(taps_part, nseq, place).T
    outputs = (out_own + out_away.astype(F32)).astype(BF16)
    grad_product = (back[length:] + ahead.astype(F32)).astype(BF16)
    grad_keys = mul(grad_product, values)
    grad_values = mul(grad_product, keys)
    return (outputs, grad_queries, grad_keys, grad_values, taps_grad)


def on_device(queries, keys, values, w_out, taps, seg_ids, cotangent):
    rows, chans = queries.shape
    length = taps.shape[1]
    assert rows == length
    nseq = lax.axis_size("seq")
    place = lax.axis_index("seq")
    table, high, low = spectrum_table(length)
    table_now, high_now, low_now = table[:, length:], high[:, length:], low[:, length:]
    scale = 1.0 / length
    later = [(i, i + 1) for i in range(nseq - 1)]
    earlier = [(i + 1, i) for i in range(nseq - 1)]
    linked = links(seg_ids, place)

    product = mul(keys, values)
    before = lax.ppermute(product, "seq", later)
    before = jnp.where(linked, before, jnp.zeros_like(before))
    data = forward_dft(high, low, jnp.concatenate([before, product], 0), ((1,), (0,)))
    filt = forward_dft(high_now, low_now, taps, ((1,), (1,)))
    filtered = inverse_dft(table_now, times(filt, data), scale).astype(BF16)
    gated = mul(queries, filtered)

    grad_gated, outputs = gathered_products(gated, cotangent, w_out)
    grad_queries = mul(grad_gated, filtered)
    grad_filtered = mul(grad_gated, queries)
    grads = forward_dft(high_now, low_now, grad_filtered, ((1,), (0,)))
    back = inverse_dft(table, times_conj(grads, filt), scale)
    across = jnp.where(linked, back[:length], 0.0).astype(BF16)
    ahead = lax.ppermute(across, "seq", earlier)
    taps_part = inverse_dft(table_now, times_conj(grads, data), scale)
    taps_grad = scatter_sum(taps_part, nseq, place, ()).T
    grad_product = (back[length:] + ahead.astype(F32)).astype(BF16)
    grad_keys = mul(grad_product, values)
    grad_values = mul(grad_product, keys)
    return (outputs, grad_queries, grad_keys, grad_values, taps_grad)


def solution(mesh):
    block = P("seq", "tp")
    count = mesh.shape["seq"]
    ring = mesh.shape["tp"] == 1 and count & (count - 1) == 0 and count >= 16

    def run(queries, keys, values, w_out, taps, seg_ids, cotangent):
        rows, chans = queries.shape
        place = on_ring if ring and rows * count == chans else on_device
        return place(queries, keys, values, w_out, taps, seg_ids, cotangent)

    return jax.shard_map(
        run,
        mesh=mesh,
        in_specs=(block, block, block, block, P("tp", None), P(), block),
        out_specs=(block, block, block, block, P(("tp", "seq"), None)),
        check_vma=False,
    )
```

```python
import functools

import jax
import jax.numpy as jnp
import numpy as np
from jax import lax
from jax.experimental import pallas as pl
from jax.experimental.pallas import tpu as pltpu
from jax.sharding import PartitionSpec as P

F32 = jnp.float32
BF16 = jnp.bfloat16
GRANT = 16 << 20


def spectrum_table(length):
    angles = np.pi * (2 * np.arange(length)[:, None] + 1) * np.arange(-length, length)[None, :] / (2 * length)
    table = np.concatenate([np.cos(angles), -np.sin(angles)], 0).astype(np.float32)
    high = table.astype(BF16)
    low = (table - high.astype(np.float32)).astype(BF16)
    return table, high, low


def forward_dft(high, low, data, dims):
    first = lax.dot_general(high, data, (dims, ((), ())), preferred_element_type=F32)
    second = lax.dot_general(low, data, (dims, ((), ())), preferred_element_type=F32)
    return first + second


def times(a, b):
    half = a.shape[0] // 2
    ar, ai, br, bi = a[:half], a[half:], b[:half], b[half:]
    return jnp.concatenate([ar * br - ai * bi, ar * bi + ai * br], 0)


def times_conj(a, b):
    half = a.shape[0] // 2
    ar, ai, br, bi = a[:half], a[half:], b[:half], b[half:]
    return jnp.concatenate([ar * br + ai * bi, ai * br - ar * bi], 0)


def inverse_dft(table, spectrum, scale):
    done = lax.dot_general(
        table, spectrum, (((0,), (0,)), ((), ())), precision=lax.Precision.HIGH, preferred_element_type=F32
    )
    return done * scale


def mul(a, b):
    return (a.astype(F32) * b.astype(F32)).astype(BF16)


def pick(data, width, side):
    blocks = [data[:, i : i + width] for i in range(0, data.shape[1], width)]
    return jnp.concatenate([jnp.where(side == 0, a, b) for a, b in zip(blocks[::2], blocks[1::2])], 1)


def scatter_sum(part, nseq, place, order):
    share = part.shape[1] // nseq
    bits = nseq.bit_length() - 1
    if nseq != 1 << bits:
        return lax.psum_scatter(part, "seq", scatter_dimension=1, tiled=True)
    left = list(range(bits))
    for step in [b for b in order if b < bits] + [b for b in range(bits) if b not in order]:
        width = share << sum(b < step for b in left)
        left.remove(step)
        mine = (place >> step) & 1
        away = pick(part, width, 1 - mine)
        if step:
            away = away.astype(BF16)
        away = lax.ppermute(away, "seq", [(i, i ^ (1 << step)) for i in range(nseq)])
        part = pick(part, width, mine) + away.astype(F32)
    return part


def deal_kernel(sides, scalars, data, kept, away):
    width = kept.shape[-1]
    for i in range(data.shape[1] // (2 * width)):
        for ref, side in ((kept, scalars[0]), (away, 1 - scalars[0])):
            block = data[:, pl.ds(pl.multiple_of((2 * i + side) * width, width), width)]
            if sides:
                ref[i % sides, i // sides] = block
            else:
                ref[i] = block


def deal(side, data, width, sides=0):
    rows, chans = data.shape
    count = chans // (2 * width)
    lead = (sides, count // sides) if sides else (count,)
    out = jax.ShapeDtypeStruct(lead + (rows, width), data.dtype)
    vmem = pl.BlockSpec(memory_space=pltpu.VMEM)
    return pl.pallas_call(
        functools.partial(deal_kernel, sides),
        out_shape=(out, out),
        in_specs=[pl.BlockSpec(memory_space=pltpu.SMEM), vmem],
        out_specs=(vmem, vmem),
        compiler_params=pltpu.CompilerParams(vmem_limit_bytes=GRANT),
        cost_estimate=pl.CostEstimate(flops=0, bytes_accessed=8 * rows * chans, transcendentals=0),
    )(side.reshape(1), data)


def sum_over_ring(part, nseq, place):
    core, pair, row = place & 1, (place >> 1) & 1, place >> 2
    lags, chans = part.shape
    size, chans = nseq // 4, chans // nseq

    def halve(part, bit, mine, kind):
        away = lax.dynamic_index_in_dim(part, 1 - mine, 1, False).astype(kind)
        away = lax.ppermute(away, "seq", [(i, i ^ bit) for i in range(nseq)])
        return lax.dynamic_index_in_dim(part, mine, 1, False) + away.astype(F32)

    kept, away = deal(core.astype(jnp.int32), part, chans, 2)
    part = kept + lax.ppermute(away, "seq", [(i, i ^ 1) for i in range(nseq)])
    part = part.reshape(2, size, lags, chans)
    left = size
    while left > 1:
        bit = size // left
        mine = (row // bit) & 1
        part = part.reshape(2 * left // 2, 2, lags, chans)
        part = halve(part, 4 * bit, mine, BF16).reshape(2, left // 2, lags, chans)
        left //= 2
    return halve(part.reshape(1, 2, lags, chans), 2, pair, BF16).reshape(lags, chans)


def links(seg_ids, place):
    own = lax.dynamic_index_in_dim(seg_ids, place, 0, False)
    prior = lax.dynamic_index_in_dim(seg_ids, jnp.maximum(place - 1, 0), 0, False)
    return (place > 0) & (own == prior)


def gathered_products(gated, cotangent, w_out):
    weights = lax.all_gather(w_out, "seq", axis=0, tiled=True)
    grad_gated = lax.dot_general(cotangent, weights, (((1,), (1,)), ((), ())), preferred_element_type=F32)
    grad_gated = lax.psum_scatter(grad_gated, "tp", scatter_dimension=1, tiled=True).astype(BF16)
    outputs = jnp.dot(
        lax.all_gather(gated, "tp", axis=1, tiled=True), weights, preferred_element_type=F32
    ).astype(BF16)
    return grad_gated, outputs


def ring_place(step, size):
    half = (size + 1) // 2
    return jnp.where(step < half, 2 * step, 2 * (size - 1 - step) + 1)


def ring_step(row, size):
    return jnp.where(row & 1 == 0, row >> 1, size - 1 - (row >> 1))


def products_kernel(size, scalars, cot_own, cot_away, gated_own, gated_away, *refs):
    pieces, (grad_own, grad_away, out_own, out_away, grad) = refs[: 4 * size], refs[4 * size :]
    rows = cot_own.shape[0]

    @pl.when(pl.program_id(0) == 0)
    def _():
        grad[...] = jnp.zeros_like(grad)

    def add(order):
        cot = jnp.concatenate([cot_own[...], cot_away[...]], 0)
        total = None
        for s in range(size):
            m = (size - s) % size
            block = (pieces[4 * s], pieces[4 * m + 2], pieces[4 * s + 1], pieces[4 * m + 3])
            block = jnp.concatenate([block[k][...] for k in order], 0)
            grad[s] += lax.dot_general(cot, block, (((1,), (1,)), ((), ())), preferred_element_type=F32)
            left = jnp.concatenate([gated_own[scalars[1 + s]], gated_away[scalars[1 + s]]], 0)
            part = jnp.dot(left, block, preferred_element_type=F32)
            total = part if total is None else total + part
        out_own[...] = total[:rows]
        out_away[...] = total[rows:].astype(BF16)

    @pl.when(scalars[0] == 0)
    def _():
        add((0, 1, 2, 3))

    @pl.when(scalars[0] != 0)
    def _():
        add((2, 3, 0, 1))

    @pl.when(pl.program_id(0) == pl.num_programs(0) - 1)
    def _():
        for s in range(size):
            grad_own[scalars[1 + s]] = grad[s, :rows].astype(BF16)
            grad_away[scalars[1 + s]] = grad[s, rows:].astype(BF16)


def products(scalars, cot_own, cot_away, gated_own, gated_away, pieces):
    rows, feats = cot_own.shape
    size, _, width = gated_own.shape
    depth = pieces[0].shape[0]
    tile = min(1024, feats)
    block = pl.BlockSpec((rows, tile), lambda j, s: (0, j))
    whole = pl.BlockSpec(gated_own.shape, lambda j, s: (0, 0, 0))
    return pl.pallas_call(
        functools.partial(products_kernel, size),
        out_shape=(
            jax.ShapeDtypeStruct(gated_own.shape, BF16),
            jax.ShapeDtypeStruct(gated_own.shape, BF16),
            jax.ShapeDtypeStruct((rows, feats), F32),
            jax.ShapeDtypeStruct((rows, feats), BF16),
        ),
        grid_spec=pltpu.PrefetchScalarGridSpec(
            num_scalar_prefetch=1,
            grid=(feats // tile,),
            in_specs=[block] * 2 + [whole] * 2 + [pl.BlockSpec((depth, tile), lambda j, s: (0, j))] * len(pieces),
            out_specs=(whole, whole, block, block),
            scratch_shapes=[pltpu.VMEM((size, 2 * rows, width), F32)],
        ),
        compiler_params=pltpu.CompilerParams(vmem_limit_bytes=28 << 20),
        cost_estimate=pl.CostEstimate(
            flops=8 * rows * depth * len(pieces) * feats,
            bytes_accessed=2 * depth * len(pieces) * feats + 10 * rows * feats,
            transcendentals=0,
        ),
    )(
        scalars,
        *[
            pltpu.with_memory_space_constraint(a, pltpu.HBM)
            for a in (cot_own, cot_away, gated_own, gated_away, *pieces)
        ],
    )


def merge_kernel(scalars, own, away, out):
    size, _, width = own.shape
    for r in range(size):
        for ref, side in ((own, scalars[0]), (away, 1 - scalars[0])):
            out[:, pl.ds(pl.multiple_of((2 * r + side) * width, width), width)] = ref[r]


def merge(side, own, away):
    size, rows, width = own.shape
    vmem = pl.BlockSpec(memory_space=pltpu.VMEM)
    return pl.pallas_call(
        merge_kernel,
        out_shape=jax.ShapeDtypeStruct((rows, 2 * size * width), own.dtype),
        in_specs=[pl.BlockSpec(memory_space=pltpu.SMEM), vmem, vmem],
        out_specs=vmem,
        compiler_params=pltpu.CompilerParams(vmem_limit_bytes=GRANT),
        cost_estimate=pl.CostEstimate(flops=0, bytes_accessed=8 * own.size, transcendentals=0),
    )(side.reshape(1), own, away)


def on_ring(queries, keys, values, w_out, taps, seg_ids, cotangent):
    rows, chans = queries.shape
    length = rows
    nseq = lax.axis_size("seq")
    place = lax.axis_index("seq")
    size = nseq // 4
    core, pair, row = [i.astype(jnp.int32) for i in (place & 1, (place >> 1) & 1, place >> 2)]
    at = ring_step(row, size)
    swap_core = [(i, i ^ 1) for i in range(nseq)]
    swap_pair = [(i, i ^ 2) for i in range(nseq)]
    walk = list(range(0, size, 2)) + list(range(1, size, 2))[::-1]
    onward = [(4 * walk[i] + k, 4 * walk[(i + 1) % size] + k) for i in range(size) for k in range(4)]
    behind = [(b, a) for a, b in onward]
    later = [(i, i + 1) for i in range(nseq - 1)]
    earlier = [(i + 1, i) for i in range(nseq - 1)]
    send = functools.partial(lax.ppermute, axis_name="seq")
    tie = lax.optimization_barrier
    linked = links(seg_ids, place)
    table, high, low = spectrum_table(length)
    table_now, high_now, low_now = table[:, length:], high[:, length:], low[:, length:]
    scale = 1.0 / length

    half = rows // 2
    first, second = w_out[:half], w_out[half:]
    swapped = send(w_out, perm=swap_core)
    cot_away = send(cotangent, perm=swap_pair)
    product, cot_away = tie((mul(keys, values), cot_away))
    before = send(product, perm=later)
    filt = forward_dft(high_now, low_now, tie(taps.T), ((1,), (0,)))

    pieces = [first, swapped[:half], second, swapped[half:]]
    for step in range(1, size):
        first, second = send(first, perm=onward), send(second, perm=behind)
        swap = (first, second)
        if step == 1:
            *swap, filt = tie((*swap, filt))
        if step == 3:
            before = jnp.where(linked, before, jnp.zeros_like(before))
            data = forward_dft(high, low, jnp.concatenate([before, product], 0), ((1,), (0,)))
            filtered = inverse_dft(table_now, times(filt, data), scale).astype(BF16)
            gated = mul(queries, filtered)
            gated_own, gated_away = deal(pair, gated, chans // (2 * size))
            *swap, gated_own, gated_away = tie((*swap, gated_own, gated_away))
            gated_away = send(gated_away, perm=swap_pair)
        pieces += [first, send(swap[0], perm=swap_core), second, send(swap[1], perm=swap_core)]
    places = [core] + [ring_place(lax.rem(at - s + size, size), size) for s in range(size)]
    grad_own, grad_away, out_own, out_away = products(
        jnp.stack(places), cotangent, cot_away, gated_own, gated_away, pieces
    )
    grad_gated = merge(pair, grad_own, send(grad_away, perm=swap_pair))
    out_away = send(out_away, perm=swap_pair)
    grad_queries = mul(grad_gated, filtered)
    grad_filtered = mul(grad_gated, queries)
    grads = forward_dft(high_now, low_now, grad_filtered, ((1,), (0,)))
    back = inverse_dft(table, times_conj(grads, filt), scale)
    across = jnp.where(linked, back[:length], 0.0).astype(BF16)
    ahead = send(across, perm=earlier)
    taps_part = inverse_dft(table_now, times_conj(grads, data), scale)
    taps_grad = sum_over_ring(taps_part, nseq, place).T
    outputs = (out_own + out_away.astype(F32)).astype(BF16)
    grad_product = (back[length:] + ahead.astype(F32)).astype(BF16)
    grad_keys = mul(grad_product, values)
    grad_values = mul(grad_product, keys)
    return (outputs, grad_queries, grad_keys, grad_values, taps_grad)


def on_device(queries, keys, values, w_out, taps, seg_ids, cotangent):
    rows, chans = queries.shape
    length = taps.shape[1]
    assert rows == length
    nseq = lax.axis_size("seq")
    place = lax.axis_index("seq")
    table, high, low = spectrum_table(length)
    table_now, high_now, low_now = table[:, length:], high[:, length:], low[:, length:]
    scale = 1.0 / length
    later = [(i, i + 1) for i in range(nseq - 1)]
    earlier = [(i + 1, i) for i in range(nseq - 1)]
    linked = links(seg_ids, place)

    product = mul(keys, values)
    before = lax.ppermute(product, "seq", later)
    before = jnp.where(linked, before, jnp.zeros_like(before))
    data = forward_dft(high, low, jnp.concatenate([before, product], 0), ((1,), (0,)))
    filt = forward_dft(high_now, low_now, taps, ((1,), (1,)))
    filtered = inverse_dft(table_now, times(filt, data), scale).astype(BF16)
    gated = mul(queries, filtered)

    grad_gated, outputs = gathered_products(gated, cotangent, w_out)
    grad_queries = mul(grad_gated, filtered)
    grad_filtered = mul(grad_gated, queries)
    grads = forward_dft(high_now, low_now, grad_filtered, ((1,), (0,)))
    back = inverse_dft(table, times_conj(grads, filt), scale)
    across = jnp.where(linked, back[:length], 0.0).astype(BF16)
    ahead = lax.ppermute(across, "seq", earlier)
    taps_part = inverse_dft(table_now, times_conj(grads, data), scale)
    taps_grad = scatter_sum(taps_part, nseq, place, ()).T
    grad_product = (back[length:] + ahead.astype(F32)).astype(BF16)
    grad_keys = mul(grad_product, values)
    grad_values = mul(grad_product, keys)
    return (outputs, grad_queries, grad_keys, grad_values, taps_grad)


def solution(mesh):
    block = P("seq", "tp")
    count = mesh.shape["seq"]
    ring = mesh.shape["tp"] == 1 and count & (count - 1) == 0 and count >= 16

    def run(queries, keys, values, w_out, taps, seg_ids, cotangent):
        rows, chans = queries.shape
        place = on_ring if ring and rows * count == chans else on_device
        return place(queries, keys, values, w_out, taps, seg_ids, cotangent)

    return jax.shard_map(
        run,
        mesh=mesh,
        in_specs=(block, block, block, block, P("tp", None), P(), block),
        out_specs=(block, block, block, block, P(("tp", "seq"), None)),
        check_vma=False,
    )
```
